256 devices in a mesh: pts: 32 (over x, z_hi, core), ctr: 8 (over z_lo, y).
Axes of the slice: x: 4, y: 4, z: 8 (z_hi: 4, z_lo: 2; z = z_hi * 2 + z_lo), core: 2. Of those that a mesh axis runs over, the one named last changes fastest.
Arguments:
- embeddings: bfloat16 [16384, 128], P('pts'), may hold values from -1.1953125 to 1.1953125
- centres: bfloat16 [65536, 128], P('ctr'), may hold values from -1.1953125 to 1.1953125
- prior_freq: float32 [65536], P('ctr'), may hold values from 0.1 to 1
Outputs:
- embed_grad: float32 [16384, 128], P('pts')
- centre_grad: float32 [8, 8192, 128], P('ctr', 'pts')
The draws below stay inside these ranges and needn't reach their ends.
All inputs are finite; a program needn't handle non-finite values.
Results may differ from the reference program's by a relative error of at most 0.0003.
Values sent between devices are 32-bit elements; how exact they have to be, the bound alone decides.
No kernel may reach another device: no remote copies, remote signals or barrier semaphores. Data moves between devices by JAX's collectives and lax.ppermute only.
A program may use at most 64 MiB of HBM per device.

```python
import math
import jax
import jax.numpy as jnp
from jax import lax

D = 128
K_DEV = 8192
K = 65536
TOKENS = 16384
N_CTR = 8


def levels(stream_key, dims, cuts, low, top_value):
    def one(dim, shards_of):
        draws = jax.random.uniform(jax.random.fold_in(jax.random.fold_in(stream_key, 6), dim), (shards_of,), jnp.float32, low / len(cuts), top_value / len(cuts))
        return jnp.repeat(jnp.exp(draws), dims[dim] // shards_of).reshape((-1,) + (1,) * (len(dims) - dim - 1))

    factor_of = one(*cuts[0])
    for cut in cuts[1:]:
        factor_of = factor_of * one(*cut)
    return factor_of


def scatter_about(key, extent, deviation, reach, split=(), kind=jnp.bfloat16):
    loudness = levels(key, extent, split, -0.22, 0.18) if split else 1.0
    array = jax.random.normal(key, extent, jnp.float32) * deviation * loudness
    return jnp.minimum(jnp.maximum(array, -reach), reach).astype(kind)


def setup_inputs(seed: int = 0) -> dict:
    key_of = jax.random.split(jax.random.key(seed), 4)
    return {
        "embeddings": scatter_about(key_of[0], (TOKENS, D), 0.2, 1.1953125, ((0, 32),)),
        "centres": scatter_about(key_of[1], (K, D), 0.2, 1.1953125, ((0, 8),)),
        "prior_freq": jnp.clip(jnp.exp(math.log(1.0) - 2.3025851 * jax.random.uniform(key_of[2], (K,), jnp.float32) ** levels(key_of[2], (K,), ((0, 8),), -0.2, 0.2)), 0.1, 1.0),
    }


loss_scale = 64.0


def kernel(points, point_norms, block):
    cross = jnp.dot(points, block.T, preferred_element_type=jnp.float32)
    block_norms = jnp.sum(jnp.square(block.astype(jnp.float32)), axis=1)
    dist = point_norms[:, None] + block_norms[None, :] - 2.0 * cross
    return 1.0 / (1.0 + dist)


def reference(embeddings, centres, prior_freq):
    points_wide = embeddings.astype(jnp.float32)
    point_norms = jnp.sum(points_wide * points_wide, axis=1)
    block_size = math.gcd(K, 4096)
    block_count = K // block_size
    blocks = centres.reshape(block_count, block_size, D)
    priors = prior_freq.reshape(block_count, block_size)

    def row_part(block):
        return jnp.sum(kernel(embeddings, point_norms, block), axis=1)

    row_total = jnp.sum(lax.map(row_part, blocks), axis=0)

    def freq_part(block):
        return jnp.sum(kernel(embeddings, point_norms, block) / row_total[:, None], axis=0)

    freqs = lax.map(freq_part, blocks) + priors

    def target_part(pair):
        block, freq = pair
        kern = kernel(embeddings, point_norms, block)
        return jnp.sum(kern * kern / freq[None, :], axis=1)

    target_total = jnp.sum(lax.map(target_part, (blocks, freqs)), axis=0)

    def grad_step(carry, pair):
        block, freq = pair
        kern = kernel(embeddings, point_norms, block)
        block_wide = block.astype(jnp.float32)
        weight = kern * (kern * kern / (freq[None, :] * target_total[:, None]) - kern / row_total[:, None])
        embed_part = jnp.sum(weight, axis=1)[:, None] * points_wide - jnp.dot(weight, block_wide, precision=lax.Precision.HIGHEST)
        centre_part = jnp.sum(weight, axis=0)[:, None] * block_wide - jnp.dot(weight.T, points_wide, precision=lax.Precision.HIGHEST)
        return carry + embed_part, centre_part

    embed_sum, centre_parts = lax.scan(grad_step, jnp.zeros((TOKENS, D), jnp.float32), (blocks, freqs))
    embed_grad = 2.0 * loss_scale * embed_sum
    centre_grad = (2.0 * loss_scale * centre_parts).reshape(N_CTR, K_DEV, D)
    return embed_grad, centre_grad
```

```python
import jax
import jax.numpy as jnp
from jax import lax
from jax.experimental import pallas as pl
from jax.experimental.pallas import tpu as pltpu
from jax.sharding import PartitionSpec as P

SIDE = 4
CORES = 2
LANES = 128
ONES = 16
SCALE = 128.0
ROWS_X = 88
MIB = 2**20
F32 = jnp.float32
BF16 = jnp.bfloat16


def core_perm(size):
    return [(i, i ^ 1) for i in range(size)]


def x_perm(size, s):
    return [(i, i ^ (s * SIDE * CORES)) for i in range(size)]


def h_perm(size, s):
    return [(i, i ^ (s * CORES)) for i in range(size)]


def ctr_perm(size, s):
    return [(i, i ^ s) for i in range(size)]


def tile_lanes(column, width):
    return jnp.concatenate([column] * (width // LANES), axis=1)


def spread(row):
    return jnp.broadcast_to(row, (LANES, row.shape[1])).T


def four(refs):
    a, b, c, d = refs
    return (a[...] + b[...]) + (c[...] + d[...])


def kern_body(z_ref, zo_ref, c_ref, kern_ref, row_ref, ct_ref, zt_ref, za, zn, acc):
    half = z_ref.shape[0]
    step = 512
    for base, part in ((0, z_ref[...].astype(F32)), (half, zo_ref[...])):
        zn[base : base + half] = jnp.broadcast_to(
            jnp.sum(part * part, axis=1, keepdims=True) + 1.0, (half, LANES)
        )
        za[base : base + half] = (-2.0 * part).astype(BF16)
        zt_ref[:LANES, base : base + half] = (-SCALE * part.T).astype(BF16)
    zt_ref[LANES:] = jnp.full((ONES, 2 * half), SCALE, BF16)
    acc[...] = jnp.zeros_like(acc)

    @pl.loop(0, c_ref.shape[0] // step)
    def _(t):
        at = pl.ds(pl.multiple_of(t * step, step), step)
        ct = c_ref[at, :].astype(F32).T
        ct_ref[:, at] = ct
        norms = jnp.sum(ct * ct, axis=0, keepdims=True)
        cross = jnp.dot(za[...], ct.astype(BF16), preferred_element_type=F32)
        kern = 1.0 / (cross + norms + tile_lanes(zn[...], step))
        kern_ref[:, at] = kern
        total = acc[...]
        for g in range(step // LANES):
            total = total + kern[:, g * LANES : (g + 1) * LANES]
        acc[...] = total

    row_ref[...] = jnp.sum(acc[...].T, axis=0, keepdims=True)


def freq_body(kern_ref, r0, r1, r2, r3, f_ref, rinv_ref):
    points, count = kern_ref.shape
    rinv = 1.0 / four((r0, r1, r2, r3))
    rinv_ref[...] = rinv
    spread_r = spread(rinv)
    for g in range(count // LANES):
        at = slice(g * LANES, (g + 1) * LANES)
        total = jnp.zeros((8, LANES), F32)
        for i in range(0, points, 128):
            value = kern_ref[i : i + 128, at] * spread_r[i : i + 128]
            total = total + jnp.sum(value.reshape(16, 8, LANES), axis=0)
        f_ref[:, at] = jnp.sum(total, axis=0, keepdims=True)


def target_body(kern_ref, f0, f1, f2, f3, prior_ref, t_ref, finv_ref, acc):
    points, count = kern_ref.shape
    finv_ref[...] = 1.0 / (four((f0, f1, f2, f3)) + prior_ref[...])
    step = 64
    for i in range(0, points, step):
        total = jnp.zeros((step, LANES), F32)
        for g in range(count // LANES):
            at = slice(g * LANES, (g + 1) * LANES)
            kern = kern_ref[i : i + step, at]
            total = total + kern * kern * finv_ref[:, at]
        acc[i : i + step] = total
    t_ref[...] = jnp.sum(acc[...].T, axis=0, keepdims=True)


def weights(kern, finv, tinv, rinv):
    weight = kern * kern * (kern * finv * tinv - rinv)
    high = weight.astype(BF16)
    return high, (weight - high.astype(F32)).astype(BF16)


def centre_body(kern_ref, rinv_ref, finv_ref, t0, t1, t2, t3, zt_ref, ct_ref, *outs):
    outs, (tinv_ref, ts, rs) = outs[:-3], outs[-3:]
    pieces_x, pieces_h = outs[:SIDE], outs[SIDE:]
    inner = kern_ref.shape[1] // (SIDE * SIDE)
    tinv = 1.0 / four((t0, t1, t2, t3))
    tinv_ref[...] = tinv
    ts[...] = spread(tinv)
    rs[...] = spread(rinv_ref[...])
    place = lax.axis_index("pts") // CORES
    x, h = place // SIDE, place % SIDE
    for s in range(SIDE):
        for t in range(SIDE):
            block = (x ^ s) * SIDE + (h ^ t)
            at = pl.ds(pl.multiple_of(block * inner, inner), inner)
            high, low = weights(
                kern_ref[:, at],
                finv_ref[:, at],
                tile_lanes(ts[...], inner),
                tile_lanes(rs[...], inner),
            )
            sums = jnp.dot(zt_ref[...], high, preferred_element_type=F32) + jnp.dot(
                zt_ref[...], low, preferred_element_type=F32
            )
            grad = sums[:LANES] + sums[LANES : LANES + 1] * ct_ref[:, at]
            pieces_x[s][:, t * inner : (t + 1) * inner] = grad[:ROWS_X]
            pieces_h[t][:, s * inner : (s + 1) * inner] = grad[ROWS_X:]


def embed_body(kern_ref, rinv_ref, finv_ref, tinv_ref, z_ref, zo_ref, c_ref, own, other, ts, rs, acc):
    step = 512
    half = z_ref.shape[0]
    ts[...] = spread(tinv_ref[...])
    rs[...] = spread(rinv_ref[...])
    acc[...] = jnp.zeros_like(acc)

    @pl.loop(0, c_ref.shape[0] // step)
    def _(t):
        at = pl.ds(pl.multiple_of(t * step, step), step)
        high, low = weights(
            kern_ref[:, at],
            finv_ref[:, at],
            tile_lanes(ts[...], step),
            tile_lanes(rs[...], step),
        )
        wide = jnp.concatenate([c_ref[at, :], jnp.ones((step, LANES), BF16)], axis=1)
        acc[...] += jnp.dot(high, wide, preferred_element_type=F32) + jnp.dot(
            low, wide, preferred_element_type=F32
        )

    for base, part, out in ((0, z_ref[...].astype(F32), own), (half, zo_ref[...], other)):
        sums = acc[base : base + half]
        out[...] = SCALE * (sums[:, LANES:] * part - sums[:, :LANES])


def split_body(*refs):
    ins, outs = refs[:SIDE], refs[SIDE:]
    inner = outs[0].shape[1]
    for t in range(SIDE):
        outs[t][...] = four([r.at[:, t * inner : (t + 1) * inner] for r in ins])


def final_body(*refs):
    ins, out = refs[:-1], refs[-1]
    out[...] = jnp.concatenate([four(ins[:SIDE]), four(ins[SIDE:])], axis=0).T


VMEM = pl.BlockSpec(memory_space=pltpu.VMEM)


def call(body, outs, *args, scratch=(), limit=20, name=None, flops=0):
    shapes = tuple(jax.ShapeDtypeStruct(*o) for o in outs)
    moved = sum(a.size * a.dtype.itemsize for a in args)
    return pl.pallas_call(
        body,
        out_shape=shapes,
        in_specs=[VMEM] * len(args),
        out_specs=tuple(VMEM for _ in outs),
        scratch_shapes=scratch,
        compiler_params=pltpu.CompilerParams(vmem_limit_bytes=limit * MIB),
        cost_estimate=pl.CostEstimate(flops=flops, bytes_accessed=moved, transcendentals=0),
        name=name,
    )(*args)


def body(embeddings, centres, prior_freq):
    n_pts, n_ctr = lax.axis_size("pts"), lax.axis_size("ctr")
    half, width = embeddings.shape
    points = CORES * half
    inner = centres.shape[0] // n_pts
    count = centres.shape[0] // CORES
    core = lax.axis_index("pts") % CORES

    def swap_core(v):
        return lax.ppermute(v, "pts", core_perm(n_pts))

    def over_ctr(v):
        other = swap_core(v)
        v = v + jnp.concatenate([other[:, half:], other[:, :half]], axis=1)
        v = v + lax.ppermute(v, "ctr", ctr_perm(n_ctr, SIDE))
        return [v] + [lax.ppermute(v, "ctr", ctr_perm(n_ctr, s)) for s in (1, 2, 3)]

    z_other = swap_core(embeddings.astype(F32))
    own = lax.dynamic_index_in_dim(
        centres.reshape(n_pts // CORES, CORES, inner, width), core, 1, keepdims=False
    ).reshape(count, width)
    prior = lax.dynamic_index_in_dim(
        prior_freq.reshape(n_pts // CORES, CORES, inner), core, 1, keepdims=False
    ).reshape(1, count)

    kern, row, ct, zt = call(
        kern_body,
        [((points, count), F32), ((1, points), F32), ((width, count), F32), ((width + ONES, points), BF16)],
        embeddings,
        z_other,
        own,
        scratch=[
            pltpu.VMEM((points, width), BF16),
            pltpu.VMEM((points, LANES), F32),
            pltpu.VMEM((points, LANES), F32),
        ],
        name="kern",
    )
    freq, rinv = call(
        freq_body, [((1, count), F32), ((1, points), F32)], kern, *over_ctr(row), name="freq"
    )
    freq = [freq] + [lax.ppermute(freq, "pts", x_perm(n_pts, s)) for s in (1, 2, 3)]
    freq = (freq[0] + freq[1]) + (freq[2] + freq[3])
    freq = [freq] + [lax.ppermute(freq, "pts", h_perm(n_pts, s)) for s in (1, 2, 3)]
    target, finv = call(
        target_body,
        [((1, points), F32), ((1, count), F32)],
        kern,
        *freq,
        prior,
        scratch=[pltpu.VMEM((points, LANES), F32)],
        name="target",
    )
    spreads = [pltpu.VMEM((points, LANES), F32)] * 2
    *pieces, tinv = call(
        centre_body,
        [((ROWS_X, SIDE * inner), F32)] * SIDE
        + [((width - ROWS_X, SIDE * inner), F32)] * SIDE
        + [((1, points), F32)],
        kern,
        rinv,
        finv,
        *over_ctr(target),
        zt,
        ct,
        scratch=spreads,
        name="centre",
    )
    by_x, by_h = pieces[:SIDE], pieces[SIDE:]
    by_x = [by_x[0]] + [lax.ppermute(by_x[s], "pts", x_perm(n_pts, s)) for s in (1, 2, 3)]
    by_h = [by_h[0]] + [lax.ppermute(by_h[s], "pts", h_perm(n_pts, s)) for s in (1, 2, 3)]
    mine, other = call(
        embed_body,
        [((half, width), F32)] * 2,
        kern,
        rinv,
        finv,
        tinv,
        embeddings,
        z_other,
        own,
        scratch=spreads + [pltpu.VMEM((points, 2 * LANES), F32)],
        name="embed",
    )
    embed = mine + swap_core(other)
    for s in (SIDE, 1, 3):
        embed = embed + lax.ppermute(embed, "ctr", ctr_perm(n_ctr, s))

    by_x = call(split_body, [((ROWS_X, inner), F32)] * SIDE, *by_x, name="split_x")
    by_h = call(split_body, [((width - ROWS_X, inner), F32)] * SIDE, *by_h, name="split_h")
    by_x = [by_x[0]] + [lax.ppermute(by_x[s], "pts", h_perm(n_pts, s)) for s in (1, 2, 3)]
    by_h = [by_h[0]] + [lax.ppermute(by_h[s], "pts", x_perm(n_pts, s)) for s in (1, 2, 3)]
    (grad,) = call(final_body, [((inner, width), F32)], *by_x, *by_h, name="final")
    return embed, grad.reshape(1, inner, width)


def solution(mesh):
    in_specs = (P("pts", None), P("ctr", None), P("ctr"))
    out_specs = (P("pts", None), P("ctr", "pts", None))
    return jax.shard_map(body, mesh=mesh, in_specs=in_specs, out_specs=out_specs, check_vma=False)
```

```python
import jax
import jax.numpy as jnp
from jax import lax
from jax.experimental import pallas as pl
from jax.experimental.pallas import tpu as pltpu
from jax.sharding import PartitionSpec as P

SIDE = 4
CORES = 2
LANES = 128
ONES = 16
SCALE = 128.0
ROWS_X = 88
MIB = 2**20
F32 = jnp.float32
BF16 = jnp.bfloat16


def core_perm(size):
    return [(i, i ^ 1) for i in range(size)]


def x_perm(size, s):
    return [(i, i ^ (s * SIDE * CORES)) for i in range(size)]


def h_perm(size, s):
    return [(i, i ^ (s * CORES)) for i in range(size)]


def ctr_perm(size, s):
    return [(i, i ^ s) for i in range(size)]


def tile_lanes(column, width):
    return jnp.concatenate([column] * (width // LANES), axis=1)


def spread(row):
    return jnp.broadcast_to(row, (LANES, row.shape[1])).T


def four(refs):
    a, b, c, d = refs
    return (a[...] + b[...]) + (c[...] + d[...])


def block_rows(block, inner, core):
    return pl.ds(pl.multiple_of((block * CORES + core) * inner, inner), inner)


def kern_part(part, c_ref, kern_ref, za, zn):
    points = part.shape[0]
    inner = c_ref.shape[0] // lax.axis_size("pts")
    core = lax.axis_index("pts") % CORES
    zn[...] = jnp.broadcast_to(jnp.sum(part * part, axis=1, keepdims=True) + 1.0, (points, LANES))
    za[...] = (-2.0 * part).astype(BF16)
    total = jnp.zeros((points, LANES), F32)
    for block in range(kern_ref.shape[1] // inner):
        ct = c_ref[block_rows(block, inner, core), :].astype(F32).T
        norms = jnp.sum(ct * ct, axis=0, keepdims=True)
        cross = jnp.dot(za[...], ct.astype(BF16), preferred_element_type=F32)
        kern = 1.0 / (cross + norms + tile_lanes(zn[...], inner))
        kern_ref[:, block * inner : (block + 1) * inner] = kern
        for g in range(inner // LANES):
            total = total + kern[:, g * LANES : (g + 1) * LANES]
    return jnp.sum(total.T, axis=0, keepdims=True)


def own_body(z_ref, c_ref, kern_ref, row_ref, za, zn):
    row_ref[...] = kern_part(z_ref[...].astype(F32), c_ref, kern_ref, za, zn)


def other_body(zo_ref, c_ref, row_ref, kern_ref, rows_ref, za, zn):
    rows_ref[:1] = row_ref[...]
    rows_ref[1:] = kern_part(zo_ref[...], c_ref, kern_ref, za, zn)


def swap_add_body(mine, theirs, out):
    out[:1] = mine[:1] + theirs[1:]
    out[1:] = mine[1:] + theirs[:1]


def add_body(*refs):
    refs[-1][...] = four(refs[:-1]) if len(refs) == 5 else refs[0][...] + refs[1][...]


def freq_body(own_ref, other_ref, r0, r1, r2, r3, f_ref, rinv_ref):
    half, count = own_ref.shape
    rinv = 1.0 / four((r0, r1, r2, r3))
    rinv_ref[...] = rinv
    parts = ((own_ref, spread(rinv[:1])), (other_ref, spread(rinv[1:])))
    for g in range(count // LANES):
        at = slice(g * LANES, (g + 1) * LANES)
        total = jnp.zeros((8, LANES), F32)
        for kern_ref, scale in parts:
            for i in range(0, half, 128):
                value = kern_ref[i : i + 128, at] * scale[i : i + 128]
                total = total + jnp.sum(value.reshape(16, 8, LANES), axis=0)
        f_ref[:, at] = jnp.sum(total, axis=0, keepdims=True)


def target_body(own_ref, other_ref, f0, f1, f2, f3, prior_ref, t_ref, finv_ref, acc):
    half, count = own_ref.shape
    inner = prior_ref.shape[1] // lax.axis_size("pts")
    core = lax.axis_index("pts") % CORES
    prior = [prior_ref[:, block_rows(b, inner, core)] for b in range(count // inner)]
    finv_ref[...] = 1.0 / (four((f0, f1, f2, f3)) + jnp.concatenate(prior, axis=1))
    step = 64
    for row, kern_ref in ((0, own_ref), (1, other_ref)):
        for i in range(0, half, step):
            total = jnp.zeros((step, LANES), F32)
            for g in range(count // LANES):
                at = slice(g * LANES, (g + 1) * LANES)
                kern = kern_ref[i : i + step, at]
                total = total + kern * kern * finv_ref[:, at]
            acc[i : i + step] = total
        t_ref[row : row + 1] = jnp.sum(acc[...].T, axis=0, keepdims=True)


def weights(kern, finv, tinv, rinv):
    weight = kern * kern * (kern * finv * tinv - rinv)
    high = weight.astype(BF16)
    return high, (weight - high.astype(F32)).astype(BF16)


def grad_body(own_ref, other_ref, rinv_ref, finv_ref, t0, t1, t2, t3, z_ref, zo_ref, c_ref, *outs):
    pieces_x, pieces_h, embeds = outs[:SIDE], outs[SIDE : 2 * SIDE], outs[2 * SIDE : -4]
    zt, ts, rs, acc = outs[-4:]
    half, count = own_ref.shape
    inner = count // (SIDE * SIDE)
    tinv = 1.0 / four((t0, t1, t2, t3))
    points = (z_ref[...].astype(F32), zo_ref[...])
    kerns = (own_ref, other_ref)
    for p in range(CORES):
        ts[p] = spread(tinv[p : p + 1])
        rs[p] = spread(rinv_ref[p : p + 1])
        zt[p, :LANES] = (-SCALE * points[p].T).astype(BF16)
        zt[p, LANES:] = jnp.full((ONES, half), SCALE, BF16)
    acc[...] = jnp.zeros_like(acc)
    core = lax.axis_index("pts") % CORES
    place = lax.axis_index("pts") // CORES
    x, h = place // SIDE, place % SIDE
    for s in (2, 1, 3, 0):
        for t in range(SIDE):
            block = (x ^ s) * SIDE + (h ^ t)
            at = pl.ds(pl.multiple_of(block * inner, inner), inner)
            c = c_ref[block_rows(block, inner, core), :]
            wide = jnp.concatenate([c, jnp.ones((inner, LANES), BF16)], axis=1)
            sums = jnp.zeros((LANES + ONES, inner), F32)
            for p in range(CORES):
                high, low = weights(
                    kerns[p][:, at],
                    finv_ref[:, at],
                    tile_lanes(ts[p], inner),
                    tile_lanes(rs[p], inner),
                )
                sums += jnp.dot(zt[p], high, preferred_element_type=F32)
                sums += jnp.dot(zt[p], low, preferred_element_type=F32)
                acc[p] += jnp.dot(high, wide, preferred_element_type=F32) + jnp.dot(
                    low, wide, preferred_element_type=F32
                )
            grad = sums[:LANES] + sums[LANES : LANES + 1] * c.astype(F32).T
            pieces_x[s][:, t * inner : (t + 1) * inner] = grad[:ROWS_X]
            pieces_h[t][:, s * inner : (s + 1) * inner] = grad[ROWS_X:]
    for p in range(CORES):
        sums = acc[p]
        embeds[p][...] = SCALE * (sums[:, LANES:] * points[p] - sums[:, :LANES])


def split_body(*refs):
    ins, outs = refs[:SIDE], refs[SIDE:]
    inner = outs[0].shape[1]
    for t in range(SIDE):
        outs[t][...] = four([r.at[:, t * inner : (t + 1) * inner] for r in ins])


def final_body(*refs):
    ins, out = refs[:-1], refs[-1]
    out[...] = jnp.concatenate([four(ins[:SIDE]), four(ins[SIDE:])], axis=0).T


def embed_split_body(mine, theirs, *outs):
    y = lax.axis_index("ctr") % SIDE
    rows = outs[0].shape[0]
    for s in range(SIDE):
        at = pl.ds(pl.multiple_of((y ^ s) * rows, rows), rows)
        outs[s][...] = mine[at, :] + theirs[at, :]


def embed_join_body(*refs):
    ins, out = refs[:-1], refs[-1]
    y = lax.axis_index("ctr") % SIDE
    rows = ins[0].shape[0]
    for s in range(SIDE):
        out[pl.ds(pl.multiple_of((y ^ s) * rows, rows), rows), :] = ins[s][...]


VMEM = pl.BlockSpec(memory_space=pltpu.VMEM)


def call(body, outs, *args, scratch=(), limit=2, name=None, flops=0):
    shapes = tuple(jax.ShapeDtypeStruct(shape, F32) for shape in outs)
    moved = sum(a.size * a.dtype.itemsize for a in args)
    out = pl.pallas_call(
        body,
        out_shape=shapes,
        in_specs=[VMEM] * len(args),
        out_specs=tuple(VMEM for _ in outs),
        scratch_shapes=scratch,
        compiler_params=pltpu.CompilerParams(vmem_limit_bytes=limit * MIB),
        cost_estimate=pl.CostEstimate(flops=flops, bytes_accessed=moved, transcendentals=0),
        name=name,
    )(*args)
    return out if len(out) > 1 else out[0]


def body(embeddings, centres, prior_freq):
    n_pts, n_ctr = lax.axis_size("pts"), lax.axis_size("ctr")
    half, width = embeddings.shape
    inner = centres.shape[0] // n_pts
    count = centres.shape[0] // CORES
    prior = prior_freq.reshape(1, centres.shape[0])

    def swap_core(v):
        return lax.ppermute(v, "pts", core_perm(n_pts))

    def swap_zl(v):
        return lax.ppermute(v, "ctr", ctr_perm(n_ctr, SIDE))

    def around_y(vs):
        return [vs[0]] + [lax.ppermute(vs[s], "ctr", ctr_perm(n_ctr, s)) for s in (1, 2, 3)]

    def around_x(vs):
        return [vs[0]] + [lax.ppermute(vs[s], "pts", x_perm(n_pts, s)) for s in (1, 2, 3)]

    def around_h(vs):
        return [vs[0]] + [lax.ppermute(vs[s], "pts", h_perm(n_pts, s)) for s in (1, 2, 3)]

    def over_ctr(v):
        v = call(swap_add_body, [v.shape], v, swap_core(v), name="sum_core")
        v = call(add_body, [v.shape], v, swap_zl(v), name="sum_zl")
        return around_y([v] * SIDE)

    rows = (CORES, half)
    z_other = swap_core(embeddings.astype(F32))
    kern_scratch = [pltpu.VMEM((half, width), BF16), pltpu.VMEM((half, LANES), F32)]
    kern_own, row = call(
        own_body,
        [(half, count), (1, half)],
        embeddings,
        centres,
        scratch=kern_scratch,
        limit=20,
        name="kern_own",
    )
    kern_other, row = call(
        other_body,
        [(half, count), rows],
        z_other,
        centres,
        row,
        scratch=kern_scratch,
        limit=20,
        name="kern_other",
    )
    freq, rinv = call(
        freq_body, [(1, count), rows], kern_own, kern_other, *over_ctr(row), limit=20, name="freq"
    )
    freq = call(add_body, [freq.shape], *around_x([freq] * SIDE), name="sum_x")
    target, finv = call(
        target_body,
        [rows, (1, count)],
        kern_own,
        kern_other,
        *around_h([freq] * SIDE),
        prior,
        scratch=[pltpu.VMEM((half, LANES), F32)],
        limit=20,
        name="target",
    )
    *pieces, mine, other = call(
        grad_body,
        [(ROWS_X, SIDE * inner)] * SIDE
        + [(width - ROWS_X, SIDE * inner)] * SIDE
        + [(half, width)] * 2,
        kern_own,
        kern_other,
        rinv,
        finv,
        *over_ctr(target),
        embeddings,
        z_other,
        centres,
        scratch=[
            pltpu.VMEM((CORES, width + ONES, half), BF16),
            pltpu.VMEM((CORES, half, LANES), F32),
            pltpu.VMEM((CORES, half, LANES), F32),
            pltpu.VMEM((CORES, half, 2 * LANES), F32),
        ],
        limit=24,
        name="grad",
    )
    by_x, by_h = around_x(pieces[:SIDE]), around_h(pieces[SIDE:])

    quarter = (half // SIDE, width)
    embed = call(embed_split_body, [quarter] * SIDE, mine, swap_core(other), name="embed_split")
    embed = call(add_body, [quarter], *around_y(embed), name="embed_y")
    embed = call(add_body, [quarter], embed, swap_zl(embed), name="embed_zl")
    embed = call(embed_join_body, [(half, width)], *around_y([embed] * SIDE), name="embed_join")

    by_x = call(split_body, [(ROWS_X, inner)] * SIDE, *by_x, name="split_x")
    by_h = call(split_body, [(width - ROWS_X, inner)] * SIDE, *by_h, name="split_h")
    grad = call(
        final_body, [(inner, width)], *around_h(by_x), *around_x(by_h), name="final"
    )
    return embed, grad.reshape(1, inner, width)


def solution(mesh):
    in_specs = (P("pts", None), P("ctr", None), P("ctr"))
    out_specs = (P("pts", None), P("ctr", "pts", None))
    return jax.shard_map(body, mesh=mesh, in_specs=in_specs, out_specs=out_specs, check_vma=False)
```

```python
import jax
import jax.numpy as jnp
from jax import lax
from jax.experimental import pallas as pl
from jax.experimental.pallas import tpu as pltpu
from jax.sharding import PartitionSpec as P

SIDE = 4
CORES = 2
LANES = 128
ONES = 16
SCALE = 128.0
MIB = 2**20
F32 = jnp.float32
BF16 = jnp.bfloat16


def tile_lanes(column, width):
    return jnp.concatenate([column] * (width // LANES), axis=1)


def spread(row):
    return jnp.broadcast_to(row, (LANES, row.shape[1])).T


def four(refs):
    a, b, c, d = refs
    return (a[...] + b[...]) + (c[...] + d[...])


def block_rows(block, inner, core):
    return pl.ds(pl.multiple_of((block * CORES + core) * inner, inner), inner)


def kern_block(za, zn, ct, norms):
    cross = jnp.dot(za[...], ct, preferred_element_type=F32)
    return 1.0 / (cross + norms + tile_lanes(zn[...], ct.shape[1]))


def kern_setup(part, za, zn):
    zn[...] = jnp.broadcast_to(jnp.sum(part * part, axis=1, keepdims=True) + 1.0, zn.shape)
    za[...] = (-2.0 * part).astype(BF16)


def lane_sums(total, kern):
    for g in range(kern.shape[1] // LANES):
        total = total + kern[:, g * LANES : (g + 1) * LANES]
    return total


def own_body(z_ref, c_ref, kern_ref, row_ref, ct_ref, norm_ref, za, zn, buf, points, sems):
    half, count = kern_ref.shape
    inner = buf.shape[1]
    core = lax.axis_index("core")
    fetch = pltpu.make_async_copy(z_ref, points, sems.at[0])
    fetch.start()
    copies = [
        pltpu.make_async_copy(c_ref.at[block_rows(b, inner, core), :], buf.at[b], sems.at[b + 1])
        for b in range(count // inner)
    ]
    for copy in copies:
        copy.start()
    fetch.wait()
    kern_setup(points[...].astype(F32), za, zn)
    for copy in copies:
        copy.wait()
    total = jnp.zeros((half, LANES), F32)
    for b in range(count // inner):
        at = slice(b * inner, (b + 1) * inner)
        ct = buf[b].astype(F32).T
        norms = jnp.sum(ct * ct, axis=0, keepdims=True)
        ct = ct.astype(BF16)
        ct_ref[:, at] = ct
        norm_ref[:, at] = norms
        kern = kern_block(za, zn, ct, norms)
        kern_ref[:, at] = kern
        total = lane_sums(total, kern)
    row_ref[...] = jnp.sum(total.T, axis=0, keepdims=True)


def other_body(zo_ref, ct_ref, norm_ref, row_ref, kern_ref, rows_ref, za, zn):
    half, count = kern_ref.shape
    step = 256
    rows_ref[:1] = row_ref[...]
    kern_setup(zo_ref[...], za, zn)
    total = jnp.zeros((half, LANES), F32)
    for b in range(count // step):
        at = slice(b * step, (b + 1) * step)
        kern = kern_block(za, zn, ct_ref[:, at], norm_ref[:, at])
        kern_ref[:, at] = kern
        total = lane_sums(total, kern)
    rows_ref[1:] = jnp.sum(total.T, axis=0, keepdims=True)


def swap_add_body(mine, theirs, out):
    for n in range(out.shape[0]):
        out[n, :1] = mine[:1] + theirs[1:]
        out[n, 1:] = mine[1:] + theirs[:1]


def summed(ref):
    total = ref[0]
    for n in range(1, ref.shape[0]):
        total = total + ref[n]
    return total


def add_body(*refs):
    refs[-1][...] = four(refs[:-1]) if len(refs) == 5 else refs[0][...] + refs[1][...]


def freq_body(own_ref, other_ref, rows_ref, f_ref, rinv_ref):
    half, count = own_ref.shape
    rinv = 1.0 / summed(rows_ref)
    rinv_ref[...] = rinv
    parts = ((own_ref, spread(rinv[:1])), (other_ref, spread(rinv[1:])))
    for g in range(count // LANES):
        at = slice(g * LANES, (g + 1) * LANES)
        total = jnp.zeros((8, LANES), F32)
        for kern_ref, scale in parts:
            for i in range(0, half, 128):
                value = kern_ref[i : i + 128, at] * scale[i : i + 128]
                total = total + jnp.sum(value.reshape(16, 8, LANES), axis=0)
        f_ref[:, at] = jnp.sum(total, axis=0, keepdims=True)


def target_body(own_ref, other_ref, f0, f1, f2, f3, prior_ref, t_ref, finv_ref, acc):
    half, count = own_ref.shape
    inner = count // (SIDE * SIDE)
    core = lax.axis_index("core")
    prior = [prior_ref[:, block_rows(b, inner, core)] for b in range(count // inner)]
    finv_ref[...] = 1.0 / (four((f0, f1, f2, f3)) + jnp.concatenate(prior, axis=1))
    step = 64
    for row, kern_ref in ((0, own_ref), (1, other_ref)):
        for i in range(0, half, step):
            total = jnp.zeros((step, LANES), F32)
            for g in range(count // LANES):
                at = slice(g * LANES, (g + 1) * LANES)
                kern = kern_ref[i : i + step, at]
                total = total + kern * kern * finv_ref[:, at]
            acc[i : i + step] = total
        t_ref[row : row + 1] = jnp.sum(acc[...].T, axis=0, keepdims=True)


def weights(kern, finv, tinv, rinv):
    weight = kern * kern * (kern * finv * tinv - rinv)
    high = weight.astype(BF16)
    return high, (weight - high.astype(F32)).astype(BF16)


def grad_setup(tinv, rinv_ref, points, zt, ts, rs):
    for p in range(CORES):
        ts[p] = spread(tinv[p : p + 1])
        rs[p] = spread(rinv_ref[p : p + 1])
        zt[p, :LANES] = (-SCALE * points[p].T).astype(BF16)
        zt[p, LANES:] = jnp.full((ONES, points[p].shape[0]), SCALE, BF16)


def grad_piece(s, kerns, finv_ref, c_ref, zt, ts, rs, acc, piece):
    inner = piece.shape[1] // SIDE
    core, x = lax.axis_index("core"), lax.axis_index("x")
    for h in range(SIDE):
        block = (x ^ s) * SIDE + h
        at = pl.ds(pl.multiple_of(block * inner, inner), inner)
        c = c_ref[block_rows(block, inner, core), :]
        wide = jnp.concatenate([c, jnp.ones((inner, LANES), BF16)], axis=1)
        sums = jnp.zeros((LANES + ONES, inner), F32)
        for p in range(CORES):
            high, low = weights(
                kerns[p][:, at], finv_ref[:, at], tile_lanes(ts[p], inner), tile_lanes(rs[p], inner)
            )
            sums += jnp.dot(zt[p], high, preferred_element_type=F32)
            sums += jnp.dot(zt[p], low, preferred_element_type=F32)
            acc[p] += jnp.dot(high, wide, preferred_element_type=F32) + jnp.dot(
                low, wide, preferred_element_type=F32
            )
        piece[:, h * inner : (h + 1) * inner] = (
            sums[:LANES] + sums[LANES : LANES + 1] * c.astype(F32).T
        )


def far_body(own_ref, other_ref, rinv_ref, finv_ref, rows_ref, z_ref, zo_ref, c_ref, *outs):
    pieces, (tinv_ref, acc, zt, ts, rs) = outs[:3], outs[3:]
    points = (z_ref[...].astype(F32), zo_ref[...])
    tinv = 1.0 / summed(rows_ref)
    tinv_ref[...] = tinv
    grad_setup(tinv, rinv_ref, points, zt, ts, rs)
    acc[...] = jnp.zeros_like(acc)
    for s, piece in zip((1, 3, 2), pieces):
        grad_piece(s, (own_ref, other_ref), finv_ref, c_ref, zt, ts, rs, acc, piece)


def near_body(own_ref, other_ref, rinv_ref, finv_ref, tinv_ref, acc_ref, z_ref, zo_ref, c_ref, *outs):
    piece, own, other, zt, ts, rs, acc = outs
    points = (z_ref[...].astype(F32), zo_ref[...])
    grad_setup(tinv_ref[...], rinv_ref, points, zt, ts, rs)
    acc[...] = acc_ref[...]
    grad_piece(0, (own_ref, other_ref), finv_ref, c_ref, zt, ts, rs, acc, piece)
    for p, out in enumerate((own, other)):
        sums = acc[p]
        out[...] = SCALE * (sums[:, LANES:] * points[p] - sums[:, :LANES])


def split_body(near, far0, far1, far2, _, *outs):
    h = lax.axis_index("h")
    inner = outs[0].shape[1]
    for t in range(SIDE):
        at = pl.ds(pl.multiple_of((h ^ t) * inner, inner), inner)
        outs[t][...] = four([r.at[:, at] for r in (near, far0, far1, far2)])


def final_body(*refs):
    refs[SIDE][...] = four(refs[:SIDE]).T


VMEM = pl.BlockSpec(memory_space=pltpu.VMEM)
HBM = pl.BlockSpec(memory_space=pltpu.HBM)


def call(body, outs, *args, scratch=(), limit=2, name=None, flops=0, specs=None):
    shapes = tuple(o if hasattr(o, "dtype") else jax.ShapeDtypeStruct(o, F32) for o in outs)
    moved = sum(a.size * a.dtype.itemsize for a in args)
    out = pl.pallas_call(
        body,
        out_shape=shapes,
        in_specs=specs or [VMEM] * len(args),
        out_specs=tuple(VMEM for _ in outs),
        scratch_shapes=scratch,
        compiler_params=pltpu.CompilerParams(vmem_limit_bytes=limit * MIB),
        cost_estimate=pl.CostEstimate(flops=flops, bytes_accessed=moved, transcendentals=0),
        name=name,
    )(*args)
    return out if len(out) > 1 else out[0]


def swap(v, axis, s):
    return lax.ppermute(v, axis, [(i, i ^ s) for i in range(lax.axis_size(axis))])


def around(pieces, axis):
    return [pieces[0]] + [swap(pieces[s], axis, s) for s in (1, 3, 2)]


def body(embeddings, centres, prior_freq):
    half, width = embeddings.shape
    count = centres.shape[0] // CORES
    inner = count // (SIDE * SIDE)
    prior = prior_freq.reshape(1, centres.shape[0])
    rows = (CORES, half)

    def over_ctr(v):
        parts = lax.axis_size("zl") * lax.axis_size("y")
        v = call(swap_add_body, [(parts, *rows)], v, swap(v, "core", 1), name="sum_core")
        return lax.all_to_all(v, ("zl", "y"), 0, 0)

    z_other = swap(embeddings.astype(F32), "core", 1)
    kern_scratch = [pltpu.VMEM((half, width), BF16), pltpu.VMEM((half, LANES), F32)]
    kern_own, row, ct, norms = call(
        own_body,
        [(half, count), (1, half), jax.ShapeDtypeStruct((width, count), BF16), (1, count)],
        embeddings,
        centres,
        scratch=kern_scratch
        + [
            pltpu.VMEM((SIDE * SIDE, inner, width), BF16),
            pltpu.VMEM((half, width), BF16),
            pltpu.SemaphoreType.DMA((SIDE * SIDE + 1,)),
        ],
        limit=16,
        specs=[HBM, HBM],
        name="kern_own",
    )
    kern_other, row = call(
        other_body,
        [(half, count), rows],
        z_other,
        ct,
        norms,
        row,
        scratch=kern_scratch,
        limit=16,
        name="kern_other",
    )
    freq, rinv = call(
        freq_body,
        [(1, count), rows],
        kern_own,
        kern_other,
        over_ctr(row),
        limit=20,
        name="freq",
    )
    freq = call(add_body, [freq.shape], *around([freq] * SIDE, "x"), name="sum_x")
    target, finv = call(
        target_body,
        [rows, (1, count)],
        kern_own,
        kern_other,
        *around([freq] * SIDE, "h"),
        prior,
        scratch=[pltpu.VMEM((half, LANES), F32)],
        limit=20,
        name="target",
    )
    setup = [
        pltpu.VMEM((CORES, width + ONES, half), BF16),
        pltpu.VMEM((CORES, half, LANES), F32),
        pltpu.VMEM((CORES, half, LANES), F32),
    ]
    sums = (CORES, half, 2 * LANES)
    piece = (width, SIDE * inner)
    *far, tinv, acc = call(
        far_body,
        [piece] * 3 + [rows, sums],
        kern_own,
        kern_other,
        rinv,
        finv,
        over_ctr(target),
        embeddings,
        z_other,
        centres,
        scratch=setup,
        limit=24,
        name="grad_far",
    )
    far = [swap(v, "x", s) for v, s in zip(far, (1, 3, 2))]
    near, mine, other = call(
        near_body,
        [piece, (half, width), (half, width)],
        kern_own,
        kern_other,
        rinv,
        finv,
        tinv,
        acc,
        embeddings,
        z_other,
        centres,
        scratch=setup + [pltpu.VMEM(sums, F32)],
        limit=24,
        name="grad_near",
    )
    embed = call(add_body, [mine.shape], mine, swap(other, "core", 1), name="embed_core")
    embed = call(add_body, [mine.shape], embed, swap(embed, "zl", 1), name="embed_zl")
    by_h = call(
        split_body,
        [(width, inner)] * SIDE,
        near,
        *far,
        embed,
        specs=[VMEM] * SIDE + [pl.BlockSpec(memory_space=pl.ANY)],
        name="split",
    )
    embed = call(add_body, [mine.shape], embed, swap(embed, "y", 1), name="embed_y")
    embed = call(add_body, [mine.shape], embed, swap(embed, "y", 3), name="embed")
    grad = call(final_body, [(inner, width)], *around(by_h, "h"), name="final")
    return embed, grad.reshape(1, inner, width)


def solution(mesh):
    names = ("x", "h", "core", "zl", "y")
    grid = jax.sharding.Mesh(mesh.devices.reshape(SIDE, SIDE, CORES, CORES, SIDE), names)
    pts, ctr = names[:3], names[3:]
    in_specs = (P(pts, None), P(ctr, None), P(ctr))
    out_specs = (P(pts, None), P(ctr, pts, None))
    return jax.shard_map(body, mesh=grid, in_specs=in_specs, out_specs=out_specs, check_vma=False)
```

```python
import jax
import jax.numpy as jnp
from jax import lax
from jax.experimental import pallas as pl
from jax.experimental.pallas import tpu as pltpu
from jax.sharding import PartitionSpec as P

SIDE = 4
CORES = 2
LANES = 128
ONES = 16
SCALE = 128.0
MIB = 2**20
HINT = 10**10
F32 = jnp.float32
BF16 = jnp.bfloat16


def tile_lanes(column, width):
    return jnp.concatenate([column] * (width // LANES), axis=1)


def spread(row):
    return jnp.broadcast_to(row, (LANES, row.shape[1])).T


def four(refs):
    a, b, c, d = refs
    return (a[...] + b[...]) + (c[...] + d[...])


def block_rows(block, inner, core):
    return pl.ds(pl.multiple_of((block * CORES + core) * inner, inner), inner)


def kern_block(za, zn, ct, norms):
    cross = jnp.dot(za[...], ct, preferred_element_type=F32)
    return 1.0 / (cross + norms + tile_lanes(zn[...], ct.shape[1]))


def kern_setup(part, za, zn):
    zn[...] = jnp.broadcast_to(jnp.sum(part * part, axis=1, keepdims=True) + 1.0, zn.shape)
    za[...] = (-2.0 * part).astype(BF16)


def lane_sums(total, kern):
    for g in range(kern.shape[1] // LANES):
        total = total + kern[:, g * LANES : (g + 1) * LANES]
    return total


def own_body(z_ref, c_ref, kern_ref, row_ref, ct_ref, norm_ref, za, zn):
    half, count = kern_ref.shape
    inner = count // (SIDE * SIDE)
    core = lax.axis_index("core")
    kern_setup(z_ref[...], za, zn)
    total = jnp.zeros((half, LANES), F32)
    for b in range(count // inner):
        at = slice(b * inner, (b + 1) * inner)
        ct = c_ref[block_rows(b, inner, core), :].astype(F32).T
        norms = jnp.sum(ct * ct, axis=0, keepdims=True)
        ct = ct.astype(BF16)
        ct_ref[:, at] = ct
        norm_ref[:, at] = norms
        kern = kern_block(za, zn, ct, norms)
        kern_ref[:, at] = kern
        total = lane_sums(total, kern)
    row_ref[...] = jnp.sum(total.T, axis=0, keepdims=True)


def other_body(zo_ref, ct_ref, norm_ref, row_ref, kern_ref, rows_ref, za, zn):
    half, count = kern_ref.shape
    step = 256
    rows_ref[:1] = row_ref[...]
    kern_setup(zo_ref[...], za, zn)
    total = jnp.zeros((half, LANES), F32)
    for b in range(count // step):
        at = slice(b * step, (b + 1) * step)
        kern = kern_block(za, zn, ct_ref[:, at], norm_ref[:, at])
        kern_ref[:, at] = kern
        total = lane_sums(total, kern)
    rows_ref[1:] = jnp.sum(total.T, axis=0, keepdims=True)


def swap_add_body(mine, theirs, out):
    for n in range(out.shape[0]):
        out[n, :1] = mine[:1] + theirs[1:]
        out[n, 1:] = mine[1:] + theirs[:1]


def summed(ref):
    total = ref[0]
    for n in range(1, ref.shape[0]):
        total = total + ref[n]
    return total


def add_body(*refs):
    refs[-1][...] = four(refs[:-1]) if len(refs) == 5 else refs[0][...] + refs[1][...]


def freq_body(own_ref, other_ref, rows_ref, f_ref, rinv_ref):
    half, count = own_ref.shape
    rinv = 1.0 / summed(rows_ref)
    rinv_ref[...] = rinv
    parts = ((own_ref, spread(rinv[:1])), (other_ref, spread(rinv[1:])))
    for g in range(count // LANES):
        at = slice(g * LANES, (g + 1) * LANES)
        total = jnp.zeros((8, LANES), F32)
        for kern_ref, scale in parts:
            for i in range(0, half, 128):
                value = kern_ref[i : i + 128, at] * scale[i : i + 128]
                total = total + jnp.sum(value.reshape(16, 8, LANES), axis=0)
        f_ref[:, at] = jnp.sum(total, axis=0, keepdims=True)


def target_body(own_ref, other_ref, f0, f1, f2, f3, prior_ref, t_ref, finv_ref, acc):
    half, count = own_ref.shape
    inner = count // (SIDE * SIDE)
    core = lax.axis_index("core")
    prior = [prior_ref[:, block_rows(b, inner, core)] for b in range(count // inner)]
    finv_ref[...] = 1.0 / (four((f0, f1, f2, f3)) + jnp.concatenate(prior, axis=1))
    step = 64
    for row, kern_ref in ((0, own_ref), (1, other_ref)):
        for i in range(0, half, step):
            total = jnp.zeros((step, LANES), F32)
            for g in range(count // LANES):
                at = slice(g * LANES, (g + 1) * LANES)
                kern = kern_ref[i : i + step, at]
                total = total + kern * kern * finv_ref[:, at]
            acc[i : i + step] = total
        t_ref[row : row + 1] = jnp.sum(acc[...].T, axis=0, keepdims=True)


def weights(kern, finv, tinv, rinv):
    weight = kern * kern * (kern * finv * tinv - rinv)
    high = weight.astype(BF16)
    return high, (weight - high.astype(F32)).astype(BF16)


def grad_setup(tinv, rinv_ref, points, zt, ts, rs):
    for p in range(CORES):
        ts[p] = spread(tinv[p : p + 1])
        rs[p] = spread(rinv_ref[p : p + 1])
        zt[p, :LANES] = (-SCALE * points[p].T).astype(BF16)
        zt[p, LANES:] = jnp.full((ONES, points[p].shape[0]), SCALE, BF16)


def grad_weights(block, kerns, finv_ref, ts, rs, p):
    inner = kerns[p].shape[1] // (SIDE * SIDE)
    at = pl.ds(pl.multiple_of(block * inner, inner), inner)
    return weights(
        kerns[p][:, at], finv_ref[:, at], tile_lanes(ts[p], inner), tile_lanes(rs[p], inner)
    )


def grad_block(parts, zt, c):
    sums = jnp.zeros((LANES + ONES, c.shape[0]), F32)
    for p, terms in enumerate(parts):
        for term in terms:
            sums += jnp.dot(zt[p], term, preferred_element_type=F32)
    return sums[:LANES] + sums[LANES : LANES + 1] * c.astype(F32).T


def far_body(own_ref, other_ref, rinv_ref, finv_ref, rows_ref, z_ref, zo_ref, c_ref, *outs):
    first, third, keep1, keep3, tinv_ref, zt, ts, rs = outs
    kerns = (own_ref, other_ref)
    points = (z_ref[...].astype(F32), zo_ref[...])
    tinv = 1.0 / summed(rows_ref)
    tinv_ref[...] = tinv
    grad_setup(tinv, rinv_ref, points, zt, ts, rs)
    core, x = lax.axis_index("core"), lax.axis_index("x")
    cut, wide = keep1.shape
    inner = wide // SIDE
    targets = {1: (first, 0, keep1, 0), 3: (keep3, 0, third, 0), 2: (first, wide, third, wide)}
    for s, (low, low_at, high, high_at) in targets.items():
        for h in range(SIDE):
            block = (x ^ s) * SIDE + h
            parts = [grad_weights(block, kerns, finv_ref, ts, rs, p) for p in range(CORES)]
            grad = grad_block(parts, zt, c_ref[block_rows(block, inner, core), :])
            low[:, low_at + h * inner : low_at + (h + 1) * inner] = grad[:cut]
            high[:, high_at + h * inner : high_at + (h + 1) * inner] = grad[cut:]


def near_body(own_ref, other_ref, rinv_ref, finv_ref, tinv_ref, z_ref, zo_ref, c_ref, *outs):
    piece, own, other, zt, ts, rs, acc = outs
    kerns = (own_ref, other_ref)
    points = (z_ref[...].astype(F32), zo_ref[...])
    grad_setup(tinv_ref[...], rinv_ref, points, zt, ts, rs)
    acc[...] = jnp.zeros_like(acc)
    core, x = lax.axis_index("core"), lax.axis_index("x")
    inner = piece.shape[1] // SIDE
    for s in range(SIDE):
        for h in range(SIDE):
            block = (x ^ s) * SIDE + h
            c = c_ref[block_rows(block, inner, core), :]
            wide = jnp.concatenate([c, jnp.ones((inner, LANES), BF16)], axis=1)
            parts = [grad_weights(block, kerns, finv_ref, ts, rs, p) for p in range(CORES)]
            for p, (high, low) in enumerate(parts):
                acc[p] += jnp.dot(high, wide, preferred_element_type=F32) + jnp.dot(
                    low, wide, preferred_element_type=F32
                )
            if s == 0:
                piece[:, h * inner : (h + 1) * inner] = grad_block(parts, zt, c)
    for p, out in enumerate((own, other)):
        sums = acc[p]
        out[...] = SCALE * (sums[:, LANES:] * points[p] - sums[:, :LANES])


def second_body(keep1, keep3, first, third, to_first, to_third):
    wide = keep1.shape[1]
    to_first[...] = keep1[...] + third[:, wide:]
    to_third[...] = keep3[...] + first[:, wide:]


def split_body(near, first, third, from_first, from_third, *outs):
    h = lax.axis_index("h")
    cut = from_third.shape[0]
    inner = outs[0].shape[1]
    for t in range(SIDE):
        at = pl.ds(pl.multiple_of((h ^ t) * inner, inner), inner)
        outs[t][:cut] = near[:cut, at] + first[:, at] + from_third[:, at]
        outs[t][cut:] = near[cut:, at] + third[:, at] + from_first[:, at]


def final_body(*refs):
    refs[SIDE][...] = four(refs[:SIDE]).T


VMEM = pl.BlockSpec(memory_space=pltpu.VMEM)


def call(body, outs, *args, scratch=(), limit=2, name=None, flops=0, specs=None):
    shapes = tuple(o if hasattr(o, "dtype") else jax.ShapeDtypeStruct(o, F32) for o in outs)
    moved = sum(a.size * a.dtype.itemsize for a in args)
    out = pl.pallas_call(
        body,
        out_shape=shapes,
        in_specs=specs or [VMEM] * len(args),
        out_specs=tuple(VMEM for _ in outs),
        scratch_shapes=scratch,
        compiler_params=pltpu.CompilerParams(vmem_limit_bytes=limit * MIB),
        cost_estimate=pl.CostEstimate(flops=flops, bytes_accessed=moved, transcendentals=0),
        name=name,
    )(*args)
    return out if len(out) > 1 else out[0]


def swap(v, axis, s):
    return lax.ppermute(v, axis, [(i, i ^ s) for i in range(lax.axis_size(axis))])


def around(pieces, axis):
    return [pieces[0]] + [swap(pieces[s], axis, s) for s in (1, 3, 2)]


def body(embeddings, centres, prior_freq):
    half, width = embeddings.shape
    count = centres.shape[0] // CORES
    inner = count // (SIDE * SIDE)
    prior = prior_freq.reshape(1, centres.shape[0])
    rows = (CORES, half)

    def over_ctr(v):
        parts = lax.axis_size("zl") * lax.axis_size("y")
        v = call(swap_add_body, [(parts, *rows)], v, swap(v, "core", 1), name="sum_core")
        return lax.all_to_all(v, ("zl", "y"), 0, 0)

    z_own = embeddings.astype(F32)
    z_other = swap(z_own, "core", 1)
    kern_scratch = [pltpu.VMEM((half, width), BF16), pltpu.VMEM((half, LANES), F32)]
    kern_own, row, ct, norms = call(
        own_body,
        [(half, count), (1, half), jax.ShapeDtypeStruct((width, count), BF16), (1, count)],
        z_own,
        centres,
        scratch=kern_scratch,
        limit=16,
        name="kern_own",
    )
    kern_other, row = call(
        other_body,
        [(half, count), rows],
        z_other,
        ct,
        norms,
        row,
        scratch=kern_scratch,
        limit=16,
        name="kern_other",
    )
    freq, rinv = call(
        freq_body,
        [(1, count), rows],
        kern_own,
        kern_other,
        over_ctr(row),
        limit=20,
        name="freq",
    )
    freq = call(add_body, [freq.shape], *around([freq] * SIDE, "x"), name="sum_x")
    target, finv = call(
        target_body,
        [rows, (1, count)],
        kern_own,
        kern_other,
        *around([freq] * SIDE, "h"),
        prior,
        scratch=[pltpu.VMEM((half, LANES), F32)],
        limit=20,
        name="target",
    )
    setup = [
        pltpu.VMEM((CORES, width + ONES, half), BF16),
        pltpu.VMEM((CORES, half, LANES), F32),
        pltpu.VMEM((CORES, half, LANES), F32),
    ]
    sums = (CORES, half, 2 * LANES)
    piece = (width, SIDE * inner)
    half_piece = (width // 2, SIDE * inner)
    pair = (width // 2, 2 * SIDE * inner)
    first, third, keep1, keep3, tinv = call(
        far_body,
        [pair, pair, half_piece, half_piece, rows],
        kern_own,
        kern_other,
        rinv,
        finv,
        over_ctr(target),
        embeddings,
        z_other,
        centres,
        scratch=setup,
        limit=24,
        name="grad_far",
    )
    first, third = swap(first, "x", 1), swap(third, "x", 3)
    near, mine, other = call(
        near_body,
        [piece, (half, width), (half, width)],
        kern_own,
        kern_other,
        rinv,
        finv,
        tinv,
        embeddings,
        z_other,
        centres,
        scratch=setup + [pltpu.VMEM(sums, F32)],
        limit=24,
        name="grad_near",
    )
    embed = call(add_body, [mine.shape], mine, swap(other, "core", 1), name="embed_core")
    embed = call(add_body, [mine.shape], embed, swap(embed, "zl", 1), name="embed_zl")
    to_first, to_third = call(
        second_body, [half_piece] * 2, keep1, keep3, first, third, name="second", flops=HINT
    )
    by_h = call(
        split_body,
        [(width, inner)] * SIDE,
        near,
        first,
        third,
        swap(to_first, "x", 1),
        swap(to_third, "x", 3),
        name="split",
        flops=HINT,
    )
    embed = call(add_body, [mine.shape], embed, swap(embed, "y", 1), name="embed_y")
    embed = call(add_body, [mine.shape], embed, swap(embed, "y", 3), name="embed")
    grad = call(final_body, [(inner, width)], *around(by_h, "h"), name="final", flops=HINT)
    return embed, grad.reshape(1, inner, width)


def solution(mesh):
    names = ("x", "h", "core", "zl", "y")
    grid = jax.sharding.Mesh(mesh.devices.reshape(SIDE, SIDE, CORES, CORES, SIDE), names)
    pts, ctr = names[:3], names[3:]
    in_specs = (P(pts, None), P(ctr, None), P(ctr))
    out_specs = (P(pts, None), P(ctr, pts, None))
    return jax.shard_map(body, mesh=grid, in_specs=in_specs, out_specs=out_specs, check_vma=False)
```

```python
import functools

import jax
import jax.numpy as jnp
from jax import lax
from jax.experimental import pallas as pl
from jax.experimental.pallas import tpu as pltpu
from jax.sharding import PartitionSpec as P

SIDE = 4
CORES = 2
LANES = 128
ONES = 16
SCALE = 128.0
MIB = 2**20
HINT = 10**10
HOPS = (2, 1, 3, 0)
F32 = jnp.float32
BF16 = jnp.bfloat16


def tile_lanes(column, width):
    return jnp.concatenate([column] * (width // LANES), axis=1)


def spread(row):
    return jnp.broadcast_to(row, (LANES, row.shape[1])).T


def four(refs):
    a, b, c, d = refs
    return (a[...] + b[...]) + (c[...] + d[...])


def block_rows(block, inner, core):
    return pl.ds(pl.multiple_of((block * CORES + core) * inner, inner), inner)


def kern_block(za, zn, ct, norms):
    cross = jnp.dot(za[...], ct, preferred_element_type=F32)
    return 1.0 / (cross + norms + tile_lanes(zn[...], ct.shape[1]))


def kern_setup(part, za, zn):
    zn[...] = jnp.broadcast_to(jnp.sum(part * part, axis=1, keepdims=True) + 1.0, zn.shape)
    za[...] = (-2.0 * part).astype(BF16)


def lane_sums(total, kern):
    for g in range(kern.shape[1] // LANES):
        total = total + kern[:, g * LANES : (g + 1) * LANES]
    return total


def own_body(z_ref, c_ref, kern_ref, row_ref, ct_ref, norm_ref, za, zn):
    half, count = kern_ref.shape
    inner = count // (SIDE * SIDE)
    core = lax.axis_index("core")
    kern_setup(z_ref[...], za, zn)
    total = jnp.zeros((half, LANES), F32)
    for b in range(count // inner):
        at = slice(b * inner, (b + 1) * inner)
        ct = c_ref[block_rows(b, inner, core), :].astype(F32).T
        norms = jnp.sum(ct * ct, axis=0, keepdims=True)
        ct = ct.astype(BF16)
        ct_ref[:, at] = ct
        norm_ref[:, at] = norms
        kern = kern_block(za, zn, ct, norms)
        kern_ref[:, at] = kern
        total = lane_sums(total, kern)
    row_ref[...] = jnp.sum(total.T, axis=0, keepdims=True)


def other_body(zo_ref, ct_ref, norm_ref, row_ref, kern_ref, rows_ref, za, zn):
    half, count = kern_ref.shape
    step = 256
    rows_ref[:1] = row_ref[...]
    kern_setup(zo_ref[...], za, zn)
    total = jnp.zeros((half, LANES), F32)
    for b in range(count // step):
        at = slice(b * step, (b + 1) * step)
        kern = kern_block(za, zn, ct_ref[:, at], norm_ref[:, at])
        kern_ref[:, at] = kern
        total = lane_sums(total, kern)
    rows_ref[1:] = jnp.sum(total.T, axis=0, keepdims=True)


def swap_core_body(mine, theirs, out):
    out[:1] = mine[:1] + theirs[1:]
    out[1:] = mine[1:] + theirs[:1]


def swap_add_body(mine, theirs, out):
    for n in range(out.shape[0]):
        out[n, :1] = mine[:1] + theirs[1:]
        out[n, 1:] = mine[1:] + theirs[:1]


def summed(ref):
    total = ref[0]
    for n in range(1, ref.shape[0]):
        total = total + ref[n]
    return total


def add_body(*refs):
    refs[-1][...] = four(refs[:-1]) if len(refs) == 5 else refs[0][...] + refs[1][...]


def freq_body(own_ref, other_ref, rows_ref, f_ref, rinv_ref):
    half, count = own_ref.shape
    rinv = 1.0 / summed(rows_ref)
    rinv_ref[...] = rinv
    step = 2048
    scales = [spread(rinv[p : p + 1]) for p in range(CORES)]
    for base in range(0, count, step):
        at = slice(base, base + step)
        total = jnp.zeros((8, step), F32)
        for kern_ref, scale in zip((own_ref, other_ref), scales):
            for i in range(0, half, 8):
                total = total + kern_ref[i : i + 8, at] * tile_lanes(scale[i : i + 8], step)
        f_ref[:, at] = jnp.sum(total, axis=0, keepdims=True)


def target_body(own_ref, other_ref, f0, f1, f2, f3, prior_ref, t_ref, finv_ref, acc):
    half, count = own_ref.shape
    inner = count // (SIDE * SIDE)
    core = lax.axis_index("core")
    prior = [prior_ref[:, block_rows(b, inner, core)] for b in range(count // inner)]
    finv_ref[...] = 1.0 / (four((f0, f1, f2, f3)) + jnp.concatenate(prior, axis=1))
    step = 64
    for row, kern_ref in ((0, own_ref), (1, other_ref)):
        for i in range(0, half, step):
            total = jnp.zeros((step, LANES), F32)
            for g in range(count // LANES):
                at = slice(g * LANES, (g + 1) * LANES)
                kern = kern_ref[i : i + step, at]
                total = total + kern * kern * finv_ref[:, at]
            acc[i : i + step] = total
        t_ref[row : row + 1] = jnp.sum(acc[...].T, axis=0, keepdims=True)


def two_terms(value):
    high = value.astype(BF16)
    return high, (value - high.astype(F32)).astype(BF16)


def weights(kern, finv, tinv, rinv):
    return two_terms(kern * kern * (kern * finv * tinv - rinv))


def grad_setup(tinv, rinv_ref, points, zt, ts, rs):
    for p in range(CORES):
        ts[p] = spread(tinv[p : p + 1])
        rs[p] = spread(rinv_ref[p : p + 1])
        zt[p, :LANES] = (-SCALE * points[p].T).astype(BF16)
        zt[p, LANES:] = jnp.full((ONES, points[p].shape[0]), SCALE, BF16)


def grad_weights(block, kerns, finv_ref, ts, rs, p):
    inner = kerns[p].shape[1] // (SIDE * SIDE)
    at = pl.ds(pl.multiple_of(block * inner, inner), inner)
    return weights(
        kerns[p][:, at], finv_ref[:, at], tile_lanes(ts[p], inner), tile_lanes(rs[p], inner)
    )


def grad_block(parts, zt, c):
    sums = jnp.zeros((LANES + ONES, c.shape[0]), F32)
    for p, terms in enumerate(parts):
        for term in terms:
            sums += jnp.dot(zt[p], term, preferred_element_type=F32)
    return sums[:LANES] + sums[LANES : LANES + 1] * c.astype(F32).T


def embed_sums(kern_ref, c_ref, out, power):
    half, count = kern_ref.shape
    inner = count // (SIDE * SIDE)
    core = lax.axis_index("core")
    total = jnp.zeros(out.shape, F32)
    for b in range(count // inner):
        at = slice(b * inner, (b + 1) * inner)
        c = c_ref[block_rows(b, inner, core), :]
        wide = jnp.concatenate([c, jnp.ones((inner, LANES), BF16)], axis=1)
        for term in two_terms(power(kern_ref[:, at], at)):
            total += jnp.dot(term, wide, preferred_element_type=F32)
    out[...] = total


def square_body(kern_ref, c_ref, out):
    embed_sums(kern_ref, c_ref, out, lambda kern, at: kern * kern)


def cube_body(kern_ref, finv_ref, c_ref, out):
    embed_sums(kern_ref, c_ref, out, lambda kern, at: kern * kern * (kern * finv_ref[:, at]))


def embed_body(a0, a1, b0, b1, t0, t1, t2, t3, rinv_ref, z_ref, zo_ref, own, other):
    tinv = 1.0 / four((t0, t1, t2, t3))
    points = (z_ref[...].astype(F32), zo_ref[...])
    for p, (cubes, squares, out) in enumerate(((a0, b0, own), (a1, b1, other))):
        ts, rs = spread(tinv[p : p + 1]), spread(rinv_ref[p : p + 1])
        total = ts * cubes[:, LANES:] - rs * squares[:, LANES:]
        moved = ts * cubes[:, :LANES] - rs * squares[:, :LANES]
        out[...] = SCALE * (total * points[p] - moved)


def centre_grads(s, refs, tinv, outs):
    kerns, rinv_ref, finv_ref, z_ref, zo_ref, c_ref, zt, ts, rs = refs
    points = (z_ref[...].astype(F32), zo_ref[...])
    grad_setup(tinv, rinv_ref, points, zt, ts, rs)
    core, x, h = lax.axis_index("core"), lax.axis_index("x"), lax.axis_index("h")
    inner = kerns[0].shape[1] // (SIDE * SIDE)
    for step, out in zip(s, outs):
        for n, hop in enumerate(HOPS):
            block = (x ^ step) * SIDE + (h ^ hop)
            parts = [grad_weights(block, kerns, finv_ref, ts, rs, p) for p in range(CORES)]
            grad = grad_block(parts, zt, c_ref[block_rows(block, inner, core), :])
            at = slice(n * inner, (n + 1) * inner)
            if len(out) == 1:
                out[0][:, at] = grad
            else:
                cut = out[0].shape[0]
                out[0][:, at] = grad[:cut]
                out[1][:, at] = grad[cut:]


def far_body(own, other, rinv, finv, t0, t1, t2, t3, z, zo, c, low, high, tinv_ref, zt, ts, rs):
    tinv = 1.0 / four((t0, t1, t2, t3))
    tinv_ref[...] = tinv
    refs = ((own, other), rinv, finv, z, zo, c, zt, ts, rs)
    centre_grads((2,), refs, tinv, ((low, high),))


def mid_body(own, other, rinv, finv, tinv, z, zo, c, first, third, zt, ts, rs):
    refs = ((own, other), rinv, finv, z, zo, c, zt, ts, rs)
    centre_grads((1, 3), refs, tinv[...], ((first,), (third,)))


def near_body(own, other, rinv, finv, tinv, z, zo, c, near, zt, ts, rs):
    refs = ((own, other), rinv, finv, z, zo, c, zt, ts, rs)
    centre_grads((0,), refs, tinv[...], ((near,),))


def second_body(base, first, third, low, high, to_first, to_third):
    cut = low.shape[0]
    at = slice(base, base + to_first.shape[1])
    to_first[:cut] = first[:cut, at]
    to_first[cut:] = first[cut:, at] + high[:, at]
    to_third[:cut] = third[:cut, at] + low[:, at]
    to_third[cut:] = third[cut:, at]


def split_body(base, near, first, third, *outs):
    inner = outs[0].shape[1]
    for n, out in enumerate(outs):
        at = slice(n * inner, (n + 1) * inner)
        out[...] = near[:, base + n * inner : base + (n + 1) * inner] + first[:, at] + third[:, at]


def final_body(p0, p1, p2, p3, mine, theirs, grad, embed):
    grad[...] = four((p0, p1, p2, p3)).T
    embed[...] = mine[...] + theirs[...]


VMEM = pl.BlockSpec(memory_space=pltpu.VMEM)
ANY = pl.BlockSpec(memory_space=pl.ANY)


def call(body, outs, *args, scratch=(), limit=2, name=None, flops=0, after=()):
    used = len(args)

    def kernel(*refs):
        body(*refs[:used], *refs[used + len(after) :])

    args = (*args, *after)
    shapes = tuple(o if hasattr(o, "dtype") else jax.ShapeDtypeStruct(o, F32) for o in outs)
    moved = sum(a.size * a.dtype.itemsize for a in args)
    out = pl.pallas_call(
        kernel,
        out_shape=shapes,
        in_specs=[VMEM] * used + [ANY] * len(after),
        out_specs=tuple(VMEM for _ in outs),
        scratch_shapes=scratch,
        compiler_params=pltpu.CompilerParams(vmem_limit_bytes=limit * MIB),
        cost_estimate=pl.CostEstimate(flops=flops, bytes_accessed=moved, transcendentals=0),
        name=name,
    )(*args)
    return out if len(out) > 1 else out[0]


def swap(v, axis, s):
    return lax.ppermute(v, axis, [(i, i ^ s) for i in range(lax.axis_size(axis))])


def around(pieces, axis):
    return [pieces[0]] + [swap(pieces[s], axis, s) for s in (1, 3, 2)]


def body(embeddings, centres, prior_freq):
    half, width = embeddings.shape
    count = centres.shape[0] // CORES
    inner = count // (SIDE * SIDE)
    prior = prior_freq.reshape(1, centres.shape[0])
    rows = (CORES, half)

    def over_ctr(v):
        parts = lax.axis_size("zl") * lax.axis_size("y")
        v = call(swap_add_body, [(parts, *rows)], v, swap(v, "core", 1), name="sum_core")
        return lax.all_to_all(v, ("zl", "y"), 0, 0)

    z_own = embeddings.astype(F32)
    z_other = swap(z_own, "core", 1)
    kern_scratch = [pltpu.VMEM((half, width), BF16), pltpu.VMEM((half, LANES), F32)]
    kern_own, row, ct, norms = call(
        own_body,
        [(half, count), (1, half), jax.ShapeDtypeStruct((width, count), BF16), (1, count)],
        z_own,
        centres,
        scratch=kern_scratch,
        limit=16,
        name="kern_own",
    )
    kern_other, row = call(
        other_body,
        [(half, count), rows],
        z_other,
        ct,
        norms,
        row,
        scratch=kern_scratch,
        limit=16,
        name="kern_other",
    )
    freq, rinv = call(
        freq_body,
        [(1, count), rows],
        kern_own,
        kern_other,
        over_ctr(row),
        limit=20,
        name="freq",
    )
    kerns = (kern_own, kern_other)
    sums = (half, 2 * LANES)
    work = 4 * half * count * 2 * LANES
    squares = [
        call(square_body, [sums], kern, centres, limit=20, name="squares", flops=work)
        for kern in kerns
    ]
    freq = call(
        add_body, [freq.shape], *around([freq] * SIDE, "x"), name="sum_x", after=squares[:1]
    )
    freq = around([freq] * SIDE, "h")
    target, finv = call(
        target_body,
        [rows, (1, count)],
        *kerns,
        *freq,
        prior,
        scratch=[pltpu.VMEM((half, LANES), F32)],
        limit=20,
        name="target",
        after=squares[1:],
    )
    cubes = [
        call(cube_body, [sums], kern, finv, centres, limit=20, name="cubes", flops=work)
        for kern in kerns
    ]
    target = call(swap_core_body, [rows], target, swap(target, "core", 1), name="target_core")
    target = call(add_body, [rows], target, swap(target, "zl", 1), name="target_zl")
    target = around([target] * SIDE, "y")

    setup = [
        pltpu.VMEM((CORES, width + ONES, half), BF16),
        pltpu.VMEM((CORES, half, LANES), F32),
        pltpu.VMEM((CORES, half, LANES), F32),
    ]
    piece, part, pair = (width, SIDE * inner), (width // 2, SIDE * inner), (width, 2 * inner)
    base = (*kerns, rinv, finv)
    data = (embeddings, z_other, centres)
    low, high, tinv = call(
        far_body, [part, part, rows], *base, *target, *data, scratch=setup, limit=24, name="grad_far"
    )
    low, high = swap(low, "x", 1), swap(high, "x", 3)
    mine, other = call(
        embed_body,
        [(half, width)] * 2,
        *cubes,
        *squares,
        *target,
        rinv,
        embeddings,
        z_other,
        limit=8,
        name="embed_part",
    )
    first, third = call(
        mid_body, [piece, piece], *base, tinv, *data, scratch=setup, limit=24, name="grad_mid"
    )
    near = call(near_body, [piece], *base, tinv, *data, scratch=setup, limit=24, name="grad_near")

    def second(start, name, after=()):
        to_first, to_third = call(
            functools.partial(second_body, start),
            [pair] * 2,
            first,
            third,
            low,
            high,
            name=name,
            flops=HINT,
            after=after,
        )
        return swap(to_first, "x", 1), swap(to_third, "x", 3)

    first_a, third_a = second(0, "second_a")
    first_b, third_b = second(2 * inner, "second_b", after=[near])

    embed = call(add_body, [mine.shape], mine, swap(other, "core", 1), name="embed_core")
    embed = call(add_body, [mine.shape], embed, swap(embed, "zl", 1), name="embed_zl")
    embed = call(add_body, [mine.shape], embed, swap(embed, "y", 1), name="embed_y")
    embed = (embed, swap(embed, "y", 3))

    block = (width, inner)
    def split(start, pieces, name, after=()):
        return call(
            functools.partial(split_body, start),
            [block] * 2,
            near,
            *pieces,
            name=name,
            flops=HINT,
            after=after,
        )

    far2, far1 = split(0, (first_a, third_a), "split_a")
    h2, h1 = swap(far2, "h", 2), swap(far1, "h", 1)
    h3, h0 = split(2 * inner, (first_b, third_b), "split_b", after=[far2])
    grad, embed = call(
        final_body,
        [(inner, width), (half, width)],
        h0,
        h1,
        h2,
        swap(h3, "h", 3),
        *embed,
        name="final",
        flops=HINT,
    )
    return embed, grad.reshape(1, inner, width)


def solution(mesh):
    names = ("x", "h", "core", "zl", "y")
    grid = jax.sharding.Mesh(mesh.devices.reshape(SIDE, SIDE, CORES, CORES, SIDE), names)
    pts, ctr = names[:3], names[3:]
    in_specs = (P(pts, None), P(ctr, None), P(ctr))
    out_specs = (P(pts, None), P(ctr, pts, None))
    return jax.shard_map(body, mesh=grid, in_specs=in_specs, out_specs=out_specs, check_vma=False)
```

```python
import functools

import jax
import jax.numpy as jnp
from jax import lax
from jax.experimental import pallas as pl
from jax.experimental.pallas import tpu as pltpu
from jax.sharding import PartitionSpec as P

SIDE = 4
CORES = 2
LANES = 128
ONES = 16
SCALE = 128.0
MIB = 2**20
HINT = 10**10
HOPS = (2, 1, 3, 0)
F32 = jnp.float32
BF16 = jnp.bfloat16


def tile_lanes(column, width):
    return jnp.concatenate([column] * (width // LANES), axis=1)


def spread(row):
    return jnp.broadcast_to(row, (LANES, row.shape[1])).T


def four(refs):
    a, b, c, d = refs
    return (a[...] + b[...]) + (c[...] + d[...])


def block_rows(block, inner, core):
    return pl.ds(pl.multiple_of((block * CORES + core) * inner, inner), inner)


def kern_block(za, zn, ct, norms):
    cross = jnp.dot(za[...], ct, preferred_element_type=F32)
    return 1.0 / (cross + norms + tile_lanes(zn[...], ct.shape[1]))


def kern_setup(part, za, zn):
    zn[...] = jnp.broadcast_to(jnp.sum(part * part, axis=1, keepdims=True) + 1.0, zn.shape)
    za[...] = (-2.0 * part).astype(BF16)


def lane_sums(total, kern):
    for g in range(kern.shape[1] // LANES):
        total = total + kern[:, g * LANES : (g + 1) * LANES]
    return total


def own_body(z_ref, c_ref, kern_ref, row_ref, ct_ref, norm_ref, za, zn):
    half, count = kern_ref.shape
    inner = count // (SIDE * SIDE)
    core = lax.axis_index("core")
    kern_setup(z_ref[...], za, zn)
    total = jnp.zeros((half, LANES), F32)
    for b in range(count // inner):
        at = slice(b * inner, (b + 1) * inner)
        ct = c_ref[block_rows(b, inner, core), :].astype(F32).T
        norms = jnp.sum(ct * ct, axis=0, keepdims=True)
        ct = ct.astype(BF16)
        ct_ref[:, at] = ct
        norm_ref[:, at] = norms
        kern = kern_block(za, zn, ct, norms)
        kern_ref[:, at] = kern
        total = lane_sums(total, kern)
    row_ref[...] = jnp.sum(total.T, axis=0, keepdims=True)


def other_body(zo_ref, ct_ref, norm_ref, row_ref, kern_ref, rows_ref, za, zn):
    half, count = kern_ref.shape
    step = 256
    rows_ref[:1] = row_ref[...]
    kern_setup(zo_ref[...], za, zn)
    total = jnp.zeros((half, LANES), F32)
    for b in range(count // step):
        at = slice(b * step, (b + 1) * step)
        kern = kern_block(za, zn, ct_ref[:, at], norm_ref[:, at])
        kern_ref[:, at] = kern
        total = lane_sums(total, kern)
    rows_ref[1:] = jnp.sum(total.T, axis=0, keepdims=True)


def swap_core_body(mine, theirs, out):
    out[:1] = mine[:1] + theirs[1:]
    out[1:] = mine[1:] + theirs[:1]


def swap_add_body(mine, theirs, out):
    for n in range(out.shape[0]):
        out[n, :1] = mine[:1] + theirs[1:]
        out[n, 1:] = mine[1:] + theirs[:1]


def summed(ref):
    total = ref[0]
    for n in range(1, ref.shape[0]):
        total = total + ref[n]
    return total


def add_body(*refs):
    refs[-1][...] = four(refs[:-1]) if len(refs) == 5 else refs[0][...] + refs[1][...]


def freq_body(own_ref, other_ref, rows_ref, f_ref, rinv_ref, scale_ref):
    half, count = own_ref.shape
    rinv = 1.0 / summed(rows_ref)
    rinv_ref[...] = rinv
    step, rows = 2048, 64
    scales = [spread(rinv[p : p + 1]) for p in range(CORES)]
    for p in range(CORES):
        scale_ref[p] = scales[p]
    for base in range(0, count, step):
        at = slice(base, base + step)
        total = jnp.zeros((8, step), F32)
        for p, kern_ref in enumerate((own_ref, other_ref)):

            def add_rows(n, total, p=p, kern_ref=kern_ref, at=at):
                for i in range(0, rows, 8):
                    tile = pl.ds(pl.multiple_of(n * rows + i, 8), 8)
                    total = total + kern_ref[tile, at] * tile_lanes(scale_ref[p, tile, :], step)
                return total

            total = lax.fori_loop(0, half // rows, add_rows, total)
        f_ref[:, at] = jnp.sum(total, axis=0, keepdims=True)


def target_body(own_ref, other_ref, f0, f1, f2, f3, prior_ref, t_ref, finv_ref, acc):
    half, count = own_ref.shape
    inner = count // (SIDE * SIDE)
    core = lax.axis_index("core")
    prior = [prior_ref[:, block_rows(b, inner, core)] for b in range(count // inner)]
    finv_ref[...] = 1.0 / (four((f0, f1, f2, f3)) + jnp.concatenate(prior, axis=1))
    step = 64
    for row, kern_ref in ((0, own_ref), (1, other_ref)):

        @pl.loop(0, half // (2 * step))
        def _(n):
            for i in range(2):
                tile = pl.ds(pl.multiple_of((2 * n + i) * step, step), step)
                total = jnp.zeros((step, LANES), F32)
                for g in range(count // LANES):
                    at = slice(g * LANES, (g + 1) * LANES)
                    kern = kern_ref[tile, at]
                    total = total + kern * kern * finv_ref[:, at]
                acc[tile, :] = total

        t_ref[row : row + 1] = jnp.sum(acc[...].T, axis=0, keepdims=True)


def two_terms(value):
    high = value.astype(BF16)
    return high, (value - high.astype(F32)).astype(BF16)


def weights(kern, finv, tinv, rinv):
    return two_terms(kern * kern * (kern * finv * tinv - rinv))


def grad_setup(tinv, rinv_ref, points, zt, ts, rs):
    for p in range(CORES):
        ts[p] = spread(tinv[p : p + 1])
        rs[p] = spread(rinv_ref[p : p + 1])
        zt[p, :LANES] = (-SCALE * points[p].T).astype(BF16)
        zt[p, LANES:] = jnp.full((ONES, points[p].shape[0]), SCALE, BF16)


def grad_weights(block, kerns, finv_ref, ts, rs, p):
    inner = kerns[p].shape[1] // (SIDE * SIDE)
    at = pl.ds(pl.multiple_of(block * inner, inner), inner)
    return weights(
        kerns[p][:, at], finv_ref[:, at], tile_lanes(ts[p], inner), tile_lanes(rs[p], inner)
    )


def grad_block(parts, zt, c):
    sums = jnp.zeros((LANES + ONES, c.shape[0]), F32)
    for p, terms in enumerate(parts):
        for term in terms:
            sums += jnp.dot(zt[p], term, preferred_element_type=F32)
    return sums[:LANES] + sums[LANES : LANES + 1] * c.astype(F32).T


def embed_sums(kern_ref, c_ref, out, power):
    half, count = kern_ref.shape
    inner = count // (SIDE * SIDE)
    core = lax.axis_index("core")
    step = 2 * SIDE
    out[...] = jnp.zeros_like(out)

    @pl.loop(0, count // (inner * step))
    def _(n):
        total = out[...]
        for i in range(step):
            b = n * step + i
            at = pl.ds(pl.multiple_of(b * inner, inner), inner)
            c = c_ref[block_rows(b, inner, core), :]
            wide = jnp.concatenate([c, jnp.ones((inner, LANES), BF16)], axis=1)
            for term in two_terms(power(kern_ref[:, at], at)):
                total += jnp.dot(term, wide, preferred_element_type=F32)
        out[...] = total


def square_body(kern_ref, c_ref, out):
    embed_sums(kern_ref, c_ref, out, lambda kern, at: kern * kern)


def cube_body(kern_ref, finv_ref, c_ref, out):
    embed_sums(kern_ref, c_ref, out, lambda kern, at: kern * kern * (kern * finv_ref[:, at]))


def embed_body(a0, a1, b0, b1, t0, t1, t2, t3, rinv_ref, z_ref, zo_ref, own, other):
    tinv = 1.0 / four((t0, t1, t2, t3))
    points = (z_ref[...].astype(F32), zo_ref[...])
    for p, (cubes, squares, out) in enumerate(((a0, b0, own), (a1, b1, other))):
        ts, rs = spread(tinv[p : p + 1]), spread(rinv_ref[p : p + 1])
        total = ts * cubes[:, LANES:] - rs * squares[:, LANES:]
        moved = ts * cubes[:, :LANES] - rs * squares[:, :LANES]
        out[...] = SCALE * (total * points[p] - moved)


def centre_grads(s, refs, tinv, outs):
    kerns, rinv_ref, finv_ref, z_ref, zo_ref, c_ref, zt, ts, rs = refs
    points = (z_ref[...].astype(F32), zo_ref[...])
    grad_setup(tinv, rinv_ref, points, zt, ts, rs)
    core, x, h = lax.axis_index("core"), lax.axis_index("x"), lax.axis_index("h")
    inner = kerns[0].shape[1] // (SIDE * SIDE)
    for step, out in zip(s, outs):
        for n, hop in enumerate(HOPS):
            block = (x ^ step) * SIDE + (h ^ hop)
            parts = [grad_weights(block, kerns, finv_ref, ts, rs, p) for p in range(CORES)]
            grad = grad_block(parts, zt, c_ref[block_rows(block, inner, core), :])
            at = slice(n * inner, (n + 1) * inner)
            if len(out) == 1:
                out[0][:, at] = grad
            else:
                cut = out[0].shape[0]
                out[0][:, at] = grad[:cut]
                out[1][:, at] = grad[cut:]


def far_body(own, other, rinv, finv, t0, t1, t2, t3, z, zo, c, low, high, tinv_ref, zt, ts, rs):
    tinv = 1.0 / four((t0, t1, t2, t3))
    tinv_ref[...] = tinv
    refs = ((own, other), rinv, finv, z, zo, c, zt, ts, rs)
    centre_grads((2,), refs, tinv, ((low, high),))


def mid_body(own, other, rinv, finv, tinv, z, zo, c, first, third, zt, ts, rs):
    refs = ((own, other), rinv, finv, z, zo, c, zt, ts, rs)
    centre_grads((1, 3), refs, tinv[...], ((first,), (third,)))


def near_body(own, other, rinv, finv, tinv, z, zo, c, near, zt, ts, rs):
    refs = ((own, other), rinv, finv, z, zo, c, zt, ts, rs)
    centre_grads((0,), refs, tinv[...], ((near,),))


def second_body(base, first, third, low, high, to_first, to_third):
    cut = low.shape[0]
    at = slice(base, base + to_first.shape[1])
    to_first[:cut] = first[:cut, at]
    to_first[cut:] = first[cut:, at] + high[:, at]
    to_third[:cut] = third[:cut, at] + low[:, at]
    to_third[cut:] = third[cut:, at]


def split_body(base, near, first, third, *outs):
    inner = outs[0].shape[1]
    for n, out in enumerate(outs):
        at = slice(n * inner, (n + 1) * inner)
        out[...] = near[:, base + n * inner : base + (n + 1) * inner] + first[:, at] + third[:, at]


def final_body(p0, p1, p2, p3, mine, theirs, grad, embed):
    grad[...] = four((p0, p1, p2, p3)).T
    embed[...] = mine[...] + theirs[...]


VMEM = pl.BlockSpec(memory_space=pltpu.VMEM)
ANY = pl.BlockSpec(memory_space=pl.ANY)


def call(body, outs, *args, scratch=(), limit=2, name=None, flops=0, after=()):
    used = len(args)

    def kernel(*refs):
        body(*refs[:used], *refs[used + len(after) :])

    args = (*args, *after)
    shapes = tuple(o if hasattr(o, "dtype") else jax.ShapeDtypeStruct(o, F32) for o in outs)
    moved = sum(a.size * a.dtype.itemsize for a in args)
    out = pl.pallas_call(
        kernel,
        out_shape=shapes,
        in_specs=[VMEM] * used + [ANY] * len(after),
        out_specs=tuple(VMEM for _ in outs),
        scratch_shapes=scratch,
        compiler_params=pltpu.CompilerParams(vmem_limit_bytes=limit * MIB),
        cost_estimate=pl.CostEstimate(flops=flops, bytes_accessed=moved, transcendentals=0),
        name=name,
    )(*args)
    return out if len(out) > 1 else out[0]


def swap(v, axis, s):
    return lax.ppermute(v, axis, [(i, i ^ s) for i in range(lax.axis_size(axis))])


def around(pieces, axis):
    return [pieces[0]] + [swap(pieces[s], axis, s) for s in (1, 3, 2)]


def body(embeddings, centres, prior_freq):
    half, width = embeddings.shape
    count = centres.shape[0] // CORES
    inner = count // (SIDE * SIDE)
    prior = prior_freq.reshape(1, centres.shape[0])
    rows = (CORES, half)

    def over_ctr(v):
        parts = lax.axis_size("zl") * lax.axis_size("y")
        v = call(swap_add_body, [(parts, *rows)], v, swap(v, "core", 1), name="sum_core")
        return lax.all_to_all(v, ("zl", "y"), 0, 0)

    z_own = embeddings.astype(F32)
    z_other = swap(z_own, "core", 1)
    kern_scratch = [pltpu.VMEM((half, width), BF16), pltpu.VMEM((half, LANES), F32)]
    kern_own, row, ct, norms = call(
        own_body,
        [(half, count), (1, half), jax.ShapeDtypeStruct((width, count), BF16), (1, count)],
        z_own,
        centres,
        scratch=kern_scratch,
        limit=16,
        name="kern_own",
    )
    kern_other, row = call(
        other_body,
        [(half, count), rows],
        z_other,
        ct,
        norms,
        row,
        scratch=kern_scratch,
        limit=16,
        name="kern_other",
    )
    freq, rinv = call(
        freq_body,
        [(1, count), rows],
        kern_own,
        kern_other,
        over_ctr(row),
        scratch=[pltpu.VMEM((CORES, half, LANES), F32)],
        limit=20,
        name="freq",
    )
    kerns = (kern_own, kern_other)
    sums = (half, 2 * LANES)
    work = 4 * half * count * 2 * LANES
    squares = [
        call(square_body, [sums], kern, centres, limit=20, name="squares", flops=work)
        for kern in kerns
    ]
    freq = call(
        add_body, [freq.shape], *around([freq] * SIDE, "x"), name="sum_x", after=squares[:1]
    )
    freq = around([freq] * SIDE, "h")
    target, finv = call(
        target_body,
        [rows, (1, count)],
        *kerns,
        *freq,
        prior,
        scratch=[pltpu.VMEM((half, LANES), F32)],
        limit=20,
        name="target",
        after=squares[1:],
    )
    cubes = [
        call(cube_body, [sums], kern, finv, centres, limit=20, name="cubes", flops=work)
        for kern in kerns
    ]
    target = call(swap_core_body, [rows], target, swap(target, "core", 1), name="target_core")
    target = call(add_body, [rows], target, swap(target, "zl", 1), name="target_zl")
    target = around([target] * SIDE, "y")

    setup = [
        pltpu.VMEM((CORES, width + ONES, half), BF16),
        pltpu.VMEM((CORES, half, LANES), F32),
        pltpu.VMEM((CORES, half, LANES), F32),
    ]
    piece, part, pair = (width, SIDE * inner), (width // 2, SIDE * inner), (width, 2 * inner)
    base = (*kerns, rinv, finv)
    data = (embeddings, z_other, centres)
    low, high, tinv = call(
        far_body, [part, part, rows], *base, *target, *data, scratch=setup, limit=24, name="grad_far"
    )
    low, high = swap(low, "x", 1), swap(high, "x", 3)
    mine, other = call(
        embed_body,
        [(half, width)] * 2,
        *cubes,
        *squares,
        *target,
        rinv,
        embeddings,
        z_other,
        limit=8,
        name="embed_part",
    )
    first, third = call(
        mid_body, [piece, piece], *base, tinv, *data, scratch=setup, limit=24, name="grad_mid"
    )
    near = call(near_body, [piece], *base, tinv, *data, scratch=setup, limit=24, name="grad_near")

    def second(start, name, after=()):
        to_first, to_third = call(
            functools.partial(second_body, start),
            [pair] * 2,
            first,
            third,
            low,
            high,
            name=name,
            flops=HINT,
            after=after,
        )
        return swap(to_first, "x", 1), swap(to_third, "x", 3)

    first_a, third_a = second(0, "second_a")
    first_b, third_b = second(2 * inner, "second_b", after=[near])

    embed = call(add_body, [mine.shape], mine, swap(other, "core", 1), name="embed_core")
    embed = call(add_body, [mine.shape], embed, swap(embed, "zl", 1), name="embed_zl")
    embed = call(add_body, [mine.shape], embed, swap(embed, "y", 1), name="embed_y")
    embed = (embed, swap(embed, "y", 3))

    block = (width, inner)
    def split(start, pieces, name, after=()):
        return call(
            functools.partial(split_body, start),
            [block] * 2,
            near,
            *pieces,
            name=name,
            flops=HINT,
            after=after,
        )

    far2, far1 = split(0, (first_a, third_a), "split_a")
    h2, h1 = swap(far2, "h", 2), swap(far1, "h", 1)
    h3, h0 = split(2 * inner, (first_b, third_b), "split_b", after=[far2])
    grad, embed = call(
        final_body,
        [(inner, width), (half, width)],
        h0,
        h1,
        h2,
        swap(h3, "h", 3),
        *embed,
        name="final",
        flops=HINT,
    )
    return embed, grad.reshape(1, inner, width)


def solution(mesh):
    names = ("x", "h", "core", "zl", "y")
    grid = jax.sharding.Mesh(mesh.devices.reshape(SIDE, SIDE, CORES, CORES, SIDE), names)
    pts, ctr = names[:3], names[3:]
    in_specs = (P(pts, None), P(ctr, None), P(ctr))
    out_specs = (P(pts, None), P(ctr, pts, None))
    return jax.shard_map(body, mesh=grid, in_specs=in_specs, out_specs=out_specs, check_vma=False)
```

```python
import functools

import jax
import jax.numpy as jnp
from jax import lax
from jax.experimental import pallas as pl
from jax.experimental.pallas import tpu as pltpu
from jax.sharding import PartitionSpec as P

SIDE = 4
CORES = 2
LANES = 128
ONES = 16
SCALE = 128.0
MIB = 2**20
HINT = 10**10
HOPS = (2, 1, 3, 0)
F32 = jnp.float32
BF16 = jnp.bfloat16


def tile_lanes(column, width):
    return jnp.concatenate([column] * (width // LANES), axis=1)


def spread(row):
    return jnp.broadcast_to(row, (LANES, row.shape[1])).T


def four(refs):
    a, b, c, d = refs
    return (a[...] + b[...]) + (c[...] + d[...])


def block_rows(block, inner, core):
    return pl.ds(pl.multiple_of((block * CORES + core) * inner, inner), inner)


def kern_block(za, zn, ct, norms):
    cross = jnp.dot(za[...], ct, preferred_element_type=F32)
    return 1.0 / (cross + norms + tile_lanes(zn[...], ct.shape[1]))


def kern_setup(part, za, zn):
    zn[...] = jnp.broadcast_to(jnp.sum(part * part, axis=1, keepdims=True) + 1.0, zn.shape)
    za[...] = (-2.0 * part).astype(BF16)


def lane_sums(total, kern):
    for g in range(kern.shape[1] // LANES):
        total = total + kern[:, g * LANES : (g + 1) * LANES]
    return total


def own_body(z_ref, c_ref, kern_ref, row_ref, ct_ref, norm_ref, za, zn):
    half, count = kern_ref.shape
    inner = count // (SIDE * SIDE)
    core = lax.axis_index("core")
    kern_setup(z_ref[...], za, zn)
    total = jnp.zeros((half, LANES), F32)
    for b in range(count // inner):
        at = slice(b * inner, (b + 1) * inner)
        ct = c_ref[block_rows(b, inner, core), :].astype(F32).T
        norms = jnp.sum(ct * ct, axis=0, keepdims=True)
        ct = ct.astype(BF16)
        ct_ref[:, at] = ct
        norm_ref[:, at] = norms
        kern = kern_block(za, zn, ct, norms)
        kern_ref[:, at] = kern
        total = lane_sums(total, kern)
    row_ref[...] = jnp.sum(total.T, axis=0, keepdims=True)


def other_body(zo_ref, ct_ref, norm_ref, row_ref, kern_ref, rows_ref, za, zn):
    half, count = kern_ref.shape
    step = 256
    rows_ref[:1] = row_ref[...]
    kern_setup(zo_ref[...], za, zn)
    total = jnp.zeros((half, LANES), F32)
    for b in range(count // step):
        at = slice(b * step, (b + 1) * step)
        kern = kern_block(za, zn, ct_ref[:, at], norm_ref[:, at])
        kern_ref[:, at] = kern
        total = lane_sums(total, kern)
    rows_ref[1:] = jnp.sum(total.T, axis=0, keepdims=True)


def swap_core_body(mine, theirs, out):
    out[:1] = mine[:1] + theirs[1:]
    out[1:] = mine[1:] + theirs[:1]


def swap_add_body(mine, theirs, out):
    for n in range(out.shape[0]):
        out[n, :1] = mine[:1] + theirs[1:]
        out[n, 1:] = mine[1:] + theirs[:1]


def summed(ref):
    total = ref[0]
    for n in range(1, ref.shape[0]):
        total = total + ref[n]
    return total


def add_body(*refs):
    refs[-1][...] = four(refs[:-1]) if len(refs) == 5 else refs[0][...] + refs[1][...]


def freq_body(own_ref, other_ref, rows_ref, f_ref, rinv_ref, scale_ref):
    half, count = own_ref.shape
    rinv = 1.0 / summed(rows_ref)
    rinv_ref[...] = rinv
    step, rows = 2048, 64
    scales = [spread(rinv[p : p + 1]) for p in range(CORES)]
    for p in range(CORES):
        scale_ref[p] = scales[p]
    for base in range(0, count, step):
        at = slice(base, base + step)
        total = jnp.zeros((8, step), F32)
        for p, kern_ref in enumerate((own_ref, other_ref)):

            def add_rows(n, total, p=p, kern_ref=kern_ref, at=at):
                for i in range(0, rows, 8):
                    tile = pl.ds(pl.multiple_of(n * rows + i, 8), 8)
                    total = total + kern_ref[tile, at] * tile_lanes(scale_ref[p, tile, :], step)
                return total

            total = lax.fori_loop(0, half // rows, add_rows, total)
        f_ref[:, at] = jnp.sum(total, axis=0, keepdims=True)


def target_body(own_ref, other_ref, f0, f1, f2, f3, prior_ref, t_ref, finv_ref, acc):
    half, count = own_ref.shape
    inner = count // (SIDE * SIDE)
    core = lax.axis_index("core")
    prior = [prior_ref[:, block_rows(b, inner, core)] for b in range(count // inner)]
    finv_ref[...] = 1.0 / (four((f0, f1, f2, f3)) + jnp.concatenate(prior, axis=1))
    step = 64
    for row, kern_ref in ((0, own_ref), (1, other_ref)):

        for i in range(0, half, step):
            total = jnp.zeros((step, LANES), F32)
            for g in range(count // LANES):
                at = slice(g * LANES, (g + 1) * LANES)
                kern = kern_ref[i : i + step, at]
                total = total + kern * kern * finv_ref[:, at]
            acc[i : i + step] = total

        t_ref[row : row + 1] = jnp.sum(acc[...].T, axis=0, keepdims=True)


def two_terms(value):
    high = value.astype(BF16)
    return high, (value - high.astype(F32)).astype(BF16)


def weights(kern, finv, tinv, rinv):
    return two_terms(kern * kern * (kern * finv * tinv - rinv))


def grad_setup(tinv, rinv_ref, points, zt, ts, rs):
    for p in range(CORES):
        ts[p] = spread(tinv[p : p + 1])
        rs[p] = spread(rinv_ref[p : p + 1])
        zt[p, :LANES] = (-SCALE * points[p].T).astype(BF16)
        zt[p, LANES:] = jnp.full((ONES, points[p].shape[0]), SCALE, BF16)


def grad_weights(block, kerns, finv_ref, ts, rs, p):
    inner = kerns[p].shape[1] // (SIDE * SIDE)
    at = pl.ds(pl.multiple_of(block * inner, inner), inner)
    return weights(
        kerns[p][:, at], finv_ref[:, at], tile_lanes(ts[p], inner), tile_lanes(rs[p], inner)
    )


def grad_block(parts, zt, c):
    sums = jnp.zeros((LANES + ONES, c.shape[0]), F32)
    for p, terms in enumerate(parts):
        for term in terms:
            sums += jnp.dot(zt[p], term, preferred_element_type=F32)
    return sums[:LANES] + sums[LANES : LANES + 1] * c.astype(F32).T


def embed_sums(kern_ref, c_ref, out, power):
    half, count = kern_ref.shape
    inner = count // (SIDE * SIDE)
    core = lax.axis_index("core")
    step = 2 * SIDE
    out[...] = jnp.zeros_like(out)

    @pl.loop(0, count // (inner * step))
    def _(n):
        total = out[...]
        for i in range(step):
            b = n * step + i
            at = pl.ds(pl.multiple_of(b * inner, inner), inner)
            c = c_ref[block_rows(b, inner, core), :]
            wide = jnp.concatenate([c, jnp.ones((inner, LANES), BF16)], axis=1)
            for term in two_terms(power(kern_ref[:, at], at)):
                total += jnp.dot(term, wide, preferred_element_type=F32)
        out[...] = total


def square_body(kern_ref, c_ref, out):
    embed_sums(kern_ref, c_ref, out, lambda kern, at: kern * kern)


def cube_body(kern_ref, finv_ref, c_ref, out):
    embed_sums(kern_ref, c_ref, out, lambda kern, at: kern * kern * (kern * finv_ref[:, at]))


def embed_grads(sums, tinv, rinv_ref, points, outs):
    for p, (cubes, squares, out) in enumerate(zip(sums[:CORES], sums[CORES:], outs)):
        ts, rs = spread(tinv[p : p + 1]), spread(rinv_ref[p : p + 1])
        total = ts * cubes[:, LANES:] - rs * squares[:, LANES:]
        moved = ts * cubes[:, :LANES] - rs * squares[:, :LANES]
        out[...] = SCALE * (total * points[p] - moved)


def centre_grads(s, refs, tinv, outs):
    kerns, rinv_ref, finv_ref, z_ref, zo_ref, c_ref, zt, ts, rs = refs
    points = (z_ref[...].astype(F32), zo_ref[...])
    grad_setup(tinv, rinv_ref, points, zt, ts, rs)
    core, x, h = lax.axis_index("core"), lax.axis_index("x"), lax.axis_index("h")
    inner = kerns[0].shape[1] // (SIDE * SIDE)
    for step, out in zip(s, outs):
        for n, hop in enumerate(HOPS):
            block = (x ^ step) * SIDE + (h ^ hop)
            parts = [grad_weights(block, kerns, finv_ref, ts, rs, p) for p in range(CORES)]
            grad = grad_block(parts, zt, c_ref[block_rows(block, inner, core), :])
            at = slice(n * inner, (n + 1) * inner)
            if len(out) == 1:
                out[0][:, at] = grad
            else:
                cut = out[0].shape[0]
                out[0][:, at] = grad[:cut]
                out[1][:, at] = grad[cut:]


def far_body(own, other, rinv, finv, t0, t1, t2, t3, z, zo, c, low, high, tinv_ref, zt, ts, rs):
    tinv = 1.0 / four((t0, t1, t2, t3))
    tinv_ref[...] = tinv
    refs = ((own, other), rinv, finv, z, zo, c, zt, ts, rs)
    centre_grads((2,), refs, tinv, ((low, high),))


def mid_body(own, other, rinv, finv, tinv, z, zo, c, first, third, zt, ts, rs):
    refs = ((own, other), rinv, finv, z, zo, c, zt, ts, rs)
    centre_grads((1, 3), refs, tinv[...], ((first,), (third,)))


def near_body(own, other, rinv, finv, tinv, z, zo, c, a0, a1, b0, b1, near, e0, e1, zt, ts, rs):
    points = (z[...].astype(F32), zo[...])
    embed_grads((a0, a1, b0, b1), tinv[...], rinv, points, (e0, e1))
    refs = ((own, other), rinv, finv, z, zo, c, zt, ts, rs)
    centre_grads((0,), refs, tinv[...], ((near,),))


def second_body(base, first, third, low, high, to_first, to_third):
    cut = low.shape[0]
    at = slice(base, base + to_first.shape[1])
    to_first[:cut] = first[:cut, at]
    to_first[cut:] = first[cut:, at] + high[:, at]
    to_third[:cut] = third[:cut, at] + low[:, at]
    to_third[cut:] = third[cut:, at]


def split_body(base, near, first, third, *outs):
    inner = outs[0].shape[1]
    for n, out in enumerate(outs):
        at = slice(n * inner, (n + 1) * inner)
        out[...] = near[:, base + n * inner : base + (n + 1) * inner] + first[:, at] + third[:, at]


def final_body(p0, p1, p2, p3, mine, theirs, grad, embed):
    grad[...] = four((p0, p1, p2, p3)).T
    embed[...] = mine[...] + theirs[...]


VMEM = pl.BlockSpec(memory_space=pltpu.VMEM)
ANY = pl.BlockSpec(memory_space=pl.ANY)


def call(body, outs, *args, scratch=(), limit=2, name=None, flops=0, after=()):
    used = len(args)

    def kernel(*refs):
        body(*refs[:used], *refs[used + len(after) :])

    args = (*args, *after)
    shapes = tuple(o if hasattr(o, "dtype") else jax.ShapeDtypeStruct(o, F32) for o in outs)
    moved = sum(a.size * a.dtype.itemsize for a in args)
    out = pl.pallas_call(
        kernel,
        out_shape=shapes,
        in_specs=[VMEM] * used + [ANY] * len(after),
        out_specs=tuple(VMEM for _ in outs),
        scratch_shapes=scratch,
        compiler_params=pltpu.CompilerParams(vmem_limit_bytes=limit * MIB),
        cost_estimate=pl.CostEstimate(flops=flops, bytes_accessed=moved, transcendentals=0),
        name=name,
    )(*args)
    return out if len(out) > 1 else out[0]


def swap(v, axis, s):
    return lax.ppermute(v, axis, [(i, i ^ s) for i in range(lax.axis_size(axis))])


def around(pieces, axis):
    return [pieces[0]] + [swap(pieces[s], axis, s) for s in (1, 3, 2)]


def body(embeddings, centres, prior_freq):
    half, width = embeddings.shape
    count = centres.shape[0] // CORES
    inner = count // (SIDE * SIDE)
    prior = prior_freq.reshape(1, centres.shape[0])
    rows = (CORES, half)

    def over_ctr(v):
        parts = lax.axis_size("zl") * lax.axis_size("y")
        v = call(swap_add_body, [(parts, *rows)], v, swap(v, "core", 1), name="sum_core")
        return lax.all_to_all(v, ("zl", "y"), 0, 0)

    z_own = embeddings.astype(F32)
    z_other = swap(z_own, "core", 1)
    kern_scratch = [pltpu.VMEM((half, width), BF16), pltpu.VMEM((half, LANES), F32)]
    kern_own, row, ct, norms = call(
        own_body,
        [(half, count), (1, half), jax.ShapeDtypeStruct((width, count), BF16), (1, count)],
        z_own,
        centres,
        scratch=kern_scratch,
        limit=16,
        name="kern_own",
    )
    kern_other, row = call(
        other_body,
        [(half, count), rows],
        z_other,
        ct,
        norms,
        row,
        scratch=kern_scratch,
        limit=16,
        name="kern_other",
    )
    freq, rinv = call(
        freq_body,
        [(1, count), rows],
        kern_own,
        kern_other,
        over_ctr(row),
        scratch=[pltpu.VMEM((CORES, half, LANES), F32)],
        limit=20,
        name="freq",
    )
    kerns = (kern_own, kern_other)
    sums = (half, 2 * LANES)
    work = 4 * half * count * 2 * LANES
    squares = [
        call(square_body, [sums], kern, centres, limit=20, name="squares", flops=work)
        for kern in kerns
    ]
    freq = call(
        add_body, [freq.shape], *around([freq] * SIDE, "x"), name="sum_x", after=squares[:1]
    )
    freq = around([freq] * SIDE, "h")
    target, finv = call(
        target_body,
        [rows, (1, count)],
        *kerns,
        *freq,
        prior,
        scratch=[pltpu.VMEM((half, LANES), F32)],
        limit=20,
        name="target",
        after=squares[1:],
    )
    cubes = [
        call(cube_body, [sums], kern, finv, centres, limit=20, name="cubes", flops=work)
        for kern in kerns
    ]
    target = call(swap_core_body, [rows], target, swap(target, "core", 1), name="target_core")
    target = call(add_body, [rows], target, swap(target, "zl", 1), name="target_zl")
    target = around([target] * SIDE, "y")

    setup = [
        pltpu.VMEM((CORES, width + ONES, half), BF16),
        pltpu.VMEM((CORES, half, LANES), F32),
        pltpu.VMEM((CORES, half, LANES), F32),
    ]
    piece, part, pair = (width, SIDE * inner), (width // 2, SIDE * inner), (width, 2 * inner)
    base = (*kerns, rinv, finv)
    data = (embeddings, z_other, centres)
    low, high, tinv = call(
        far_body, [part, part, rows], *base, *target, *data, scratch=setup, limit=24, name="grad_far"
    )
    low, high = swap(low, "x", 1), swap(high, "x", 3)
    first, third = call(
        mid_body, [piece, piece], *base, tinv, *data, scratch=setup, limit=24, name="grad_mid"
    )
    near, mine, other = call(
        near_body,
        [piece, (half, width), (half, width)],
        *base,
        tinv,
        *data,
        *cubes,
        *squares,
        scratch=setup,
        limit=24,
        name="grad_near",
    )

    def second(start, name, after=()):
        to_first, to_third = call(
            functools.partial(second_body, start),
            [pair] * 2,
            first,
            third,
            low,
            high,
            name=name,
            flops=HINT,
            after=after,
        )
        return swap(to_first, "x", 1), swap(to_third, "x", 3)

    first_a, third_a = second(0, "second_a")
    first_b, third_b = second(2 * inner, "second_b", after=[near])

    embed = call(add_body, [mine.shape], mine, swap(other, "core", 1), name="embed_core", after=[low, high])
    embed = call(add_body, [mine.shape], embed, swap(embed, "zl", 1), name="embed_zl")
    embed = call(add_body, [mine.shape], embed, swap(embed, "y", 1), name="embed_y")
    embed = (embed, swap(embed, "y", 3))

    block = (width, inner)
    def split(start, pieces, name, after=()):
        return call(
            functools.partial(split_body, start),
            [block] * 2,
            near,
            *pieces,
            name=name,
            flops=HINT,
            after=after,
        )

    far2, far1 = split(0, (first_a, third_a), "split_a")
    h2, h1 = swap(far2, "h", 2), swap(far1, "h", 1)
    h3, h0 = split(2 * inner, (first_b, third_b), "split_b", after=[far2])
    grad, embed = call(
        final_body,
        [(inner, width), (half, width)],
        h0,
        h1,
        h2,
        swap(h3, "h", 3),
        *embed,
        name="final",
        flops=HINT,
    )
    return embed, grad.reshape(1, inner, width)


def solution(mesh):
    names = ("x", "h", "core", "zl", "y")
    grid = jax.sharding.Mesh(mesh.devices.reshape(SIDE, SIDE, CORES, CORES, SIDE), names)
    pts, ctr = names[:3], names[3:]
    in_specs = (P(pts, None), P(ctr, None), P(ctr))
    out_specs = (P(pts, None), P(ctr, pts, None))
    return jax.shard_map(body, mesh=grid, in_specs=in_specs, out_specs=out_specs, check_vma=False)
```

```python
import functools

import jax
import jax.numpy as jnp
from jax import lax
from jax.experimental import pallas as pl
from jax.experimental.pallas import tpu as pltpu
from jax.sharding import PartitionSpec as P

SIDE = 4
CORES = 2
LANES = 128
ONES = 16
SCALE = 128.0
MIB = 2**20
HINT = 10**10
HOPS = (2, 1, 3, 0)
F32 = jnp.float32
BF16 = jnp.bfloat16


def tile_lanes(column, width):
    return jnp.concatenate([column] * (width // LANES), axis=1)


def spread(row):
    return jnp.broadcast_to(row, (LANES, row.shape[1])).T


def four(refs):
    a, b, c, d = refs
    return (a[...] + b[...]) + (c[...] + d[...])


def block_rows(block, inner, core):
    return pl.ds(pl.multiple_of((block * CORES + core) * inner, inner), inner)


def kern_block(za, zn, ct, norms):
    cross = jnp.dot(za[...], ct, preferred_element_type=F32)
    return 1.0 / (cross + norms + tile_lanes(zn[...], ct.shape[1]))


def kern_setup(part, za, zn):
    zn[...] = jnp.broadcast_to(jnp.sum(part * part, axis=1, keepdims=True) + 1.0, zn.shape)
    za[...] = (-2.0 * part).astype(BF16)


def lane_sums(total, kern):
    for g in range(kern.shape[1] // LANES):
        total = total + kern[:, g * LANES : (g + 1) * LANES]
    return total


def own_body(z_ref, c_ref, kern_ref, row_ref, ct_ref, norm_ref, za, zn):
    half, count = kern_ref.shape
    inner = count // (SIDE * SIDE)
    core = lax.axis_index("core")
    kern_setup(z_ref[...], za, zn)
    total = jnp.zeros((half, LANES), F32)
    for b in range(count // inner):
        at = slice(b * inner, (b + 1) * inner)
        ct = c_ref[block_rows(b, inner, core), :].T
        norms = jnp.sum(jnp.square(ct.astype(F32)), axis=0, keepdims=True)
        ct_ref[:, at] = ct
        norm_ref[:, at] = norms
        kern = kern_block(za, zn, ct, norms)
        kern_ref[:, at] = kern
        total = lane_sums(total, kern)
    row_ref[...] = jnp.sum(total.T, axis=0, keepdims=True)


def other_body(zo_ref, ct_ref, norm_ref, row_ref, kern_ref, rows_ref, za, zn):
    half, count = kern_ref.shape
    step = 256
    rows_ref[:1] = row_ref[...]
    kern_setup(zo_ref[...], za, zn)
    total = jnp.zeros((half, LANES), F32)
    for b in range(count // step):
        at = slice(b * step, (b + 1) * step)
        kern = kern_block(za, zn, ct_ref[:, at], norm_ref[:, at])
        kern_ref[:, at] = kern
        total = lane_sums(total, kern)
    rows_ref[1:] = jnp.sum(total.T, axis=0, keepdims=True)


def swap_core_body(mine, theirs, out):
    out[:1] = mine[:1] + theirs[1:]
    out[1:] = mine[1:] + theirs[:1]


def swap_add_body(mine, theirs, out):
    for n in range(out.shape[0]):
        out[n, :1] = mine[:1] + theirs[1:]
        out[n, 1:] = mine[1:] + theirs[:1]


def summed(ref):
    total = ref[0]
    for n in range(1, ref.shape[0]):
        total = total + ref[n]
    return total


def add_body(*refs):
    refs[-1][...] = four(refs[:-1]) if len(refs) == 5 else refs[0][...] + refs[1][...]


def freq_body(own_ref, other_ref, rows_ref, f_ref, rinv_ref, scale_ref):
    half, count = own_ref.shape
    rinv = 1.0 / summed(rows_ref)
    rinv_ref[...] = rinv
    step, rows = 2048, 64
    scales = [spread(rinv[p : p + 1]) for p in range(CORES)]
    for p in range(CORES):
        scale_ref[p] = scales[p]
    for base in range(0, count, step):
        at = slice(base, base + step)
        total = jnp.zeros((8, step), F32)
        for p, kern_ref in enumerate((own_ref, other_ref)):

            def add_rows(n, total, p=p, kern_ref=kern_ref, at=at):
                for i in range(0, rows, 8):
                    tile = pl.ds(pl.multiple_of(n * rows + i, 8), 8)
                    total = total + kern_ref[tile, at] * tile_lanes(scale_ref[p, tile, :], step)
                return total

            total = lax.fori_loop(0, half // rows, add_rows, total)
        f_ref[:, at] = jnp.sum(total, axis=0, keepdims=True)


def target_body(own_ref, other_ref, f0, f1, f2, f3, prior_ref, t_ref, finv_ref, acc):
    half, count = own_ref.shape
    inner = count // (SIDE * SIDE)
    core = lax.axis_index("core")
    prior = [prior_ref[:, block_rows(b, inner, core)] for b in range(count // inner)]
    finv_ref[...] = 1.0 / (four((f0, f1, f2, f3)) + jnp.concatenate(prior, axis=1))
    step = 64
    for row, kern_ref in ((0, own_ref), (1, other_ref)):

        for i in range(0, half, step):
            total = jnp.zeros((step, LANES), F32)
            for g in range(count // LANES):
                at = slice(g * LANES, (g + 1) * LANES)
                kern = kern_ref[i : i + step, at]
                total = total + kern * kern * finv_ref[:, at]
            acc[i : i + step] = total

        t_ref[row : row + 1] = jnp.sum(acc[...].T, axis=0, keepdims=True)


def two_terms(value):
    high = value.astype(BF16)
    return high, (value - high.astype(F32)).astype(BF16)


def weights(kern, finv, tinv, rinv):
    return two_terms(kern * kern * (kern * finv * tinv - rinv))


def grad_weights(block, kerns, finv_ref, ts, rs, p):
    inner = kerns[p].shape[1] // (SIDE * SIDE)
    at = pl.ds(pl.multiple_of(block * inner, inner), inner)
    return weights(
        kerns[p][:, at], finv_ref[:, at], tile_lanes(ts[p], inner), tile_lanes(rs[p][...], inner)
    )


def grad_block(parts, zt, c):
    sums = jnp.zeros((LANES + ONES, c.shape[0]), F32)
    for p, terms in enumerate(parts):
        for term in terms:
            sums += jnp.dot(zt[p][...], term, preferred_element_type=F32)
    return sums[:LANES] + sums[LANES : LANES + 1] * c.astype(F32).T


def embed_sums(kern_ref, c_ref, out, power):
    half, count = kern_ref.shape
    inner = count // (SIDE * SIDE)
    core = lax.axis_index("core")
    step = 2 * SIDE
    out[...] = jnp.zeros_like(out)

    @pl.loop(0, count // (inner * step))
    def _(n):
        total = out[...]
        for i in range(step):
            b = n * step + i
            at = pl.ds(pl.multiple_of(b * inner, inner), inner)
            c = c_ref[block_rows(b, inner, core), :]
            wide = jnp.concatenate([c, jnp.ones((inner, LANES), BF16)], axis=1)
            for term in two_terms(power(kern_ref[:, at], at)):
                total += jnp.dot(term, wide, preferred_element_type=F32)
        out[...] = total


def square_body(p, kern_ref, c_ref, z_ref, rinv_ref, out, zt, rs):
    zt[:LANES] = (-SCALE * z_ref[...].T).astype(BF16)
    zt[LANES:] = jnp.full((ONES, z_ref.shape[0]), SCALE, BF16)
    rs[...] = spread(rinv_ref[p : p + 1])
    embed_sums(kern_ref, c_ref, out, lambda kern, at: kern * kern)


def cube_body(kern_ref, finv_ref, c_ref, out):
    embed_sums(kern_ref, c_ref, out, lambda kern, at: kern * kern * (kern * finv_ref[:, at]))


def embed_grads(sums, ts, rs, points, outs):
    for p, (cubes, squares, out) in enumerate(zip(sums[:CORES], sums[CORES:], outs)):
        tinv, rinv = ts[p], rs[p][...]
        total = tinv * cubes[:, LANES:] - rinv * squares[:, LANES:]
        moved = tinv * cubes[:, :LANES] - rinv * squares[:, :LANES]
        out[...] = SCALE * (total * points[p][...] - moved)


def centre_grads(s, refs, tinv, outs):
    own, other, finv_ref, c_ref, zt0, zt1, rs0, rs1, ts = refs
    kerns, zt, rs = (own, other), (zt0, zt1), (rs0, rs1)
    for p in range(CORES):
        ts[p] = spread(tinv[p : p + 1])
    core, x, h = lax.axis_index("core"), lax.axis_index("x"), lax.axis_index("h")
    inner = own.shape[1] // (SIDE * SIDE)
    for step, out in zip(s, outs):
        for n, hop in enumerate(HOPS):
            block = (x ^ step) * SIDE + (h ^ hop)
            parts = [grad_weights(block, kerns, finv_ref, ts, rs, p) for p in range(CORES)]
            grad = grad_block(parts, zt, c_ref[block_rows(block, inner, core), :])
            at = slice(n * inner, (n + 1) * inner)
            if len(out) == 1:
                out[0][:, at] = grad
            else:
                cut = out[0].shape[0]
                out[0][:, at] = grad[:cut]
                out[1][:, at] = grad[cut:]


def far_body(*refs):
    base, (t0, t1, t2, t3, low, high, tinv_ref, ts) = refs[:8], refs[8:]
    tinv = 1.0 / four((t0, t1, t2, t3))
    tinv_ref[...] = tinv
    centre_grads((2,), (*base, ts), tinv, ((low, high),))


def mid_body(*refs):
    base, (tinv, first, third, ts) = refs[:8], refs[8:]
    centre_grads((1, 3), (*base, ts), tinv[...], ((first,), (third,)))


def embed_body(tinv, rs0, rs1, z, zo, a0, a1, b0, b1, e0, e1):
    ts = [spread(tinv[p : p + 1]) for p in range(CORES)]
    embed_grads((a0, a1, b0, b1), ts, (rs0, rs1), (z, zo), (e0, e1))


def second_body(base, first, third, low, high, to_first, to_third):
    cut = low.shape[0]
    at = slice(base, base + to_first.shape[1])
    to_first[:cut] = first[:cut, at]
    to_first[cut:] = first[cut:, at] + high[:, at]
    to_third[:cut] = third[:cut, at] + low[:, at]
    to_third[cut:] = third[cut:, at]


def second_near_body(start, *refs):
    base, (tinv, first, third, low, high, to_first, to_third, near, ts) = refs[:8], refs[8:]
    second_body(start, first, third, low, high, to_first, to_third)
    centre_grads((0,), (*base, ts), tinv[...], ((near,),))


def split_body(base, near, first, third, *outs):
    inner = outs[0].shape[1]
    for n, out in enumerate(outs):
        at = slice(n * inner, (n + 1) * inner)
        out[...] = near[:, base + n * inner : base + (n + 1) * inner] + first[:, at] + third[:, at]


def three_body(p0, p1, p2, out):
    out[...] = p0[...] + (p1[...] + p2[...])


def final_body(most, last, mine, theirs, grad, embed):
    grad[...] = (most[...] + last[...]).T
    embed[...] = mine[...] + theirs[...]


VMEM = pl.BlockSpec(memory_space=pltpu.VMEM)
ANY = pl.BlockSpec(memory_space=pl.ANY)


def call(body, outs, *args, scratch=(), limit=2, name=None, flops=0, after=()):
    used = len(args)

    def kernel(*refs):
        body(*refs[:used], *refs[used + len(after) :])

    args = (*args, *after)
    shapes = tuple(o if hasattr(o, "dtype") else jax.ShapeDtypeStruct(o, F32) for o in outs)
    moved = sum(a.size * a.dtype.itemsize for a in args)
    out = pl.pallas_call(
        kernel,
        out_shape=shapes,
        in_specs=[VMEM] * used + [ANY] * len(after),
        out_specs=tuple(VMEM for _ in outs),
        scratch_shapes=scratch,
        compiler_params=pltpu.CompilerParams(vmem_limit_bytes=limit * MIB),
        cost_estimate=pl.CostEstimate(flops=flops, bytes_accessed=moved, transcendentals=0),
        name=name,
    )(*args)
    return out if len(out) > 1 else out[0]


def swap(v, axis, s):
    return lax.ppermute(v, axis, [(i, i ^ s) for i in range(lax.axis_size(axis))])


def around(pieces, axis):
    return [pieces[0]] + [swap(pieces[s], axis, s) for s in (1, 3, 2)]


def body(embeddings, centres, prior_freq):
    half, width = embeddings.shape
    count = centres.shape[0] // CORES
    inner = count // (SIDE * SIDE)
    prior = prior_freq.reshape(1, centres.shape[0])
    rows = (CORES, half)

    def over_ctr(v):
        parts = lax.axis_size("zl") * lax.axis_size("y")
        v = call(swap_add_body, [(parts, *rows)], v, swap(v, "core", 1), name="sum_core")
        return lax.all_to_all(v, ("zl", "y"), 0, 0)

    z_own = embeddings.astype(F32)
    z_other = swap(z_own, "core", 1)
    kern_scratch = [pltpu.VMEM((half, width), BF16), pltpu.VMEM((half, LANES), F32)]
    kern_own, row, ct, norms = call(
        own_body,
        [(half, count), (1, half), jax.ShapeDtypeStruct((width, count), BF16), (1, count)],
        z_own,
        centres,
        scratch=kern_scratch,
        limit=16,
        name="kern_own",
    )
    kern_other, row = call(
        other_body,
        [(half, count), rows],
        z_other,
        ct,
        norms,
        row,
        scratch=kern_scratch,
        limit=16,
        name="kern_other",
    )
    freq, rinv = call(
        freq_body,
        [(1, count), rows],
        kern_own,
        kern_other,
        over_ctr(row),
        scratch=[pltpu.VMEM((CORES, half, LANES), F32)],
        limit=20,
        name="freq",
    )
    kerns = (kern_own, kern_other)
    sums = (half, 2 * LANES)
    work = 4 * half * count * 2 * LANES
    lanes = ((width + ONES, half), (half, LANES))
    squares = [
        call(
            functools.partial(square_body, p),
            [sums, jax.ShapeDtypeStruct(lanes[0], BF16), lanes[1]],
            kern,
            centres,
            points,
            rinv,
            limit=20,
            name="squares",
            flops=work,
        )
        for p, (kern, points) in enumerate(zip(kerns, (z_own, z_other)))
    ]
    squares, zt, rs = zip(*squares)
    freq = call(
        add_body, [freq.shape], *around([freq] * SIDE, "x"), name="sum_x", after=squares[:1]
    )
    freq = around([freq] * SIDE, "h")
    target, finv = call(
        target_body,
        [rows, (1, count)],
        *kerns,
        *freq,
        prior,
        scratch=[pltpu.VMEM((half, LANES), F32)],
        limit=20,
        name="target",
        after=squares[1:],
    )
    cubes = [
        call(cube_body, [sums], kern, finv, centres, limit=20, name="cubes", flops=work)
        for kern in kerns
    ]
    target = call(swap_core_body, [rows], target, swap(target, "core", 1), name="target_core")
    target = call(add_body, [rows], target, swap(target, "zl", 1), name="target_zl")
    target = around([target] * SIDE, "y")

    setup = [pltpu.VMEM((CORES, half, LANES), F32)]
    piece, part, pair = (width, SIDE * inner), (width // 2, SIDE * inner), (width, 2 * inner)
    base = (*kerns, finv, centres, *zt, *rs)
    low, high, tinv = call(
        far_body, [part, part, rows], *base, *target, scratch=setup, limit=24, name="grad_far"
    )
    low, high = swap(low, "x", 1), swap(high, "x", 3)
    first, third = call(
        mid_body, [piece, piece], *base, tinv, scratch=setup, limit=24, name="grad_mid"
    )
    mine, other = call(
        embed_body,
        [(half, width)] * 2,
        tinv,
        *rs,
        z_own,
        z_other,
        *cubes,
        *squares,
        limit=8,
        name="embed_part",
        flops=HINT // 2,
    )
    moved = (first, third, low, high)
    first_a, third_a = call(
        functools.partial(second_body, 0), [pair] * 2, *moved, name="second_a", flops=HINT
    )
    first_a, third_a = swap(first_a, "x", 1), swap(third_a, "x", 3)
    first_b, third_b, near = call(
        functools.partial(second_near_body, 2 * inner),
        [pair, pair, piece],
        *base,
        tinv,
        *moved,
        scratch=setup,
        limit=24,
        name="second_b",
        flops=HINT,
        after=[mine],
    )
    first_b, third_b = swap(first_b, "x", 1), swap(third_b, "x", 3)

    embed = call(add_body, [mine.shape], mine, swap(other, "core", 1), name="embed_core", after=[low, high])
    embed = call(add_body, [mine.shape], embed, swap(embed, "zl", 1), name="embed_zl")
    embed = call(add_body, [mine.shape], embed, swap(embed, "y", 1), name="embed_y")
    embed = (embed, swap(embed, "y", 3))

    block = (width, inner)
    def split(start, pieces, name, after=()):
        return call(
            functools.partial(split_body, start),
            [block] * 2,
            near,
            *pieces,
            name=name,
            flops=HINT,
            after=after,
        )

    far2, far1 = split(0, (first_a, third_a), "split_a")
    h2, h1 = swap(far2, "h", 2), swap(far1, "h", 1)
    h3, h0 = split(2 * inner, (first_b, third_b), "split_b", after=[far2])
    most = call(three_body, [block], h0, h1, h2, name="most", flops=HINT)
    grad, embed = call(
        final_body,
        [(inner, width), (half, width)],
        most,
        swap(h3, "h", 3),
        *embed,
        name="final",
        flops=HINT,
    )
    return embed, grad.reshape(1, inner, width)


def solution(mesh):
    names = ("x", "h", "core", "zl", "y")
    grid = jax.sharding.Mesh(mesh.devices.reshape(SIDE, SIDE, CORES, CORES, SIDE), names)
    pts, ctr = names[:3], names[3:]
    in_specs = (P(pts, None), P(ctr, None), P(ctr))
    out_specs = (P(pts, None), P(ctr, pts, None))
    return jax.shard_map(body, mesh=grid, in_specs=in_specs, out_specs=out_specs, check_vma=False)
```

```python
import functools

import jax
import jax.numpy as jnp
from jax import lax
from jax.experimental import pallas as pl
from jax.experimental.pallas import tpu as pltpu
from jax.sharding import PartitionSpec as P

SIDE = 4
CORES = 2
LANES = 128
ONES = 16
SCALE = 128.0
MIB = 2**20
HINT = 10**10
HOPS = (2, 1, 3, 0)
F32 = jnp.float32
BF16 = jnp.bfloat16


def tile_lanes(column, width):
    return jnp.concatenate([column] * (width // LANES), axis=1)


def spread(row):
    return jnp.broadcast_to(row, (LANES, row.shape[1])).T


def four(refs):
    a, b, c, d = refs
    return (a[...] + b[...]) + (c[...] + d[...])


def block_rows(block, inner, core):
    return pl.ds(pl.multiple_of((block * CORES + core) * inner, inner), inner)


def widen_body(z_ref, out):
    out[...] = z_ref[...].astype(F32)


def kern_block(za, zn, ct, norms):
    cross = jnp.dot(za[...], ct, preferred_element_type=F32)
    return 1.0 / (cross + norms + tile_lanes(zn[...], ct.shape[1]))


def kern_setup(part, za, zn):
    zn[...] = jnp.broadcast_to(jnp.sum(part * part, axis=1, keepdims=True) + 1.0, zn.shape)
    za[...] = (-2.0 * part).astype(BF16)


def lane_sums(total, kern):
    for g in range(kern.shape[1] // LANES):
        total = total + kern[:, g * LANES : (g + 1) * LANES]
    return total


def own_body(z_ref, c_ref, kern_ref, row_ref, ct_ref, norm_ref, za, zn):
    half, count = kern_ref.shape
    inner = count // (SIDE * SIDE)
    core = lax.axis_index("core")
    kern_setup(z_ref[...], za, zn)
    total = jnp.zeros((half, LANES), F32)
    for b in range(count // inner):
        at = slice(b * inner, (b + 1) * inner)
        ct = c_ref[block_rows(b, inner, core), :].T
        norms = jnp.sum(jnp.square(ct.astype(F32)), axis=0, keepdims=True)
        ct_ref[:, at] = ct
        norm_ref[:, at] = norms
        kern = kern_block(za, zn, ct, norms)
        kern_ref[:, at] = kern
        total = lane_sums(total, kern)
    row_ref[...] = jnp.sum(total.T, axis=0, keepdims=True)


def other_body(zo_ref, ct_ref, norm_ref, row_ref, kern_ref, rows_ref, za, zn):
    half, count = kern_ref.shape
    step = 256
    rows_ref[:1] = row_ref[...]
    kern_setup(zo_ref[...], za, zn)
    total = jnp.zeros((half, LANES), F32)
    for b in range(count // step):
        at = slice(b * step, (b + 1) * step)
        kern = kern_block(za, zn, ct_ref[:, at], norm_ref[:, at])
        kern_ref[:, at] = kern
        total = lane_sums(total, kern)
    rows_ref[1:] = jnp.sum(total.T, axis=0, keepdims=True)


def swap_core_body(mine, theirs, out):
    out[:1] = mine[:1] + theirs[1:]
    out[1:] = mine[1:] + theirs[:1]


def swap_add_body(mine, theirs, out):
    for n in range(out.shape[0]):
        out[n, :1] = mine[:1] + theirs[1:]
        out[n, 1:] = mine[1:] + theirs[:1]


def summed(ref):
    total = ref[0]
    for n in range(1, ref.shape[0]):
        total = total + ref[n]
    return total


def add_body(*refs):
    refs[-1][...] = four(refs[:-1]) if len(refs) == 5 else refs[0][...] + refs[1][...]


def freq_body(own_ref, other_ref, rows_ref, f_ref, rinv_ref, scale_ref):
    half, count = own_ref.shape
    rinv = 1.0 / summed(rows_ref)
    rinv_ref[...] = rinv
    step, rows = 2048, 64
    scales = [spread(rinv[p : p + 1]) for p in range(CORES)]
    for p in range(CORES):
        scale_ref[p] = scales[p]
    for base in range(0, count, step):
        at = slice(base, base + step)
        total = jnp.zeros((8, step), F32)
        for p, kern_ref in enumerate((own_ref, other_ref)):

            def add_rows(n, total, p=p, kern_ref=kern_ref, at=at):
                for i in range(0, rows, 8):
                    tile = pl.ds(pl.multiple_of(n * rows + i, 8), 8)
                    total = total + kern_ref[tile, at] * tile_lanes(scale_ref[p, tile, :], step)
                return total

            total = lax.fori_loop(0, half // rows, add_rows, total)
        f_ref[:, at] = jnp.sum(total, axis=0, keepdims=True)


def target_body(own_ref, other_ref, f0, f1, f2, f3, prior_ref, t_ref, finv_ref, acc):
    half, count = own_ref.shape
    inner = count // (SIDE * SIDE)
    core = lax.axis_index("core")
    prior = [prior_ref[:, block_rows(b, inner, core)] for b in range(count // inner)]
    finv_ref[...] = 1.0 / (four((f0, f1, f2, f3)) + jnp.concatenate(prior, axis=1))
    step = 64
    for row, kern_ref in ((0, own_ref), (1, other_ref)):

        for i in range(0, half, step):
            total = jnp.zeros((step, LANES), F32)
            for g in range(count // LANES):
                at = slice(g * LANES, (g + 1) * LANES)
                kern = kern_ref[i : i + step, at]
                total = total + kern * kern * finv_ref[:, at]
            acc[i : i + step] = total

        t_ref[row : row + 1] = jnp.sum(acc[...].T, axis=0, keepdims=True)


def two_terms(value):
    high = value.astype(BF16)
    return high, (value - high.astype(F32)).astype(BF16)


def weights(kern, finv, tinv, rinv):
    return two_terms(kern * kern * (kern * finv * tinv - rinv))


def grad_weights(block, kerns, finv_ref, ts, rs, p):
    inner = kerns[p].shape[1] // (SIDE * SIDE)
    at = pl.ds(pl.multiple_of(block * inner, inner), inner)
    return weights(
        kerns[p][:, at], finv_ref[:, at], tile_lanes(ts[p], inner), tile_lanes(rs[p][...], inner)
    )


def grad_block(parts, zt, c):
    sums = jnp.zeros((LANES + ONES, c.shape[0]), F32)
    for p, terms in enumerate(parts):
        for term in terms:
            sums += jnp.dot(zt[p][...], term, preferred_element_type=F32)
    return sums[:LANES] + sums[LANES : LANES + 1] * c.astype(F32).T


def embed_sums(kern_ref, c_ref, out, power, step):
    half, count = kern_ref.shape
    inner = count // (SIDE * SIDE)
    core = lax.axis_index("core")
    out[...] = jnp.zeros_like(out)

    @pl.loop(0, count // (inner * step))
    def _(n):
        total = out[...]
        for i in range(step):
            b = n * step + i
            at = pl.ds(pl.multiple_of(b * inner, inner), inner)
            c = c_ref[block_rows(b, inner, core), :]
            wide = jnp.concatenate([c, jnp.ones((inner, LANES), BF16)], axis=1)
            for term in two_terms(power(kern_ref[:, at], at)):
                total += jnp.dot(term, wide, preferred_element_type=F32)
        out[...] = total


def square_body(kern_ref, c_ref, out):
    embed_sums(kern_ref, c_ref, out, lambda kern, at: kern * kern, 2 * SIDE)


def square_setup_body(kern_ref, c_ref, rinv_ref, z, zo, out, zt0, zt1, rs0, rs1):
    for p, (points, zt, rs) in enumerate(((z, zt0, rs0), (zo, zt1, rs1))):
        zt[:LANES] = (-SCALE * points[...].T).astype(BF16)
        zt[LANES:] = jnp.full((ONES, points.shape[0]), SCALE, BF16)
        rs[...] = spread(rinv_ref[p : p + 1])
    square_body(kern_ref, c_ref, out)


def cube_body(kern_ref, finv_ref, c_ref, out):
    embed_sums(
        kern_ref,
        c_ref,
        out,
        lambda kern, at: kern * kern * (kern * finv_ref[:, at]),
        SIDE * SIDE,
    )


def embed_grads(sums, ts, rs, points, outs):
    for p, (cubes, squares, out) in enumerate(zip(sums[:CORES], sums[CORES:], outs)):
        tinv, rinv = ts[p], rs[p][...]
        total = tinv * cubes[:, LANES:] - rinv * squares[:, LANES:]
        moved = tinv * cubes[:, :LANES] - rinv * squares[:, :LANES]
        out[...] = SCALE * (total * points[p][...] - moved)


def centre_grads(s, refs, tinv, outs):
    own, other, finv_ref, c_ref, zt0, zt1, rs0, rs1, ts = refs
    kerns, zt, rs = (own, other), (zt0, zt1), (rs0, rs1)
    for p in range(CORES):
        ts[p] = spread(tinv[p : p + 1])
    core, x, h = lax.axis_index("core"), lax.axis_index("x"), lax.axis_index("h")
    inner = own.shape[1] // (SIDE * SIDE)
    for step, out in zip(s, outs):
        for n, hop in enumerate(HOPS):
            block = (x ^ step) * SIDE + (h ^ hop)
            parts = [grad_weights(block, kerns, finv_ref, ts, rs, p) for p in range(CORES)]
            grad = grad_block(parts, zt, c_ref[block_rows(block, inner, core), :])
            at = slice(n * inner, (n + 1) * inner)
            if len(out) == 1:
                out[0][:, at] = grad
            else:
                cut = out[0].shape[0]
                out[0][:, at] = grad[:cut]
                out[1][:, at] = grad[cut:]


def far_body(*refs):
    base, (t0, t1, t2, t3, low, high, tinv_ref, ts) = refs[:8], refs[8:]
    tinv = 1.0 / four((t0, t1, t2, t3))
    tinv_ref[...] = tinv
    centre_grads((2,), (*base, ts), tinv, ((low, high),))


def mid_body(*refs):
    base, (tinv, first, third, ts) = refs[:8], refs[8:]
    centre_grads((1, 3), (*base, ts), tinv[...], ((first,), (third,)))


def embed_body(tinv, rs0, rs1, z, zo, a0, a1, b0, b1, e0, e1):
    ts = [spread(tinv[p : p + 1]) for p in range(CORES)]
    embed_grads((a0, a1, b0, b1), ts, (rs0, rs1), (z, zo), (e0, e1))


def second_body(base, first, third, low, high, to_first, to_third):
    cut = low.shape[0]
    at = slice(base, base + to_first.shape[1])
    to_first[:cut] = first[:cut, at]
    to_first[cut:] = first[cut:, at] + high[:, at]
    to_third[:cut] = third[:cut, at] + low[:, at]
    to_third[cut:] = third[cut:, at]


def second_near_body(start, *refs):
    base, (tinv, first, third, low, high, to_first, to_third, near, ts) = refs[:8], refs[8:]
    second_body(start, first, third, low, high, to_first, to_third)
    centre_grads((0,), (*base, ts), tinv[...], ((near,),))


def split_body(base, near, first, third, *outs):
    inner = outs[0].shape[1]
    for n, out in enumerate(outs):
        at = slice(n * inner, (n + 1) * inner)
        out[...] = near[:, base + n * inner : base + (n + 1) * inner] + first[:, at] + third[:, at]


def three_body(p0, p1, p2, out):
    out[...] = p0[...] + (p1[...] + p2[...])


def final_body(most, last, mine, theirs, grad, embed):
    grad[...] = (most[...] + last[...]).T
    embed[...] = mine[...] + theirs[...]


VMEM = pl.BlockSpec(memory_space=pltpu.VMEM)
ANY = pl.BlockSpec(memory_space=pl.ANY)


def call(body, outs, *args, scratch=(), limit=2, name=None, flops=0, after=()):
    used = len(args)

    def kernel(*refs):
        body(*refs[:used], *refs[used + len(after) :])

    args = (*args, *after)
    shapes = tuple(o if hasattr(o, "dtype") else jax.ShapeDtypeStruct(o, F32) for o in outs)
    moved = sum(a.size * a.dtype.itemsize for a in args)
    out = pl.pallas_call(
        kernel,
        out_shape=shapes,
        in_specs=[VMEM] * used + [ANY] * len(after),
        out_specs=tuple(VMEM for _ in outs),
        scratch_shapes=scratch,
        compiler_params=pltpu.CompilerParams(vmem_limit_bytes=limit * MIB),
        cost_estimate=pl.CostEstimate(flops=flops, bytes_accessed=moved, transcendentals=0),
        name=name,
    )(*args)
    return out if len(out) > 1 else out[0]


def swap(v, axis, s):
    return lax.ppermute(v, axis, [(i, i ^ s) for i in range(lax.axis_size(axis))])


def around(pieces, axis):
    return [pieces[0]] + [swap(pieces[s], axis, s) for s in (1, 3, 2)]


def body(embeddings, centres, prior_freq):
    half, width = embeddings.shape
    count = centres.shape[0] // CORES
    inner = count // (SIDE * SIDE)
    prior = prior_freq.reshape(1, centres.shape[0])
    rows = (CORES, half)

    def over_ctr(v):
        parts = lax.axis_size("zl") * lax.axis_size("y")
        v = call(swap_add_body, [(parts, *rows)], v, swap(v, "core", 1), name="sum_core")
        return lax.all_to_all(v, ("zl", "y"), 0, 0)

    z_own = call(widen_body, [(half, width)], embeddings, name="widen", flops=HINT)
    z_other = swap(z_own, "core", 1)
    kern_scratch = [pltpu.VMEM((half, width), BF16), pltpu.VMEM((half, LANES), F32)]
    kern_own, row, ct, norms = call(
        own_body,
        [(half, count), (1, half), jax.ShapeDtypeStruct((width, count), BF16), (1, count)],
        z_own,
        centres,
        scratch=kern_scratch,
        limit=16,
        name="kern_own",
    )
    kern_other, row = call(
        other_body,
        [(half, count), rows],
        z_other,
        ct,
        norms,
        row,
        scratch=kern_scratch,
        limit=16,
        name="kern_other",
    )
    freq, rinv = call(
        freq_body,
        [(1, count), rows],
        kern_own,
        kern_other,
        over_ctr(row),
        scratch=[pltpu.VMEM((CORES, half, LANES), F32)],
        limit=20,
        name="freq",
    )
    kerns = (kern_own, kern_other)
    sums = (half, 2 * LANES)
    work = 4 * half * count * 2 * LANES
    zt_shape = jax.ShapeDtypeStruct((width + ONES, half), BF16)
    squares = call(
        square_body, [sums], kern_own, centres, limit=20, name="squares_own", flops=work
    )
    more, *data = call(
        square_setup_body,
        [sums, zt_shape, zt_shape, (half, LANES), (half, LANES)],
        kern_other,
        centres,
        rinv,
        z_own,
        z_other,
        limit=20,
        name="squares_other",
        flops=work,
    )
    squares = (squares, more)
    rs = data[CORES:]
    freq = call(
        add_body, [freq.shape], *around([freq] * SIDE, "x"), name="sum_x", after=squares[:1]
    )
    freq = around([freq] * SIDE, "h")
    target, finv = call(
        target_body,
        [rows, (1, count)],
        *kerns,
        *freq,
        prior,
        scratch=[pltpu.VMEM((half, LANES), F32)],
        limit=20,
        name="target",
        after=squares[1:],
    )
    cubes = [
        call(cube_body, [sums], kern, finv, centres, limit=20, name="cubes", flops=work)
        for kern in kerns
    ]
    target = call(swap_core_body, [rows], target, swap(target, "core", 1), name="target_core")
    target = call(add_body, [rows], target, swap(target, "zl", 1), name="target_zl")
    target = around([target] * SIDE, "y")

    setup = [pltpu.VMEM((CORES, half, LANES), F32)]
    piece, part, pair = (width, SIDE * inner), (width // 2, SIDE * inner), (width, 2 * inner)
    base = (*kerns, finv, centres, *data)
    low, high, tinv = call(
        far_body, [part, part, rows], *base, *target, scratch=setup, limit=24, name="grad_far"
    )
    low, high = swap(low, "x", 1), swap(high, "x", 3)
    first, third = call(
        mid_body, [piece, piece], *base, tinv, scratch=setup, limit=24, name="grad_mid"
    )
    mine, other = call(
        embed_body,
        [(half, width)] * 2,
        tinv,
        *rs,
        z_own,
        z_other,
        *cubes,
        *squares,
        limit=8,
        name="embed_part",
        flops=HINT // 2,
    )
    moved = (first, third, low, high)
    first_a, third_a = call(
        functools.partial(second_body, 0), [pair] * 2, *moved, name="second_a", flops=HINT
    )
    first_a, third_a = swap(first_a, "x", 1), swap(third_a, "x", 3)
    first_b, third_b, near = call(
        functools.partial(second_near_body, 2 * inner),
        [pair, pair, piece],
        *base,
        tinv,
        *moved,
        scratch=setup,
        limit=24,
        name="second_b",
        flops=HINT,
        after=[mine],
    )
    first_b, third_b = swap(first_b, "x", 1), swap(third_b, "x", 3)

    embed = call(add_body, [mine.shape], mine, swap(other, "core", 1), name="embed_core", after=[low, high])
    embed = call(add_body, [mine.shape], embed, swap(embed, "zl", 1), name="embed_zl")
    embed = call(add_body, [mine.shape], embed, swap(embed, "y", 1), name="embed_y")
    embed = (embed, swap(embed, "y", 3))

    block = (width, inner)
    def split(start, pieces, name, after=()):
        return call(
            functools.partial(split_body, start),
            [block] * 2,
            near,
            *pieces,
            name=name,
            flops=HINT,
            after=after,
        )

    far2, far1 = split(0, (first_a, third_a), "split_a")
    h2, h1 = swap(far2, "h", 2), swap(far1, "h", 1)
    h3, h0 = split(2 * inner, (first_b, third_b), "split_b", after=[far2])
    most = call(three_body, [block], h0, h1, h2, name="most", flops=HINT)
    grad, embed = call(
        final_body,
        [(inner, width), (half, width)],
        most,
        swap(h3, "h", 3),
        *embed,
        name="final",
        flops=HINT,
    )
    return embed, grad.reshape(1, inner, width)


def solution(mesh):
    names = ("x", "h", "core", "zl", "y")
    grid = jax.sharding.Mesh(mesh.devices.reshape(SIDE, SIDE, CORES, CORES, SIDE), names)
    pts, ctr = names[:3], names[3:]
    in_specs = (P(pts, None), P(ctr, None), P(ctr))
    out_specs = (P(pts, None), P(ctr, pts, None))
    return jax.shard_map(body, mesh=grid, in_specs=in_specs, out_specs=out_specs, check_vma=False)
```

```python
import functools

import jax
import jax.numpy as jnp
from jax import lax
from jax.experimental import pallas as pl
from jax.experimental.pallas import tpu as pltpu
from jax.sharding import PartitionSpec as P

SIDE = 4
CORES = 2
LANES = 128
ONES = 16
SCALE = 128.0
MIB = 2**20
HINT = 10**10
HOPS = (2, 1, 3, 0)
F32 = jnp.float32
BF16 = jnp.bfloat16


def tile_lanes(column, width):
    return jnp.concatenate([column] * (width // LANES), axis=1)


def spread(row):
    return jnp.broadcast_to(row, (LANES, row.shape[1])).T


def four(refs):
    a, b, c, d = refs
    return (a[...] + b[...]) + (c[...] + d[...])


def block_rows(block, inner, core):
    return pl.ds(pl.multiple_of((block * CORES + core) * inner, inner), inner)


def widen_body(z_ref, out):
    out[...] = z_ref[...].astype(F32)


def three_terms(value):
    first = value.astype(BF16).astype(F32)
    second = (value - first).astype(BF16).astype(F32)
    return first, second, value - first - second


def kern_block(za, ct):
    depth = za.shape[1] - ct.shape[0]
    ct = jnp.concatenate([ct, jnp.zeros((depth, ct.shape[1]), BF16)], axis=0)
    return 1.0 / jnp.dot(za[...], ct, preferred_element_type=F32)


def kern_setup(part, za):
    n0, n1, n2 = three_terms(
        jnp.broadcast_to(jnp.sum(part * part, axis=1, keepdims=True) + 1.0, part.shape)
    )
    lane = lax.broadcasted_iota(jnp.int32, part.shape, 1)
    norms = jnp.where(lane == 0, n0, jnp.where(lane == 1, n1, n2))
    ones = jnp.where(lane < 6, 1.0, 0.0)
    za[:, :LANES] = (-2.0 * part).astype(BF16)
    za[:, LANES:] = jnp.where(lane < 3, norms, ones).astype(BF16)


def lane_sums(total, kern):
    for g in range(kern.shape[1] // LANES):
        total = total + kern[:, g * LANES : (g + 1) * LANES]
    return total


def own_body(z_ref, c_ref, kern_ref, row_ref, ct_ref, za):
    half, count = kern_ref.shape
    inner = count // (SIDE * SIDE)
    core = lax.axis_index("core")
    kern_setup(z_ref[...], za)
    total = jnp.zeros((half, LANES), F32)
    row = lax.broadcasted_iota(jnp.int32, (ONES, inner), 0)
    for b in range(count // inner):
        at = slice(b * inner, (b + 1) * inner)
        ct = c_ref[block_rows(b, inner, core), :].T
        norms = jnp.sum(jnp.square(ct.astype(F32)), axis=0, keepdims=True)
        n0, n1, n2 = (jnp.broadcast_to(n, row.shape) for n in three_terms(norms))
        norms = jnp.where(row == 3, n0, jnp.where(row == 4, n1, jnp.where(row == 5, n2, 0.0)))
        ct = jnp.concatenate([ct, jnp.where(row < 3, 1.0, norms).astype(BF16)], axis=0)
        ct_ref[:, at] = ct
        kern = kern_block(za, ct)
        kern_ref[:, at] = kern
        total = lane_sums(total, kern)
    row_ref[...] = jnp.sum(total.T, axis=0, keepdims=True)


def other_body(zo_ref, ct_ref, row_ref, kern_ref, rows_ref, za):
    half, count = kern_ref.shape
    step = 256
    rows_ref[:1] = row_ref[...]
    kern_setup(zo_ref[...], za)
    total = jnp.zeros((half, LANES), F32)
    for b in range(count // step):
        at = slice(b * step, (b + 1) * step)
        kern = kern_block(za, ct_ref[:, at])
        kern_ref[:, at] = kern
        total = lane_sums(total, kern)
    rows_ref[1:] = jnp.sum(total.T, axis=0, keepdims=True)


def swap_core_body(mine, theirs, out):
    out[:1] = mine[:1] + theirs[1:]
    out[1:] = mine[1:] + theirs[:1]


def swap_add_body(mine, theirs, out):
    for n in range(out.shape[0]):
        out[n, :1] = mine[:1] + theirs[1:]
        out[n, 1:] = mine[1:] + theirs[:1]


def summed(ref):
    total = ref[0]
    for n in range(1, ref.shape[0]):
        total = total + ref[n]
    return total


def add_body(*refs):
    refs[-1][...] = four(refs[:-1]) if len(refs) == 5 else refs[0][...] + refs[1][...]


def freq_body(own_ref, other_ref, rows_ref, f_ref, rinv_ref, scale_ref):
    half, count = own_ref.shape
    rinv = 1.0 / summed(rows_ref)
    rinv_ref[...] = rinv
    step, rows = 2048, 64
    scales = [spread(rinv[p : p + 1]) for p in range(CORES)]
    for p in range(CORES):
        scale_ref[p] = scales[p]
    for base in range(0, count, step):
        at = slice(base, base + step)
        total = jnp.zeros((8, step), F32)
        for p, kern_ref in enumerate((own_ref, other_ref)):

            def add_rows(n, total, p=p, kern_ref=kern_ref, at=at):
                for i in range(0, rows, 8):
                    tile = pl.ds(pl.multiple_of(n * rows + i, 8), 8)
                    total = total + kern_ref[tile, at] * tile_lanes(scale_ref[p, tile, :], step)
                return total

            total = lax.fori_loop(0, half // rows, add_rows, total)
        f_ref[:, at] = jnp.sum(total, axis=0, keepdims=True)


def target_body(own_ref, other_ref, f0, f1, f2, f3, prior_ref, t_ref, finv_ref, acc):
    half, count = own_ref.shape
    inner = count // (SIDE * SIDE)
    core = lax.axis_index("core")
    prior = [prior_ref[:, block_rows(b, inner, core)] for b in range(count // inner)]
    finv_ref[...] = 1.0 / (four((f0, f1, f2, f3)) + jnp.concatenate(prior, axis=1))
    step = 64
    for row, kern_ref in ((0, own_ref), (1, other_ref)):

        for i in range(0, half, step):
            total = jnp.zeros((step, LANES), F32)
            for g in range(count // LANES):
                at = slice(g * LANES, (g + 1) * LANES)
                kern = kern_ref[i : i + step, at]
                total = total + kern * kern * finv_ref[:, at]
            acc[i : i + step] = total

        t_ref[row : row + 1] = jnp.sum(acc[...].T, axis=0, keepdims=True)


def two_terms(value):
    high = value.astype(BF16)
    return high, (value - high.astype(F32)).astype(BF16)


def weights(kern, finv, tinv, rinv):
    return two_terms(kern * kern * (kern * finv * tinv - rinv))


def grad_weights(block, kerns, finv_ref, ts, rs, p):
    inner = kerns[p].shape[1] // (SIDE * SIDE)
    at = pl.ds(pl.multiple_of(block * inner, inner), inner)
    return weights(
        kerns[p][:, at], finv_ref[:, at], tile_lanes(ts[p], inner), tile_lanes(rs[p][...], inner)
    )


def grad_block(parts, zt, c):
    sums = jnp.zeros((LANES + ONES, c.shape[0]), F32)
    for p, terms in enumerate(parts):
        for term in terms:
            sums += jnp.dot(zt[p][...], term, preferred_element_type=F32)
    return sums[:LANES] + sums[LANES : LANES + 1] * c.astype(F32).T


def embed_sums(kern_ref, c_ref, out, power, step):
    half, count = kern_ref.shape
    inner = count // (SIDE * SIDE)
    core = lax.axis_index("core")
    out[...] = jnp.zeros_like(out)

    @pl.loop(0, count // (inner * step))
    def _(n):
        total = out[...]
        for i in range(step):
            b = n * step + i
            at = pl.ds(pl.multiple_of(b * inner, inner), inner)
            c = c_ref[block_rows(b, inner, core), :]
            wide = jnp.concatenate([c, jnp.ones((inner, LANES), BF16)], axis=1)
            for term in two_terms(power(kern_ref[:, at], at)):
                total += jnp.dot(term, wide, preferred_element_type=F32)
        out[...] = total


def square_body(kern_ref, c_ref, out):
    embed_sums(kern_ref, c_ref, out, lambda kern, at: kern * kern, 2 * SIDE)


def square_setup_body(kern_ref, c_ref, rinv_ref, z, zo, out, zt0, zt1, rs0, rs1):
    for p, (points, zt, rs) in enumerate(((z, zt0, rs0), (zo, zt1, rs1))):
        zt[:LANES] = (-SCALE * points[...].T).astype(BF16)
        zt[LANES:] = jnp.full((ONES, points.shape[0]), SCALE, BF16)
        rs[...] = spread(rinv_ref[p : p + 1])
    square_body(kern_ref, c_ref, out)


def cube_body(kern_ref, finv_ref, c_ref, out):
    embed_sums(
        kern_ref,
        c_ref,
        out,
        lambda kern, at: kern * kern * (kern * finv_ref[:, at]),
        SIDE * SIDE,
    )


def embed_grads(sums, ts, rs, points, outs):
    for p, (cubes, squares, out) in enumerate(zip(sums[:CORES], sums[CORES:], outs)):
        tinv, rinv = ts[p], rs[p][...]
        total = tinv * cubes[:, LANES:] - rinv * squares[:, LANES:]
        moved = tinv * cubes[:, :LANES] - rinv * squares[:, :LANES]
        out[...] = SCALE * (total * points[p][...] - moved)


def centre_grads(s, refs, tinv, outs):
    own, other, finv_ref, c_ref, zt0, zt1, rs0, rs1, ts = refs
    kerns, zt, rs = (own, other), (zt0, zt1), (rs0, rs1)
    for p in range(CORES):
        ts[p] = spread(tinv[p : p + 1])
    core, x, h = lax.axis_index("core"), lax.axis_index("x"), lax.axis_index("h")
    inner = own.shape[1] // (SIDE * SIDE)
    for step, out in zip(s, outs):
        for n, hop in enumerate(HOPS):
            block = (x ^ step) * SIDE + (h ^ hop)
            parts = [grad_weights(block, kerns, finv_ref, ts, rs, p) for p in range(CORES)]
            grad = grad_block(parts, zt, c_ref[block_rows(block, inner, core), :])
            at = slice(n * inner, (n + 1) * inner)
            if len(out) == 1:
                out[0][:, at] = grad
            else:
                cut = out[0].shape[0]
                out[0][:, at] = grad[:cut]
                out[1][:, at] = grad[cut:]


def far_body(*refs):
    base, (t0, t1, t2, t3, low, high, tinv_ref, ts) = refs[:8], refs[8:]
    tinv = 1.0 / four((t0, t1, t2, t3))
    tinv_ref[...] = tinv
    centre_grads((2,), (*base, ts), tinv, ((low, high),))


def mid_body(*refs):
    base, (tinv, first, third, ts) = refs[:8], refs[8:]
    centre_grads((1, 3), (*base, ts), tinv[...], ((first,), (third,)))


def embed_body(tinv, rs0, rs1, z, zo, a0, a1, b0, b1, e0, e1):
    ts = [spread(tinv[p : p + 1]) for p in range(CORES)]
    embed_grads((a0, a1, b0, b1), ts, (rs0, rs1), (z, zo), (e0, e1))


def second_body(base, first, third, low, high, to_first, to_third):
    cut = low.shape[0]
    at = slice(base, base + to_first.shape[1])
    to_first[:cut] = first[:cut, at]
    to_first[cut:] = first[cut:, at] + high[:, at]
    to_third[:cut] = third[:cut, at] + low[:, at]
    to_third[cut:] = third[cut:, at]


def second_near_body(start, *refs):
    base, (tinv, first, third, low, high, to_first, to_third, near, ts) = refs[:8], refs[8:]
    second_body(start, first, third, low, high, to_first, to_third)
    centre_grads((0,), (*base, ts), tinv[...], ((near,),))


def split_body(base, near, first, third, *outs):
    inner = outs[0].shape[1]
    for n, out in enumerate(outs):
        at = slice(n * inner, (n + 1) * inner)
        out[...] = near[:, base + n * inner : base + (n + 1) * inner] + first[:, at] + third[:, at]


def three_body(p0, p1, p2, out):
    out[...] = p0[...] + (p1[...] + p2[...])


def final_body(most, last, mine, theirs, grad, embed):
    grad[...] = (most[...] + last[...]).T
    embed[...] = mine[...] + theirs[...]


VMEM = pl.BlockSpec(memory_space=pltpu.VMEM)
ANY = pl.BlockSpec(memory_space=pl.ANY)


def call(body, outs, *args, scratch=(), limit=2, name=None, flops=0, after=()):
    used = len(args)

    def kernel(*refs):
        body(*refs[:used], *refs[used + len(after) :])

    args = (*args, *after)
    shapes = tuple(o if hasattr(o, "dtype") else jax.ShapeDtypeStruct(o, F32) for o in outs)
    moved = sum(a.size * a.dtype.itemsize for a in args)
    out = pl.pallas_call(
        kernel,
        out_shape=shapes,
        in_specs=[VMEM] * used + [ANY] * len(after),
        out_specs=tuple(VMEM for _ in outs),
        scratch_shapes=scratch,
        compiler_params=pltpu.CompilerParams(vmem_limit_bytes=limit * MIB),
        cost_estimate=pl.CostEstimate(flops=flops, bytes_accessed=moved, transcendentals=0),
        name=name,
    )(*args)
    return out if len(out) > 1 else out[0]


def swap(v, axis, s):
    return lax.ppermute(v, axis, [(i, i ^ s) for i in range(lax.axis_size(axis))])


def around(pieces, axis):
    return [pieces[0]] + [swap(pieces[s], axis, s) for s in (1, 3, 2)]


def body(embeddings, centres, prior_freq):
    half, width = embeddings.shape
    count = centres.shape[0] // CORES
    inner = count // (SIDE * SIDE)
    prior = prior_freq.reshape(1, centres.shape[0])
    rows = (CORES, half)

    def over_ctr(v):
        parts = lax.axis_size("zl") * lax.axis_size("y")
        v = call(swap_add_body, [(parts, *rows)], v, swap(v, "core", 1), name="sum_core")
        return lax.all_to_all(v, ("zl", "y"), 0, 0)

    z_own = call(widen_body, [(half, width)], embeddings, name="widen", flops=HINT)
    z_other = swap(z_own, "core", 1)
    kern_scratch = [pltpu.VMEM((half, 2 * LANES), BF16)]
    kern_own, row, ct = call(
        own_body,
        [(half, count), (1, half), jax.ShapeDtypeStruct((width + ONES, count), BF16)],
        z_own,
        centres,
        scratch=kern_scratch,
        limit=16,
        name="kern_own",
    )
    kern_other, row = call(
        other_body,
        [(half, count), rows],
        z_other,
        ct,
        row,
        scratch=kern_scratch,
        limit=16,
        name="kern_other",
    )
    freq, rinv = call(
        freq_body,
        [(1, count), rows],
        kern_own,
        kern_other,
        over_ctr(row),
        scratch=[pltpu.VMEM((CORES, half, LANES), F32)],
        limit=20,
        name="freq",
    )
    kerns = (kern_own, kern_other)
    sums = (half, 2 * LANES)
    work = 4 * half * count * 2 * LANES
    zt_shape = jax.ShapeDtypeStruct((width + ONES, half), BF16)
    squares = call(
        square_body, [sums], kern_own, centres, limit=20, name="squares_own", flops=work
    )
    more, *data = call(
        square_setup_body,
        [sums, zt_shape, zt_shape, (half, LANES), (half, LANES)],
        kern_other,
        centres,
        rinv,
        z_own,
        z_other,
        limit=20,
        name="squares_other",
        flops=work,
    )
    squares = (squares, more)
    rs = data[CORES:]
    freq = call(
        add_body, [freq.shape], *around([freq] * SIDE, "x"), name="sum_x", after=squares[:1]
    )
    freq = around([freq] * SIDE, "h")
    target, finv = call(
        target_body,
        [rows, (1, count)],
        *kerns,
        *freq,
        prior,
        scratch=[pltpu.VMEM((half, LANES), F32)],
        limit=20,
        name="target",
        after=squares[1:],
    )
    cubes = [
        call(cube_body, [sums], kern, finv, centres, limit=20, name="cubes", flops=work)
        for kern in kerns
    ]
    target = call(swap_core_body, [rows], target, swap(target, "core", 1), name="target_core")
    target = call(add_body, [rows], target, swap(target, "zl", 1), name="target_zl")
    target = around([target] * SIDE, "y")

    setup = [pltpu.VMEM((CORES, half, LANES), F32)]
    piece, part, pair = (width, SIDE * inner), (width // 2, SIDE * inner), (width, 2 * inner)
    base = (*kerns, finv, centres, *data)
    low, high, tinv = call(
        far_body, [part, part, rows], *base, *target, scratch=setup, limit=24, name="grad_far"
    )
    low, high = swap(low, "x", 1), swap(high, "x", 3)
    first, third = call(
        mid_body, [piece, piece], *base, tinv, scratch=setup, limit=24, name="grad_mid"
    )
    mine, other = call(
        embed_body,
        [(half, width)] * 2,
        tinv,
        *rs,
        z_own,
        z_other,
        *cubes,
        *squares,
        limit=8,
        name="embed_part",
        flops=HINT // 2,
    )
    moved = (first, third, low, high)
    first_a, third_a = call(
        functools.partial(second_body, 0), [pair] * 2, *moved, name="second_a", flops=HINT
    )
    first_a, third_a = swap(first_a, "x", 1), swap(third_a, "x", 3)
    first_b, third_b, near = call(
        functools.partial(second_near_body, 2 * inner),
        [pair, pair, piece],
        *base,
        tinv,
        *moved,
        scratch=setup,
        limit=24,
        name="second_b",
        flops=HINT,
        after=[mine],
    )
    first_b, third_b = swap(first_b, "x", 1), swap(third_b, "x", 3)

    embed = call(add_body, [mine.shape], mine, swap(other, "core", 1), name="embed_core", after=[low, high])
    embed = call(add_body, [mine.shape], embed, swap(embed, "zl", 1), name="embed_zl")
    embed = call(add_body, [mine.shape], embed, swap(embed, "y", 1), name="embed_y")
    embed = (embed, swap(embed, "y", 3))

    block = (width, inner)
    def split(start, pieces, name, after=()):
        return call(
            functools.partial(split_body, start),
            [block] * 2,
            near,
            *pieces,
            name=name,
            flops=HINT,
            after=after,
        )

    far2, far1 = split(0, (first_a, third_a), "split_a")
    h2, h1 = swap(far2, "h", 2), swap(far1, "h", 1)
    h3, h0 = split(2 * inner, (first_b, third_b), "split_b", after=[far2])
    most = call(three_body, [block], h0, h1, h2, name="most", flops=HINT)
    grad, embed = call(
        final_body,
        [(inner, width), (half, width)],
        most,
        swap(h3, "h", 3),
        *embed,
        name="final",
        flops=HINT,
    )
    return embed, grad.reshape(1, inner, width)


def solution(mesh):
    names = ("x", "h", "core", "zl", "y")
    grid = jax.sharding.Mesh(mesh.devices.reshape(SIDE, SIDE, CORES, CORES, SIDE), names)
    pts, ctr = names[:3], names[3:]
    in_specs = (P(pts, None), P(ctr, None), P(ctr))
    out_specs = (P(pts, None), P(ctr, pts, None))
    return jax.shard_map(body, mesh=grid, in_specs=in_specs, out_specs=out_specs, check_vma=False)
```

```python
import functools

import jax
import jax.numpy as jnp
from jax import lax
from jax.experimental import pallas as pl
from jax.experimental.pallas import tpu as pltpu
from jax.sharding import PartitionSpec as P

SIDE = 4
CORES = 2
LANES = 128
ONES = 16
SCALE = 128.0
MIB = 2**20
HINT = 10**10
HOPS = (2, 1, 3, 0)
F32 = jnp.float32
BF16 = jnp.bfloat16


def tile_lanes(column, width):
    return jnp.concatenate([column] * (width // LANES), axis=1)


def spread(row):
    return jnp.broadcast_to(row, (LANES, row.shape[1])).T


def four(refs):
    a, b, c, d = refs
    return (a[...] + b[...]) + (c[...] + d[...])


def block_rows(block, inner, core):
    return pl.ds(pl.multiple_of((block * CORES + core) * inner, inner), inner)


def widen_body(z_ref, out):
    out[...] = z_ref[...].astype(F32)


def three_terms(value):
    first = value.astype(BF16).astype(F32)
    second = (value - first).astype(BF16).astype(F32)
    return first, second, value - first - second


def kern_block(za, ct):
    depth = za.shape[1] - ct.shape[0]
    ct = jnp.concatenate([ct, jnp.zeros((depth, ct.shape[1]), BF16)], axis=0)
    return 1.0 / jnp.dot(za[...], ct, preferred_element_type=F32)


def kern_setup(part, za):
    n0, n1, n2 = three_terms(
        jnp.broadcast_to(jnp.sum(part * part, axis=1, keepdims=True) + 1.0, part.shape)
    )
    lane = lax.broadcasted_iota(jnp.int32, part.shape, 1)
    norms = jnp.where(lane == 0, n0, jnp.where(lane == 1, n1, n2))
    ones = jnp.where(lane < 6, 1.0, 0.0)
    za[:, :LANES] = (-2.0 * part).astype(BF16)
    za[:, LANES:] = jnp.where(lane < 3, norms, ones).astype(BF16)


def lane_sums(total, kern):
    for g in range(kern.shape[1] // LANES):
        total = total + kern[:, g * LANES : (g + 1) * LANES]
    return total


def own_body(z_ref, c_ref, kern_ref, row_ref, ct_ref, za):
    half, count = kern_ref.shape
    inner = count // (SIDE * SIDE)
    core = lax.axis_index("core")
    kern_setup(z_ref[...], za)
    total = jnp.zeros((half, LANES), F32)
    row = lax.broadcasted_iota(jnp.int32, (ONES, inner), 0)
    for b in range(count // inner):
        at = slice(b * inner, (b + 1) * inner)
        ct = c_ref[block_rows(b, inner, core), :].T
        norms = jnp.sum(jnp.square(ct.astype(F32)), axis=0, keepdims=True)
        n0, n1, n2 = (jnp.broadcast_to(n, row.shape) for n in three_terms(norms))
        norms = jnp.where(row == 3, n0, jnp.where(row == 4, n1, jnp.where(row == 5, n2, 0.0)))
        ct = jnp.concatenate([ct, jnp.where(row < 3, 1.0, norms).astype(BF16)], axis=0)
        ct_ref[:, at] = ct
        kern = kern_block(za, ct)
        kern_ref[:, at] = kern
        total = lane_sums(total, kern)
    row_ref[...] = jnp.sum(total.T, axis=0, keepdims=True)


def other_body(zo_ref, ct_ref, row_ref, kern_ref, rows_ref, za):
    half, count = kern_ref.shape
    step = 256
    rows_ref[:1] = row_ref[...]
    kern_setup(zo_ref[...], za)
    total = jnp.zeros((half, LANES), F32)
    for b in range(count // step):
        at = slice(b * step, (b + 1) * step)
        kern = kern_block(za, ct_ref[:, at])
        kern_ref[:, at] = kern
        total = lane_sums(total, kern)
    rows_ref[1:] = jnp.sum(total.T, axis=0, keepdims=True)


def swap_core_body(mine, theirs, out):
    out[:1] = mine[:1] + theirs[1:]
    out[1:] = mine[1:] + theirs[:1]


def swap_add_body(mine, theirs, out):
    for n in range(out.shape[0]):
        out[n, :1] = mine[:1] + theirs[1:]
        out[n, 1:] = mine[1:] + theirs[:1]


def summed(ref):
    total = ref[0]
    for n in range(1, ref.shape[0]):
        total = total + ref[n]
    return total


def add_body(*refs):
    refs[-1][...] = four(refs[:-1]) if len(refs) == 5 else refs[0][...] + refs[1][...]


def freq_body(own_ref, other_ref, rows_ref, f_ref, rinv_ref, scale_ref):
    half, count = own_ref.shape
    rinv = 1.0 / summed(rows_ref)
    rinv_ref[...] = rinv
    step, rows = 2048, 64
    scales = [spread(rinv[p : p + 1]) for p in range(CORES)]
    for p in range(CORES):
        scale_ref[p] = scales[p]
    for base in range(0, count, step):
        at = slice(base, base + step)
        total = jnp.zeros((8, step), F32)
        for p, kern_ref in enumerate((own_ref, other_ref)):

            def add_rows(n, total, p=p, kern_ref=kern_ref, at=at):
                for i in range(0, rows, 8):
                    tile = pl.ds(pl.multiple_of(n * rows + i, 8), 8)
                    total = total + kern_ref[tile, at] * tile_lanes(scale_ref[p, tile, :], step)
                return total

            total = lax.fori_loop(0, half // rows, add_rows, total)
        f_ref[:, at] = jnp.sum(total, axis=0, keepdims=True)


def target_body(own_ref, other_ref, f0, f1, f2, f3, prior_ref, t_ref, finv_ref, acc):
    half, count = own_ref.shape
    inner = count // (SIDE * SIDE)
    core = lax.axis_index("core")
    prior = [prior_ref[:, block_rows(b, inner, core)] for b in range(count // inner)]
    finv_ref[...] = 1.0 / (four((f0, f1, f2, f3)) + jnp.concatenate(prior, axis=1))
    step = 64
    for row, kern_ref in ((0, own_ref), (1, other_ref)):

        for i in range(0, half, step):
            total = jnp.zeros((step, LANES), F32)
            for g in range(count // LANES):
                at = slice(g * LANES, (g + 1) * LANES)
                kern = kern_ref[i : i + step, at]
                total = total + kern * kern * finv_ref[:, at]
            acc[i : i + step] = total

        t_ref[row : row + 1] = jnp.sum(acc[...].T, axis=0, keepdims=True)


def two_terms(value):
    high = value.astype(BF16)
    return high, (value - high.astype(F32)).astype(BF16)


def weights(kern, finv, tinv, rinv):
    return two_terms(kern * kern * (kern * finv * tinv - rinv))


def grad_weights(block, kerns, finv_ref, ts, rs, p):
    inner = kerns[p].shape[1] // (SIDE * SIDE)
    at = pl.ds(pl.multiple_of(block * inner, inner), inner)
    return weights(
        kerns[p][:, at], finv_ref[:, at], tile_lanes(ts[p], inner), tile_lanes(rs[p][...], inner)
    )


def grad_block(parts, zt, c):
    sums = jnp.zeros((LANES + ONES, c.shape[0]), F32)
    for p, terms in enumerate(parts):
        for term in terms:
            sums += jnp.dot(zt[p][...], term, preferred_element_type=F32)
    return sums[:LANES] + sums[LANES : LANES + 1] * c.astype(F32).T


def embed_sums(kern_ref, c_ref, out, power, step):
    half, count = kern_ref.shape
    inner = count // (SIDE * SIDE)
    core = lax.axis_index("core")
    out[...] = jnp.zeros_like(out)

    @pl.loop(0, count // (inner * step))
    def _(n):
        total = out[...]
        for i in range(step):
            b = n * step + i
            at = pl.ds(pl.multiple_of(b * inner, inner), inner)
            c = c_ref[block_rows(b, inner, core), :]
            wide = jnp.concatenate([c, jnp.ones((inner, LANES), BF16)], axis=1)
            for term in two_terms(power(kern_ref[:, at], at)):
                total += jnp.dot(term, wide, preferred_element_type=F32)
        out[...] = total


def square_body(step, kern_ref, c_ref, out):
    embed_sums(kern_ref, c_ref, out, lambda kern, at: kern * kern, step)


def square_setup_body(kern_ref, c_ref, rinv_ref, z, zo, out, zt0, zt1, rs0, rs1):
    for p, (points, zt, rs) in enumerate(((z, zt0, rs0), (zo, zt1, rs1))):
        zt[:LANES] = (-SCALE * points[...].T).astype(BF16)
        zt[LANES:] = jnp.full((ONES, points.shape[0]), SCALE, BF16)
        rs[...] = spread(rinv_ref[p : p + 1])
    square_body(2 * SIDE, kern_ref, c_ref, out)


def cube_body(kern_ref, finv_ref, c_ref, out):
    embed_sums(
        kern_ref,
        c_ref,
        out,
        lambda kern, at: kern * kern * (kern * finv_ref[:, at]),
        SIDE * SIDE,
    )


def embed_grads(sums, ts, rs, points, outs):
    for p, (cubes, squares, out) in enumerate(zip(sums[:CORES], sums[CORES:], outs)):
        tinv, rinv = ts[p], rs[p][...]
        total = tinv * cubes[:, LANES:] - rinv * squares[:, LANES:]
        moved = tinv * cubes[:, :LANES] - rinv * squares[:, :LANES]
        out[...] = SCALE * (total * points[p][...] - moved)


def centre_grads(s, refs, tinv, outs):
    own, other, finv_ref, c_ref, zt0, zt1, rs0, rs1, ts = refs
    kerns, zt, rs = (own, other), (zt0, zt1), (rs0, rs1)
    for p in range(CORES):
        ts[p] = spread(tinv[p : p + 1])
    core, x, h = lax.axis_index("core"), lax.axis_index("x"), lax.axis_index("h")
    inner = own.shape[1] // (SIDE * SIDE)
    for step, out in zip(s, outs):
        for n, hop in enumerate(HOPS):
            block = (x ^ step) * SIDE + (h ^ hop)
            parts = [grad_weights(block, kerns, finv_ref, ts, rs, p) for p in range(CORES)]
            grad = grad_block(parts, zt, c_ref[block_rows(block, inner, core), :])
            at = slice(n * inner, (n + 1) * inner)
            if len(out) == 1:
                out[0][:, at] = grad
            else:
                cut = out[0].shape[0]
                out[0][:, at] = grad[:cut]
                out[1][:, at] = grad[cut:]


def far_body(*refs):
    base, (t0, t1, t2, t3, low, high, tinv_ref, ts) = refs[:8], refs[8:]
    tinv = 1.0 / four((t0, t1, t2, t3))
    tinv_ref[...] = tinv
    centre_grads((2,), (*base, ts), tinv, ((low, high),))


def mid_body(*refs):
    base, (tinv, first, third, ts) = refs[:8], refs[8:]
    centre_grads((1, 3), (*base, ts), tinv[...], ((first,), (third,)))


def embed_body(tinv, rs0, rs1, z, zo, a0, a1, b0, b1, e0, e1):
    ts = [spread(tinv[p : p + 1]) for p in range(CORES)]
    embed_grads((a0, a1, b0, b1), ts, (rs0, rs1), (z, zo), (e0, e1))


def second_body(base, first, third, low, high, to_first, to_third):
    cut = low.shape[0]
    at = slice(base, base + to_first.shape[1])
    to_first[:cut] = first[:cut, at]
    to_first[cut:] = first[cut:, at] + high[:, at]
    to_third[:cut] = third[:cut, at] + low[:, at]
    to_third[cut:] = third[cut:, at]


def second_near_body(start, *refs):
    base, (tinv, first, third, low, high, to_first, to_third, near, ts) = refs[:8], refs[8:]
    second_body(start, first, third, low, high, to_first, to_third)
    centre_grads((0,), (*base, ts), tinv[...], ((near,),))


def split_body(base, near, first, third, *outs):
    inner = outs[0].shape[1]
    for n, out in enumerate(outs):
        at = slice(n * inner, (n + 1) * inner)
        out[...] = near[:, base + n * inner : base + (n + 1) * inner] + first[:, at] + third[:, at]


def three_body(p0, p1, p2, out):
    out[...] = p0[...] + (p1[...] + p2[...])


def final_body(most, last, mine, theirs, grad, embed):
    grad[...] = (most[...] + last[...]).T
    embed[...] = mine[...] + theirs[...]


VMEM = pl.BlockSpec(memory_space=pltpu.VMEM)
ANY = pl.BlockSpec(memory_space=pl.ANY)


def call(body, outs, *args, scratch=(), limit=2, name=None, flops=0, after=()):
    used = len(args)

    def kernel(*refs):
        body(*refs[:used], *refs[used + len(after) :])

    args = (*args, *after)
    shapes = tuple(o if hasattr(o, "dtype") else jax.ShapeDtypeStruct(o, F32) for o in outs)
    moved = sum(a.size * a.dtype.itemsize for a in args)
    out = pl.pallas_call(
        kernel,
        out_shape=shapes,
        in_specs=[VMEM] * used + [ANY] * len(after),
        out_specs=tuple(VMEM for _ in outs),
        scratch_shapes=scratch,
        compiler_params=pltpu.CompilerParams(vmem_limit_bytes=limit * MIB),
        cost_estimate=pl.CostEstimate(flops=flops, bytes_accessed=moved, transcendentals=0),
        name=name,
    )(*args)
    return out if len(out) > 1 else out[0]


def swap(v, axis, s):
    return lax.ppermute(v, axis, [(i, i ^ s) for i in range(lax.axis_size(axis))])


def around(pieces, axis):
    return [pieces[0]] + [swap(pieces[s], axis, s) for s in (1, 3, 2)]


def body(embeddings, centres, prior_freq):
    half, width = embeddings.shape
    count = centres.shape[0] // CORES
    inner = count // (SIDE * SIDE)
    prior = prior_freq.reshape(1, centres.shape[0])
    rows = (CORES, half)

    def over_ctr(v):
        parts = lax.axis_size("zl") * lax.axis_size("y")
        v = call(swap_add_body, [(parts, *rows)], v, swap(v, "core", 1), name="sum_core")
        return lax.all_to_all(v, ("zl", "y"), 0, 0)

    z_own = call(widen_body, [(half, width)], embeddings, name="widen", flops=HINT)
    z_other = swap(z_own, "core", 1)
    kern_scratch = [pltpu.VMEM((half, 2 * LANES), BF16)]
    kern_own, row, ct = call(
        own_body,
        [(half, count), (1, half), jax.ShapeDtypeStruct((width + ONES, count), BF16)],
        z_own,
        centres,
        scratch=kern_scratch,
        limit=16,
        name="kern_own",
    )
    kern_other, row = call(
        other_body,
        [(half, count), rows],
        z_other,
        ct,
        row,
        scratch=kern_scratch,
        limit=16,
        name="kern_other",
    )
    freq, rinv = call(
        freq_body,
        [(1, count), rows],
        kern_own,
        kern_other,
        over_ctr(row),
        scratch=[pltpu.VMEM((CORES, half, LANES), F32)],
        limit=20,
        name="freq",
    )
    kerns = (kern_own, kern_other)
    sums = (half, 2 * LANES)
    work = 4 * half * count * 2 * LANES
    zt_shape = jax.ShapeDtypeStruct((width + ONES, half), BF16)
    squares = call(
        functools.partial(square_body, SIDE * SIDE),
        [sums],
        kern_own,
        centres,
        limit=20,
        name="squares_own",
        flops=work,
    )
    more, *data = call(
        square_setup_body,
        [sums, zt_shape, zt_shape, (half, LANES), (half, LANES)],
        kern_other,
        centres,
        rinv,
        z_own,
        z_other,
        limit=20,
        name="squares_other",
        flops=work,
    )
    squares = (squares, more)
    rs = data[CORES:]
    freq = call(
        add_body, [freq.shape], *around([freq] * SIDE, "x"), name="sum_x", after=squares[:1]
    )
    freq = around([freq] * SIDE, "h")
    target, finv = call(
        target_body,
        [rows, (1, count)],
        *kerns,
        *freq,
        prior,
        scratch=[pltpu.VMEM((half, LANES), F32)],
        limit=20,
        name="target",
        after=squares[1:],
    )
    cubes = [
        call(cube_body, [sums], kern, finv, centres, limit=20, name="cubes", flops=work)
        for kern in kerns
    ]
    target = call(swap_core_body, [rows], target, swap(target, "core", 1), name="target_core")
    target = call(add_body, [rows], target, swap(target, "zl", 1), name="target_zl")
    target = around([target] * SIDE, "y")

    setup = [pltpu.VMEM((CORES, half, LANES), F32)]
    piece, part, pair = (width, SIDE * inner), (width // 2, SIDE * inner), (width, 2 * inner)
    base = (*kerns, finv, centres, *data)
    low, high, tinv = call(
        far_body, [part, part, rows], *base, *target, scratch=setup, limit=24, name="grad_far"
    )
    low, high = swap(low, "x", 1), swap(high, "x", 3)
    first, third = call(
        mid_body, [piece, piece], *base, tinv, scratch=setup, limit=24, name="grad_mid"
    )
    mine, other = call(
        embed_body,
        [(half, width)] * 2,
        tinv,
        *rs,
        z_own,
        z_other,
        *cubes,
        *squares,
        limit=8,
        name="embed_part",
        flops=HINT // 2,
    )
    moved = (first, third, low, high)
    first_a, third_a = call(
        functools.partial(second_body, 0), [pair] * 2, *moved, name="second_a", flops=HINT
    )
    first_a, third_a = swap(first_a, "x", 1), swap(third_a, "x", 3)
    first_b, third_b, near = call(
        functools.partial(second_near_body, 2 * inner),
        [pair, pair, piece],
        *base,
        tinv,
        *moved,
        scratch=setup,
        limit=24,
        name="second_b",
        flops=HINT,
        after=[mine],
    )
    first_b, third_b = swap(first_b, "x", 1), swap(third_b, "x", 3)

    embed = call(add_body, [mine.shape], mine, swap(other, "core", 1), name="embed_core", after=[low, high])
    embed = call(add_body, [mine.shape], embed, swap(embed, "zl", 1), name="embed_zl")
    embed = call(add_body, [mine.shape], embed, swap(embed, "y", 1), name="embed_y")
    embed = (embed, swap(embed, "y", 3))

    block = (width, inner)
    def split(start, pieces, name, after=()):
        return call(
            functools.partial(split_body, start),
            [block] * 2,
            near,
            *pieces,
            name=name,
            flops=HINT,
            after=after,
        )

    far2, far1 = split(0, (first_a, third_a), "split_a")
    h2, h1 = swap(far2, "h", HOPS[0]), swap(far1, "h", HOPS[1])
    h3, h0 = split(2 * inner, (first_b, third_b), "split_b", after=[far2])
    most = call(three_body, [block], h0, h1, h2, name="most", flops=HINT)
    grad, embed = call(
        final_body,
        [(inner, width), (half, width)],
        most,
        swap(h3, "h", HOPS[2]),
        *embed,
        name="final",
        flops=HINT,
    )
    return embed, grad.reshape(1, inner, width)


def solution(mesh):
    names = ("x", "h", "core", "zl", "y")
    grid = jax.sharding.Mesh(mesh.devices.reshape(SIDE, SIDE, CORES, CORES, SIDE), names)
    pts, ctr = names[:3], names[3:]
    in_specs = (P(pts, None), P(ctr, None), P(ctr))
    out_specs = (P(pts, None), P(ctr, pts, None))
    return jax.shard_map(body, mesh=grid, in_specs=in_specs, out_specs=out_specs, check_vma=False)
```

```python
import functools

import jax
import jax.numpy as jnp
from jax import lax
from jax.experimental import pallas as pl
from jax.experimental.pallas import tpu as pltpu
from jax.sharding import PartitionSpec as P

SIDE = 4
CORES = 2
LANES = 128
ONES = 16
SCALE = 128.0
MIB = 2**20
HINT = 10**10
HOPS = (2, 1, 3, 0)
F32 = jnp.float32
BF16 = jnp.bfloat16


def tile_lanes(column, width):
    return jnp.concatenate([column] * (width // LANES), axis=1)


def spread(row):
    return jnp.broadcast_to(row, (LANES, row.shape[1])).T


def four(refs):
    a, b, c, d = refs
    return (a[...] + b[...]) + (c[...] + d[...])


def block_rows(block, inner, core):
    return pl.ds(pl.multiple_of((block * CORES + core) * inner, inner), inner)


def widen_body(z_ref, out):
    out[...] = z_ref[...].astype(F32)


def three_terms(value):
    first = value.astype(BF16).astype(F32)
    second = (value - first).astype(BF16).astype(F32)
    return first, second, value - first - second


def kern_block(za, ct):
    depth = za.shape[1] - ct.shape[0]
    ct = jnp.concatenate([ct, jnp.zeros((depth, ct.shape[1]), BF16)], axis=0)
    return 1.0 / jnp.dot(za[...], ct, preferred_element_type=F32)


def kern_setup(part, za):
    n0, n1, n2 = three_terms(
        jnp.broadcast_to(jnp.sum(part * part, axis=1, keepdims=True) + 1.0, part.shape)
    )
    lane = lax.broadcasted_iota(jnp.int32, part.shape, 1)
    norms = jnp.where(lane == 0, n0, jnp.where(lane == 1, n1, n2))
    ones = jnp.where(lane < 6, 1.0, 0.0)
    za[:, :LANES] = (-2.0 * part).astype(BF16)
    za[:, LANES:] = jnp.where(lane < 3, norms, ones).astype(BF16)


def lane_sums(total, kern):
    for g in range(kern.shape[1] // LANES):
        total = total + kern[:, g * LANES : (g + 1) * LANES]
    return total


def own_body(z_ref, c_ref, kern_ref, row_ref, ct_ref, za):
    half, count = kern_ref.shape
    inner = count // (SIDE * SIDE)
    core = lax.axis_index("core")
    kern_setup(z_ref[...], za)
    total = jnp.zeros((half, LANES), F32)
    row = lax.broadcasted_iota(jnp.int32, (ONES, inner), 0)
    for b in range(count // inner):
        at = slice(b * inner, (b + 1) * inner)
        ct = c_ref[block_rows(b, inner, core), :].T
        norms = jnp.sum(jnp.square(ct.astype(F32)), axis=0, keepdims=True)
        n0, n1, n2 = (jnp.broadcast_to(n, row.shape) for n in three_terms(norms))
        norms = jnp.where(row == 3, n0, jnp.where(row == 4, n1, jnp.where(row == 5, n2, 0.0)))
        ct = jnp.concatenate([ct, jnp.where(row < 3, 1.0, norms).astype(BF16)], axis=0)
        ct_ref[:, at] = ct
        kern = kern_block(za, ct)
        kern_ref[:, at] = kern
        total = lane_sums(total, kern)
    row_ref[...] = jnp.sum(total.T, axis=0, keepdims=True)


def other_body(zo_ref, ct_ref, row_ref, kern_ref, rows_ref, za):
    half, count = kern_ref.shape
    step = 256
    rows_ref[:1] = row_ref[...]
    kern_setup(zo_ref[...], za)
    total = jnp.zeros((half, LANES), F32)
    for b in range(count // step):
        at = slice(b * step, (b + 1) * step)
        kern = kern_block(za, ct_ref[:, at])
        kern_ref[:, at] = kern
        total = lane_sums(total, kern)
    rows_ref[1:] = jnp.sum(total.T, axis=0, keepdims=True)


def swap_core_body(mine, theirs, out):
    out[:1] = mine[:1] + theirs[1:]
    out[1:] = mine[1:] + theirs[:1]


def swap_add_body(mine, theirs, out):
    for n in range(out.shape[0]):
        out[n, :1] = mine[:1] + theirs[1:]
        out[n, 1:] = mine[1:] + theirs[:1]


def summed(ref):
    total = ref[0]
    for n in range(1, ref.shape[0]):
        total = total + ref[n]
    return total


def add_body(*refs):
    refs[-1][...] = four(refs[:-1]) if len(refs) == 5 else refs[0][...] + refs[1][...]


def freq_body(own_ref, other_ref, rows_ref, f_ref, rinv_ref, scale_ref):
    half, count = own_ref.shape
    rinv = 1.0 / summed(rows_ref)
    rinv_ref[...] = rinv
    step, rows = 2048, 128
    scales = [spread(rinv[p : p + 1]) for p in range(CORES)]
    for p in range(CORES):
        scale_ref[p] = scales[p]
    for base in range(0, count, step):
        at = slice(base, base + step)
        total = jnp.zeros((8, step), F32)
        for p, kern_ref in enumerate((own_ref, other_ref)):

            def add_rows(n, total, p=p, kern_ref=kern_ref, at=at):
                for i in range(0, rows, 8):
                    tile = pl.ds(pl.multiple_of(n * rows + i, 8), 8)
                    total = total + kern_ref[tile, at] * tile_lanes(scale_ref[p, tile, :], step)
                return total

            total = lax.fori_loop(0, half // rows, add_rows, total)
        f_ref[:, at] = jnp.sum(total, axis=0, keepdims=True)


def target_body(own_ref, other_ref, f0, f1, f2, f3, prior_ref, t_ref, finv_ref, acc):
    half, count = own_ref.shape
    inner = count // (SIDE * SIDE)
    core = lax.axis_index("core")
    prior = [prior_ref[:, block_rows(b, inner, core)] for b in range(count // inner)]
    finv_ref[...] = 1.0 / (four((f0, f1, f2, f3)) + jnp.concatenate(prior, axis=1))
    step = 64
    for row, kern_ref in ((0, own_ref), (1, other_ref)):

        for i in range(0, half, step):
            total = jnp.zeros((step, LANES), F32)
            for g in range(count // LANES):
                at = slice(g * LANES, (g + 1) * LANES)
                kern = kern_ref[i : i + step, at]
                total = total + kern * kern * finv_ref[:, at]
            acc[row, i : i + step] = total

    for row in range(CORES):
        t_ref[row : row + 1] = jnp.sum(acc[row].T, axis=0, keepdims=True)


def two_terms(value):
    high = value.astype(BF16)
    return high, (value - high.astype(F32)).astype(BF16)


def weights(kern, finv, tinv, rinv):
    return two_terms(kern * kern * (kern * finv * tinv - rinv))


def grad_weights(block, kerns, finv_ref, ts, rs, p):
    inner = kerns[p].shape[1] // (SIDE * SIDE)
    at = pl.ds(pl.multiple_of(block * inner, inner), inner)
    return weights(
        kerns[p][:, at], finv_ref[:, at], tile_lanes(ts[p], inner), tile_lanes(rs[p][...], inner)
    )


def grad_block(parts, zt, c):
    sums = jnp.zeros((LANES + ONES, c.shape[0]), F32)
    for p, terms in enumerate(parts):
        for term in terms:
            sums += jnp.dot(zt[p][...], term, preferred_element_type=F32)
    return sums[:LANES] + sums[LANES : LANES + 1] * c.astype(F32).T


def embed_sums(kern_ref, c_ref, out, power, step):
    half, count = kern_ref.shape
    inner = count // (SIDE * SIDE)
    core = lax.axis_index("core")
    out[...] = jnp.zeros_like(out)

    @pl.loop(0, count // (inner * step))
    def _(n):
        total = out[...]
        for i in range(step):
            b = n * step + i
            at = pl.ds(pl.multiple_of(b * inner, inner), inner)
            c = c_ref[block_rows(b, inner, core), :]
            wide = jnp.concatenate([c, jnp.ones((inner, LANES), BF16)], axis=1)
            for term in two_terms(power(kern_ref[:, at], at)):
                total += jnp.dot(term, wide, preferred_element_type=F32)
        out[...] = total


def square_body(step, kern_ref, c_ref, out):
    embed_sums(kern_ref, c_ref, out, lambda kern, at: kern * kern, step)


def square_setup_body(kern_ref, c_ref, rinv_ref, z, zo, out, zt0, zt1, rs0, rs1):
    for p, (points, zt, rs) in enumerate(((z, zt0, rs0), (zo, zt1, rs1))):
        zt[:LANES] = (-SCALE * points[...].T).astype(BF16)
        zt[LANES:] = jnp.full((ONES, points.shape[0]), SCALE, BF16)
        rs[...] = spread(rinv_ref[p : p + 1])
    square_body(2 * SIDE, kern_ref, c_ref, out)


def cube_body(kern_ref, finv_ref, c_ref, out):
    embed_sums(
        kern_ref,
        c_ref,
        out,
        lambda kern, at: kern * kern * (kern * finv_ref[:, at]),
        SIDE * SIDE,
    )


def embed_grads(sums, ts, rs, points, outs):
    for p, (cubes, squares, out) in enumerate(zip(sums[:CORES], sums[CORES:], outs)):
        tinv, rinv = ts[p], rs[p][...]
        total = tinv * cubes[:, LANES:] - rinv * squares[:, LANES:]
        moved = tinv * cubes[:, :LANES] - rinv * squares[:, :LANES]
        out[...] = SCALE * (total * points[p][...] - moved)


def centre_grads(s, refs, tinv, outs):
    own, other, finv_ref, c_ref, zt0, zt1, rs0, rs1, ts = refs
    kerns, zt, rs = (own, other), (zt0, zt1), (rs0, rs1)
    for p in range(CORES):
        ts[p] = spread(tinv[p : p + 1])
    core, x, h = lax.axis_index("core"), lax.axis_index("x"), lax.axis_index("h")
    inner = own.shape[1] // (SIDE * SIDE)
    for step, out in zip(s, outs):
        for n, hop in enumerate(HOPS):
            block = (x ^ step) * SIDE + (h ^ hop)
            parts = [grad_weights(block, kerns, finv_ref, ts, rs, p) for p in range(CORES)]
            grad = grad_block(parts, zt, c_ref[block_rows(block, inner, core), :])
            at = slice(n * inner, (n + 1) * inner)
            if len(out) == 1:
                out[0][:, at] = grad
            else:
                cut = out[0].shape[0]
                out[0][:, at] = grad[:cut]
                out[1][:, at] = grad[cut:]


def far_body(*refs):
    base, (t0, t1, t2, t3, low, high, tinv_ref, ts) = refs[:8], refs[8:]
    tinv = 1.0 / four((t0, t1, t2, t3))
    tinv_ref[...] = tinv
    centre_grads((2,), (*base, ts), tinv, ((low, high),))


def mid_body(*refs):
    base, (tinv, first, third, ts) = refs[:8], refs[8:]
    centre_grads((1, 3), (*base, ts), tinv[...], ((first,), (third,)))


def embed_body(tinv, rs0, rs1, z, zo, a0, a1, b0, b1, e0, e1):
    ts = [spread(tinv[p : p + 1]) for p in range(CORES)]
    embed_grads((a0, a1, b0, b1), ts, (rs0, rs1), (z, zo), (e0, e1))


def second_body(base, first, third, low, high, to_first, to_third):
    cut = low.shape[0]
    at = slice(base, base + to_first.shape[1])
    to_first[:cut] = first[:cut, at]
    to_first[cut:] = first[cut:, at] + high[:, at]
    to_third[:cut] = third[:cut, at] + low[:, at]
    to_third[cut:] = third[cut:, at]


def second_near_body(start, *refs):
    base, (tinv, first, third, low, high, to_first, to_third, near, ts) = refs[:8], refs[8:]
    second_body(start, first, third, low, high, to_first, to_third)
    centre_grads((0,), (*base, ts), tinv[...], ((near,),))


def split_body(base, near, first, third, *outs):
    inner = outs[0].shape[1]
    for n, out in enumerate(outs):
        at = slice(n * inner, (n + 1) * inner)
        out[...] = near[:, base + n * inner : base + (n + 1) * inner] + first[:, at] + third[:, at]


def three_body(p0, p1, p2, out):
    out[...] = p0[...] + (p1[...] + p2[...])


def final_body(most, last, mine, theirs, grad, embed):
    grad[...] = (most[...] + last[...]).T
    embed[...] = mine[...] + theirs[...]


VMEM = pl.BlockSpec(memory_space=pltpu.VMEM)
ANY = pl.BlockSpec(memory_space=pl.ANY)


def call(body, outs, *args, scratch=(), limit=2, name=None, flops=0, after=()):
    used = len(args)

    def kernel(*refs):
        body(*refs[:used], *refs[used + len(after) :])

    args = (*args, *after)
    shapes = tuple(o if hasattr(o, "dtype") else jax.ShapeDtypeStruct(o, F32) for o in outs)
    moved = sum(a.size * a.dtype.itemsize for a in args)
    out = pl.pallas_call(
        kernel,
        out_shape=shapes,
        in_specs=[VMEM] * used + [ANY] * len(after),
        out_specs=tuple(VMEM for _ in outs),
        scratch_shapes=scratch,
        compiler_params=pltpu.CompilerParams(vmem_limit_bytes=limit * MIB),
        cost_estimate=pl.CostEstimate(flops=flops, bytes_accessed=moved, transcendentals=0),
        name=name,
    )(*args)
    return out if len(out) > 1 else out[0]


def swap(v, axis, s):
    return lax.ppermute(v, axis, [(i, i ^ s) for i in range(lax.axis_size(axis))])


def around(pieces, axis):
    return [pieces[0]] + [swap(pieces[s], axis, s) for s in (1, 3, 2)]


def body(embeddings, centres, prior_freq):
    half, width = embeddings.shape
    count = centres.shape[0] // CORES
    inner = count // (SIDE * SIDE)
    prior = prior_freq.reshape(1, centres.shape[0])
    rows = (CORES, half)

    def over_ctr(v):
        parts = lax.axis_size("zl") * lax.axis_size("y")
        v = call(swap_add_body, [(parts, *rows)], v, swap(v, "core", 1), name="sum_core")
        return lax.all_to_all(v, ("zl", "y"), 0, 0)

    z_own = call(widen_body, [(half, width)], embeddings, name="widen", flops=HINT)
    z_other = swap(z_own, "core", 1)
    kern_scratch = [pltpu.VMEM((half, 2 * LANES), BF16)]
    kern_own, row, ct = call(
        own_body,
        [(half, count), (1, half), jax.ShapeDtypeStruct((width + ONES, count), BF16)],
        z_own,
        centres,
        scratch=kern_scratch,
        limit=16,
        name="kern_own",
    )
    kern_other, row = call(
        other_body,
        [(half, count), rows],
        z_other,
        ct,
        row,
        scratch=kern_scratch,
        limit=16,
        name="kern_other",
    )
    freq, rinv = call(
        freq_body,
        [(1, count), rows],
        kern_own,
        kern_other,
        over_ctr(row),
        scratch=[pltpu.VMEM((CORES, half, LANES), F32)],
        limit=20,
        name="freq",
    )
    kerns = (kern_own, kern_other)
    sums = (half, 2 * LANES)
    work = 4 * half * count * 2 * LANES
    zt_shape = jax.ShapeDtypeStruct((width + ONES, half), BF16)
    squares = call(
        functools.partial(square_body, SIDE * SIDE),
        [sums],
        kern_own,
        centres,
        limit=20,
        name="squares_own",
        flops=work,
    )
    more, *data = call(
        square_setup_body,
        [sums, zt_shape, zt_shape, (half, LANES), (half, LANES)],
        kern_other,
        centres,
        rinv,
        z_own,
        z_other,
        limit=20,
        name="squares_other",
        flops=work,
    )
    squares = (squares, more)
    rs = data[CORES:]
    freq = call(
        add_body, [freq.shape], *around([freq] * SIDE, "x"), name="sum_x", after=squares[:1]
    )
    freq = around([freq] * SIDE, "h")
    target, finv = call(
        target_body,
        [rows, (1, count)],
        *kerns,
        *freq,
        prior,
        scratch=[pltpu.VMEM((CORES, half, LANES), F32)],
        limit=20,
        name="target",
        after=squares[1:],
    )
    cubes = [
        call(cube_body, [sums], kern, finv, centres, limit=20, name="cubes", flops=work)
        for kern in kerns
    ]
    target = call(swap_core_body, [rows], target, swap(target, "core", 1), name="target_core")
    target = call(add_body, [rows], target, swap(target, "zl", 1), name="target_zl")
    target = around([target] * SIDE, "y")

    setup = [pltpu.VMEM((CORES, half, LANES), F32)]
    piece, part, pair = (width, SIDE * inner), (width // 2, SIDE * inner), (width, 2 * inner)
    base = (*kerns, finv, centres, *data)
    low, high, tinv = call(
        far_body, [part, part, rows], *base, *target, scratch=setup, limit=24, name="grad_far"
    )
    low, high = swap(low, "x", 1), swap(high, "x", 3)
    first, third = call(
        mid_body, [piece, piece], *base, tinv, scratch=setup, limit=24, name="grad_mid"
    )
    mine, other = call(
        embed_body,
        [(half, width)] * 2,
        tinv,
        *rs,
        z_own,
        z_other,
        *cubes,
        *squares,
        limit=8,
        name="embed_part",
        flops=HINT // 2,
    )
    moved = (first, third, low, high)
    first_a, third_a = call(
        functools.partial(second_body, 0), [pair] * 2, *moved, name="second_a", flops=HINT
    )
    first_a, third_a = swap(first_a, "x", 1), swap(third_a, "x", 3)
    first_b, third_b, near = call(
        functools.partial(second_near_body, 2 * inner),
        [pair, pair, piece],
        *base,
        tinv,
        *moved,
        scratch=setup,
        limit=24,
        name="second_b",
        flops=HINT,
        after=[mine],
    )
    first_b, third_b = swap(first_b, "x", 1), swap(third_b, "x", 3)

    embed = call(add_body, [mine.shape], mine, swap(other, "core", 1), name="embed_core", after=[low, high])
    embed = call(add_body, [mine.shape], embed, swap(embed, "zl", 1), name="embed_zl")
    embed = call(add_body, [mine.shape], embed, swap(embed, "y", 1), name="embed_y")
    embed = (embed, swap(embed, "y", 3))

    block = (width, inner)
    def split(start, pieces, name, after=()):
        return call(
            functools.partial(split_body, start),
            [block] * 2,
            near,
            *pieces,
            name=name,
            flops=HINT,
            after=after,
        )

    far2, far1 = split(0, (first_a, third_a), "split_a")
    h2, h1 = swap(far2, "h", HOPS[0]), swap(far1, "h", HOPS[1])
    h3, h0 = split(2 * inner, (first_b, third_b), "split_b", after=[far2])
    most = call(three_body, [block], h0, h1, h2, name="most", flops=HINT)
    grad, embed = call(
        final_body,
        [(inner, width), (half, width)],
        most,
        swap(h3, "h", HOPS[2]),
        *embed,
        name="final",
        flops=HINT,
    )
    return embed, grad.reshape(1, inner, width)


def solution(mesh):
    names = ("x", "h", "core", "zl", "y")
    grid = jax.sharding.Mesh(mesh.devices.reshape(SIDE, SIDE, CORES, CORES, SIDE), names)
    pts, ctr = names[:3], names[3:]
    in_specs = (P(pts, None), P(ctr, None), P(ctr))
    out_specs = (P(pts, None), P(ctr, pts, None))
    return jax.shard_map(body, mesh=grid, in_specs=in_specs, out_specs=out_specs, check_vma=False)
```
